128 devices in a mesh: pts: 128 (over y, z, x, core).
Axes of the slice: x: 4, y: 4, z: 4, core: 2. Of those that a mesh axis runs over, the one named last changes fastest.
Arguments:
- loader_points: bfloat16 [524288, 256], P('pts'), may hold values from -6 to 6
- cotangent: bfloat16 [262144, 256], P('pts'), may hold values from -6 to 6
- block_counts: int32 [128], replicated, may hold values from 0 to 8, as said below
- dest_table: int32 [1024], P('pts'), may hold values from -1 to 511, as said below
- norm_gain: float32 [256], replicated, may hold values from 0.25 to 1.75
- w_feature: bfloat16 [256, 256], replicated, may hold values from -0.375 to 0.375
- w_middle: bfloat16 [256, 256], replicated, may hold values from -0.5625 to 0.5625
- w_slice: bfloat16 [32, 64], replicated, may hold values from -3.171875 to 3.171875
- w_temper: float32 [32], replicated, may hold values from -1 to 1
- attend_weight: float32 [3, 32, 32], replicated, may hold values from -6.363961 to 6.363961
- w_output: bfloat16 [256, 256], replicated, may hold values from -0.375 to 0.375
Outputs:
- layer_out: bfloat16 [262144, 256], P('pts')
- grad_points: bfloat16 [262144, 256], P('pts')
- grad_gain: float32 [256], replicated
- grad_feature: float32 [256, 256], replicated
- grad_middle: float32 [256, 256], replicated
- grad_slice: float32 [32, 64], replicated
- grad_temper: float32 [32], replicated
- grad_attend: float32 [3, 32, 32], replicated
- grad_output: float32 [256, 256], replicated
The draws below stay inside these ranges and needn't reach their ends.
Inputs may be any that keep to these rules, and one draw needn't show every extreme that they name: `block_counts`: the counts sum to 512. Balanced device d owns blocks d * 4 to d * 4 + 3. Loader buffer d holds some last blocks of device d - 1, then its own blocks without some first and some last ones, then some first blocks of device d + 1; its first blocks are loaded by buffer d - 1 and its last ones by buffer d + 1. At most 2 blocks go from one device to one neighbour, and that most is reached. Some buffer is full and some buffer is empty. dest_table[d * 8 + s], for s < block_counts[d], is the balanced block index of slot s of buffer d; these rise with s. Empty slots hold -1.
All inputs are finite; a program needn't handle non-finite values.
Results may differ from the reference program's by a relative error of at most 0.013.
The reference program's roundings to bfloat16 on the way count: a program that leaves them out, or rounds other values in their place, can miss the bound.
Values may be sent and summed in bfloat16 or wider, within the bound.
No kernel may reach another device: no remote copies, remote signals or barrier semaphores. Data moves between devices by JAX's collectives and lax.ppermute only.
A program may use at most 192 MiB of HBM per device.

```python
import math
import jax
import jax.numpy as jnp
from jax import lax

C = 256
SLICES = 64
HEAD_DIM = 32
BLOCK = 512
B_DEV = 4
HALF = 2
CAP = 8
LOADERS = 128
TOTAL_ROWS = 262144
LOADER_ROWS = 524288


def rebalance_plan(key):
    inner = jax.random.fold_in(key, 17)
    key_tail, key_head = jax.random.split(inner, 2)
    tails = jax.random.randint(key_tail, (LOADERS + 1,), 0, HALF + 1)
    heads = jax.random.randint(key_head, (LOADERS + 1,), 0, HALF + 1)
    tails = tails.at[1].set(HALF).at[LOADERS - 1].set(HALF).at[0].set(0).at[LOADERS].set(0)
    heads = heads.at[1].set(HALF).at[LOADERS - 1].set(HALF).at[0].set(0).at[LOADERS].set(0)
    tails = tails.at[2].set(HALF).at[3].set(0).at[5].set(0).at[6].set(HALF)
    heads = heads.at[2].set(0).at[3].set(HALF).at[5].set(HALF).at[6].set(0)
    own_kept = B_DEV - heads[:-1] - tails[1:]
    counts = tails[:-1] + own_kept + heads[1:]
    return (counts.astype(jnp.int32), tails.astype(jnp.int32), heads.astype(jnp.int32), own_kept.astype(jnp.int32))


def draw_block_counts(key, part):
    return rebalance_plan(key)[0]


def draw_dest_table(key, part):
    counts, tails, heads, own_kept = rebalance_plan(key)
    base = B_DEV * jnp.arange(LOADERS, dtype=jnp.int32)
    from_prev = tails[:-1][:, None]
    kept = own_kept[:, None]
    slot_ids = jnp.arange(CAP, dtype=jnp.int32)[None, :]
    first_part = base[:, None] - from_prev + slot_ids
    middle_part = base[:, None] + heads[:-1][:, None] + (slot_ids - from_prev)
    last_part = base[:, None] + B_DEV + (slot_ids - from_prev - kept)
    table = jnp.where(slot_ids < from_prev, first_part, jnp.where(slot_ids < from_prev + kept, middle_part, last_part))
    table = jnp.where(slot_ids < counts[:, None], table, -1)
    return table.reshape(-1).astype(jnp.int32)


def shared_projection(key):
    return jnp.clip(jax.random.normal(key, (C, C), jnp.float32), -6.0, 6.0)


def draw_w_feature(key, part):
    shared = shared_projection(key)
    return (shared * C ** (-0.5)).astype(jnp.bfloat16)


def draw_w_middle(key, part):
    shared = shared_projection(key)
    key = jax.random.fold_in(key, 29)
    own_part = jnp.clip(jax.random.normal(key, (C, C), jnp.float32), -6.0, 6.0)
    return ((0.8 * shared + 0.6 * own_part) * C ** (-0.5)).astype(jnp.bfloat16)


def block_levels(own_key, extent, pieces, low, top_value):
    loudness, own = 1.0, jax.random.fold_in(own_key, 6)
    for dim, blocks in pieces:
        draws = jnp.exp(jax.random.uniform(jax.random.fold_in(own, dim), (blocks,), jnp.float32, low / len(pieces), top_value / len(pieces)))
        loudness = loudness * jnp.repeat(draws, extent[dim] // blocks).reshape([-1 if axis == dim else 1 for axis in range(len(extent))])
    return loudness


def centred(own_key, dims, width, limit, shards=(), held_as=jnp.bfloat16):
    drawn = width * jax.random.normal(own_key, dims, jnp.float32)
    if shards:
        drawn = drawn * block_levels(own_key, dims, shards, -0.22, 0.18)
    return jnp.clip(drawn, -limit, limit).astype(held_as)


def setup_inputs(seed: int = 0) -> dict:
    keys = jax.random.split(jax.random.key(seed), 12)
    return {
        "loader_points": centred(keys[0], (LOADER_ROWS, C), 1.0, 6.0, ((0, 128),)),
        "cotangent": centred(keys[1], (TOTAL_ROWS, C), 1.0, 6.0, ((0, 128),)),
        "block_counts": draw_block_counts(jax.random.fold_in(keys[11], 71), 0),
        "dest_table": draw_dest_table(jax.random.fold_in(keys[11], 71), 0),
        "norm_gain": jnp.clip(1.0 + 0.15 * jax.random.normal(keys[4], (C,), jnp.float32), 0.25, 1.75),
        "w_feature": draw_w_feature(jax.random.fold_in(keys[11], 71), 0),
        "w_middle": draw_w_middle(jax.random.fold_in(keys[11], 71), 0),
        "w_slice": centred(keys[7], (HEAD_DIM, SLICES), (3.0 * HEAD_DIM ** -0.5), 3.171875),
        "w_temper": centred(keys[8], (HEAD_DIM,), HEAD_DIM ** -0.5, 1.0, (), jnp.float32),
        "attend_weight": centred(keys[9], (3, HEAD_DIM, HEAD_DIM), (6.0 * HEAD_DIM ** -0.5), 6.363961, (), jnp.float32),
        "w_output": centred(keys[10], (C, C), C ** -0.5, 0.375),
    }


def mix_heads(form, left, right):
    return jnp.einsum(form, left.astype(jnp.float32), right.astype(jnp.float32))

def transpose_dot(left, right):
    return lax.dot_general(left, right, (((0,), (0,)), ((), ())), preferred_element_type=jnp.float32)

def dot_against(left, right):
    return lax.dot_general(left, right, (((1,), (1,)), ((), ())), preferred_element_type=jnp.float32)

def slice_front(point_rows, row_mask, norm_gain, w_feature, w_middle, w_slice, w_temper):
    count_of_rows, feature_width = point_rows.shape
    head_width = w_slice.shape[0]
    count_of_heads = feature_width // head_width
    point_f = point_rows.astype(jnp.float32)
    center = point_f - lax.optimization_barrier(jnp.mean(point_f, axis=-1, keepdims=True))
    inv_std = lax.rsqrt(lax.optimization_barrier(jnp.mean(center * center, axis=-1, keepdims=True)) + 1e-05)
    x_hat = center * inv_std
    normed = (x_hat * norm_gain).astype(jnp.bfloat16)
    features = jnp.dot(normed, w_feature, preferred_element_type=jnp.float32).astype(jnp.bfloat16)
    middle = jnp.dot(normed, w_middle, preferred_element_type=jnp.float32).astype(jnp.bfloat16)
    per_head = middle.reshape(count_of_rows * count_of_heads, head_width)
    temper = lax.optimization_barrier(jnp.sum(per_head.astype(jnp.float32) * w_temper, axis=-1))
    temp_scale = 0.5 + jax.nn.softplus(temper)
    logits = jnp.dot(per_head, w_slice, preferred_element_type=jnp.float32) / temp_scale[:, None]
    slice_prob = jax.nn.softmax(logits, axis=-1) * jnp.repeat(row_mask, count_of_heads)[:, None]
    weights = slice_prob.astype(jnp.bfloat16).reshape(count_of_rows, -1)
    return (x_hat, inv_std, normed, features, per_head, temper, temp_scale, logits, slice_prob, weights)

def slice_attention(numer, denom, attend_weight):
    head_width = numer.shape[-1]
    highest_precision = lax.Precision.HIGHEST
    slice_tokens = numer / (denom[..., None] + 1e-05)
    query_projection = jnp.einsum('gpu,uo->gpo', slice_tokens, attend_weight[0], precision=highest_precision)
    key_projection = jnp.einsum('gpu,uo->gpo', slice_tokens, attend_weight[1], precision=highest_precision)
    value_projection = jnp.einsum('gpu,uo->gpo', slice_tokens, attend_weight[2], precision=highest_precision)
    score_matrix = jnp.einsum('ykq,ysq->yks', query_projection, key_projection, precision=highest_precision) / math.sqrt(head_width)
    attend_slices = jax.nn.softmax(score_matrix, axis=-1)
    return jnp.einsum('vsb,vbo->vso', attend_slices, value_projection, precision=highest_precision)

def partials(front, cot_rows, w_output, head_width):
    weights, features = (front[9], front[3])
    count_of_rows = weights.shape[0]
    slices = front[7].shape[1]
    count_of_heads = features.shape[1] // head_width
    triple_weight = weights.reshape(count_of_rows, count_of_heads, slices)
    triple_features = features.reshape(count_of_rows, count_of_heads, head_width)
    numerator_partial = mix_heads('nkq,nka->kqa', triple_weight, triple_features)
    denom_part = lax.optimization_barrier(jnp.sum(triple_weight.astype(jnp.float32), axis=0))
    mixed_gradient = dot_against(cot_rows, w_output).astype(jnp.bfloat16)
    partial_gradient = mix_heads('nkq,nka->kqa', triple_weight, mixed_gradient.reshape(count_of_rows, count_of_heads, head_width))
    return (numerator_partial, denom_part, partial_gradient, mixed_gradient)

def finish(front, point_rows, cot_rows, mixed_gradient, attended, d_numer, denominator_gradient, norm_gain, w_feature, w_middle, w_slice, w_temper, w_output):
    x_hat, inv_std, normed, features, per_head, temper, temp_scale, logits, slice_prob, weights = front
    count_of_rows, feature_width = point_rows.shape
    head_width, slices = w_slice.shape
    count_of_heads = feature_width // head_width
    triple_weight = weights.reshape(count_of_rows, count_of_heads, slices)
    triple_features = features.reshape(count_of_rows, count_of_heads, head_width)
    attended_broadcast = attended.astype(jnp.bfloat16)
    mixed_heads = mix_heads('uag,agx->uax', triple_weight, attended_broadcast).astype(jnp.bfloat16).reshape(count_of_rows, feature_width)
    layer_out = (point_rows.astype(jnp.float32) + jnp.dot(mixed_heads, w_output, preferred_element_type=jnp.float32)).astype(jnp.bfloat16)
    numerator_broadcast = d_numer.astype(jnp.bfloat16)
    weights_gradient = mix_heads('qcj,cxj->qcx', mixed_gradient.reshape(count_of_rows, count_of_heads, head_width), attended_broadcast)
    weights_gradient = weights_gradient + mix_heads('qcj,cxj->qcx', triple_features, numerator_broadcast) + denominator_gradient[None]
    weights_gradient = weights_gradient.reshape(count_of_rows * count_of_heads, slices)
    d_logits = slice_prob * (weights_gradient - lax.optimization_barrier(jnp.sum(slice_prob * weights_gradient, axis=-1, keepdims=True)))
    d_temper = -lax.optimization_barrier(jnp.sum(d_logits * logits, axis=-1)) / temp_scale * jax.nn.sigmoid(temper)
    d_raw = (d_logits / temp_scale[:, None]).astype(jnp.bfloat16)
    d_middle = (dot_against(d_raw, w_slice) + d_temper[:, None] * w_temper).astype(jnp.bfloat16).reshape(count_of_rows, feature_width)
    features_gradient = mix_heads('uag,agx->uax', triple_weight, numerator_broadcast).astype(jnp.bfloat16).reshape(count_of_rows, feature_width)
    d_normed = dot_against(features_gradient, w_feature) + dot_against(d_middle, w_middle)
    scaled = d_normed * norm_gain
    grad_rows = cot_rows.astype(jnp.float32) + (scaled - lax.optimization_barrier(jnp.mean(scaled, axis=-1, keepdims=True)) - x_hat * lax.optimization_barrier(jnp.mean(scaled * x_hat, axis=-1, keepdims=True))) * inv_std
    grads = (lax.optimization_barrier(jnp.sum(d_normed * x_hat, axis=0)), transpose_dot(normed, features_gradient), transpose_dot(normed, d_middle), transpose_dot(per_head, d_raw), lax.optimization_barrier(jnp.sum(d_temper[:, None] * per_head.astype(jnp.float32), axis=0)), transpose_dot(mixed_heads, cot_rows))
    return (layer_out, grad_rows.astype(jnp.bfloat16), grads)

def reference(loader_points, cotangent, block_counts, dest_table, norm_gain, w_feature, w_middle, w_slice, w_temper, attend_weight, w_output):
    feature_width = loader_points.shape[1]
    head_width = w_slice.shape[0]
    blocks_in = loader_points.reshape(LOADERS * CAP, BLOCK, feature_width)
    slot_ids = jnp.arange(LOADERS * CAP, dtype=jnp.int32)
    owner = slot_ids // CAP
    valid = slot_ids % CAP < block_counts[owner]
    target = jnp.where(valid, dest_table, LOADERS * B_DEV).astype(jnp.int32)
    placed = jnp.zeros((LOADERS * B_DEV + 1, BLOCK, feature_width), loader_points.dtype).at[target].set(blocks_in)[:-1]
    point_rows = placed.reshape(LOADERS, B_DEV * BLOCK, feature_width)
    cot_rows = cotangent.reshape(LOADERS, B_DEV * BLOCK, feature_width)
    row_mask = jnp.ones((B_DEV * BLOCK,), jnp.float32)

    def first_pass(pair):
        front = slice_front(pair[0], row_mask, norm_gain, w_feature, w_middle, w_slice, w_temper)
        numerator_partial, denom_part, partial_gradient, mixed_gradient = partials(front, pair[1], w_output, head_width)
        return (numerator_partial, denom_part, partial_gradient)
    parts = lax.map(first_pass, (point_rows, cot_rows))
    numer = lax.optimization_barrier(jnp.sum(parts[0], axis=0))
    denom = lax.optimization_barrier(jnp.sum(parts[1], axis=0))
    deslice_grad = lax.optimization_barrier(jnp.sum(parts[2], axis=0))
    attended, back_mid = jax.vjp(slice_attention, numer, denom, attend_weight)
    d_numer, denominator_gradient, grad_attend = back_mid(deslice_grad)

    def second_pass(pair):
        front = slice_front(pair[0], row_mask, norm_gain, w_feature, w_middle, w_slice, w_temper)
        mixed_gradient = dot_against(pair[1], w_output).astype(jnp.bfloat16)
        return finish(front, pair[0], pair[1], mixed_gradient, attended, d_numer, denominator_gradient, norm_gain, w_feature, w_middle, w_slice, w_temper, w_output)
    layer_out, grad_points, grads = lax.map(second_pass, (point_rows, cot_rows))
    sums = [lax.optimization_barrier(jnp.sum(item, axis=0)) for item in grads]
    return (layer_out.reshape(TOTAL_ROWS, feature_width), grad_points.reshape(TOTAL_ROWS, feature_width), sums[0], sums[1], sums[2], sums[3], sums[4], grad_attend, sums[5])
```

```python
import math

import jax
import jax.numpy as jnp
from jax import lax
from jax.experimental import pallas as pl
from jax.experimental.pallas import tpu as pltpu
from jax.sharding import PartitionSpec as P

BLOCK = 512
B_DEV = 4
HALF = 2
CAP = 8
C = 256
HEADS = 8
HEAD = 32
SLICES = 64
HS = HEADS * SLICES
ROWS = B_DEV * BLOCK
PAY1 = 640
PAY2 = 896
BF = jnp.bfloat16
F32 = jnp.float32
HIGH = lax.Precision.HIGHEST
NN = (((1,), (0,)), ((), ()))
NT = (((1,), (1,)), ((), ()))
TN = (((0,), (0,)), ((), ()))


def dot(a, b, dims=NN):
    return lax.dot_general(a, b, dims, preferred_element_type=F32)


def dot_high(a, b, dims=NN):
    return lax.dot_general(a, b, dims, precision=HIGH, preferred_element_type=F32)


def head_mask(rows):
    row_head = lax.broadcasted_iota(jnp.int32, (rows, C), 0) // SLICES
    lane_head = lax.broadcasted_iota(jnp.int32, (rows, C), 1) // HEAD
    return row_head == lane_head


def fold_heads(full):
    masked = jnp.where(head_mask(HS), full, 0.0)
    return jnp.sum(masked.reshape(HEADS, SLICES, C), axis=0)


def spread_heads(small):
    tiled = jnp.concatenate([small] * HEADS, axis=0)
    return jnp.where(head_mask(HS), tiled, 0.0)


def normalize(points):
    point_f = points.astype(F32)
    center = point_f - jnp.mean(point_f, axis=-1, keepdims=True)
    inv_std = lax.rsqrt(jnp.mean(center * center, axis=-1, keepdims=True) + 1e-05)
    return center * inv_std, inv_std


def slice_softmax(mid, bd):
    out = dot(bd, mid, NT)
    width = mid.shape[0]
    temper = out[HS : HS + 8] + out[HS + 8 : HS + 16] + out[HS + 16 : HS + 24]
    scale = 0.5 + jnp.maximum(temper, 0.0) + jnp.log1p(jnp.exp(-jnp.abs(temper)))
    inv = 1.0 / scale
    logits = out[:HS].reshape(HEADS, SLICES, width) * inv[:, None, :]
    top = jnp.max(logits, axis=1, keepdims=True)
    e = jnp.exp(logits - top)
    prob = e * (1.0 / jnp.sum(e, axis=1, keepdims=True))
    return temper, inv, logits, prob


def front_kernel(
    sel, own, prev, nxt, dmix, gain, wfm, bd, ptsb, normed_out, feat_out, mid_out, pay, acc, den
):
    t = pl.program_id(0)
    kind = sel[3, t]

    @pl.when(kind == 0)
    def _():
        ptsb[...] = own[...]

    @pl.when(kind == 1)
    def _():
        ptsb[...] = prev[...]

    @pl.when(kind == 2)
    def _():
        ptsb[...] = nxt[...]

    x_hat, _ = normalize(ptsb[...])
    normed = (x_hat * gain[...]).astype(BF)
    normed_out[...] = normed
    fm = dot(normed, wfm[...]).astype(BF)
    feat, mid = fm[:, :C], fm[:, C:]
    feat_out[...] = feat
    mid_out[...] = mid
    _, _, _, prob = slice_softmax(mid, bd[...])
    weights = prob.reshape(HS, BLOCK).astype(BF)

    @pl.when(t == 0)
    def _():
        acc[...] = jnp.zeros_like(acc)
        den[...] = jnp.zeros_like(den)

    acc[:, :C] += dot(weights, feat)
    acc[:, C:] += dot(weights, dmix[...])
    wf = weights.astype(F32)
    den[...] += sum(wf[:, i * 128 : (i + 1) * 128] for i in range(BLOCK // 128))

    @pl.when(t == B_DEV - 1)
    def _():
        pay[:, :C] = fold_heads(acc[:, :C])
        pay[:, C : 2 * C] = fold_heads(acc[:, C:])
        total = jnp.sum(den[...], axis=1, keepdims=True)
        row_head = lax.broadcasted_iota(jnp.int32, (HS, 128), 0) // SLICES
        lane = lax.broadcasted_iota(jnp.int32, (HS, 128), 1)
        placed = jnp.where(row_head == lane, total, 0.0)
        pay[:, 2 * C :] = jnp.sum(placed.reshape(HEADS, SLICES, 128), axis=0)


def attention_step(pay, watt, an, ant, dd, gatt):
    numer = pay[:, :C]
    deslice = pay[:, C : 2 * C]
    head_of_lane = lax.broadcasted_iota(jnp.int32, (128, C), 1) // HEAD
    expand = (lax.broadcasted_iota(jnp.int32, (128, C), 0) == head_of_lane).astype(F32)
    inv_den = 1.0 / (dot_high(pay[:, 2 * C :], expand) + 1e-05)
    tokens = numer * inv_den
    mask = head_mask(HS)
    q = dot_high(tokens, watt[0])
    k = dot_high(tokens, watt[1])
    v = dot_high(tokens, watt[2])
    q_bd = spread_heads(q)
    root = 1.0 / math.sqrt(HEAD)
    scores = dot_high(q_bd, k, NT) * root
    top = jnp.max(scores, axis=-1, keepdims=True)
    e = jnp.exp(scores - top)
    att = e / jnp.sum(e, axis=-1, keepdims=True)
    attended = jnp.where(mask, dot_high(att, v), 0.0)
    do_bd = spread_heads(deslice)
    dv = dot_high(att, do_bd, TN)
    d_att = dot_high(do_bd, v, NT)
    ds = att * (d_att - jnp.sum(att * d_att, axis=-1, keepdims=True)) * root
    dq = fold_heads(dot_high(ds, k))
    dk = dot_high(ds, q_bd, TN)
    d_tokens = (
        dot_high(dq, watt[0], NT) + dot_high(dk, watt[1], NT) + dot_high(dv, watt[2], NT)
    )
    d_numer = d_tokens * inv_den
    d_den = -d_numer * tokens
    dd[...] = jnp.sum(spread_heads(d_den), axis=1, keepdims=True)
    d_numer_bd = spread_heads(d_numer)
    an[:, :C] = attended.astype(BF)
    an[:, C:] = d_numer_bd.astype(BF)
    ant[:C] = attended.T.astype(BF)
    ant[C:] = d_numer_bd.T.astype(BF)
    row_head = lax.broadcasted_iota(jnp.int32, (C, C), 0) // HEAD
    col_head = lax.broadcasted_iota(jnp.int32, (C, C), 1) // HEAD
    same = row_head == col_head
    lane_in = lax.broadcasted_iota(jnp.int32, (C, HEAD), 0) % HEAD
    fold = (lane_in == lax.broadcasted_iota(jnp.int32, (C, HEAD), 1)).astype(F32)
    for i, grad in enumerate((dq, dk, dv)):
        full = jnp.where(same, dot_high(tokens, grad, TN), 0.0)
        packed = dot_high(full, fold)
        gatt[i] = jnp.sum(packed.reshape(HEADS, HEAD, HEAD), axis=0)


def back_kernel(
    pay, watt, normed, feat, mid, dmix, cot, gain, wfmt, bd, bdt, wcol,
    res, gpay, gatt, an, ant, dd, gfm, gout, gsl,
):
    t = pl.program_id(0)

    @pl.when(t == 0)
    def _():
        attention_step(pay, watt, an, ant, dd, gatt)
        gfm[...] = jnp.zeros_like(gfm)
        gout[...] = jnp.zeros_like(gout)
        gsl[...] = jnp.zeros_like(gsl)

    mid_here = mid[...]
    temper, inv, logits, prob = slice_softmax(mid_here, bd[...])
    weights = prob.reshape(HS, BLOCK).astype(BF)
    dw = dot(an[:, :C], dmix[...], NT) + dot(an[:, C:], feat[...], NT) + dd[...]
    g = prob * dw.reshape(HEADS, SLICES, BLOCK)
    dl = g - prob * jnp.sum(g, axis=1, keepdims=True)
    d_temper = -jnp.sum(dl * logits, axis=1) * inv * jax.nn.sigmoid(temper)
    d_raw = (dl * inv[:, None, :]).reshape(HS, BLOCK).astype(BF)
    mixed_df = dot(ant[...], weights).astype(BF)
    spread = jnp.broadcast_to(d_temper[:, None, :], (HEADS, HEAD, BLOCK)).reshape(C, BLOCK)
    dm = (dot(bdt[...], d_raw) + spread * wcol[...]).astype(BF)
    res[: 2 * C] = mixed_df
    res[2 * C :] = dm
    normed_here = normed[...]
    gfm[:C] += dot(mixed_df[C:], normed_here)
    gfm[C:] += dot(dm, normed_here)
    gout[...] += dot(mixed_df[:C], cot[...])
    dt_hi = d_temper.astype(BF)
    dt_lo = (d_temper - dt_hi.astype(F32)).astype(BF)
    gsl[:HS] += dot(d_raw, mid_here)
    gsl[HS:] += dot(jnp.concatenate([dt_hi, dt_lo], axis=0), mid_here)

    @pl.when(t == B_DEV - 1)
    def _():
        grad_fm = gfm[...]
        gpay[: 2 * C] = grad_fm.astype(BF)
        gpay[2 * C : 3 * C] = gout[...].astype(BF)
        gpay[3 * C : 3 * C + SLICES] = fold_heads(gsl[:HS]).astype(BF)
        grad_gain = jnp.sum(grad_fm * wfmt[...].astype(F32), axis=0, keepdims=True) / gain[...]
        both = gsl[HS : HS + 8] + gsl[HS + 8 :]
        row = lax.broadcasted_iota(jnp.int32, (8, C), 0)
        lane_head = lax.broadcasted_iota(jnp.int32, (8, C), 1) // HEAD
        temper_row = jnp.sum(jnp.where(row == lane_head, both, 0.0), axis=0, keepdims=True)
        row = lax.broadcasted_iota(jnp.int32, (SLICES, C), 0)
        tail = jnp.where(row == 0, grad_gain, jnp.where(row == 1, temper_row, 0.0))
        gpay[3 * C + SLICES :] = tail.astype(BF)


def out_kernel(ptsb, cot, res, gain, wfmt, wout, layer, grad):
    points = ptsb[...]
    x_hat, inv_std = normalize(points)
    mixed_out = dot(res[:C], wout[...], TN)
    layer[...] = (points.astype(F32) + mixed_out).astype(BF)
    d_normed = dot(res[C:], wfmt[...], TN)
    scaled = d_normed * gain[...]
    mean_g = jnp.mean(scaled, axis=-1, keepdims=True)
    mean_gx = jnp.mean(scaled * x_hat, axis=-1, keepdims=True)
    grad[...] = (cot[...].astype(F32) + (scaled - mean_g - x_hat * mean_gx) * inv_std).astype(BF)


def unpack_kernel(got, gfeat, gmid, gout, gslice, gtemper, ggain):
    full = got[...].astype(F32).reshape(PAY2, C)
    gfeat[...] = full[:C].T
    gmid[...] = full[C : 2 * C].T
    gout[...] = full[2 * C : 3 * C]
    lane_in = lax.broadcasted_iota(jnp.int32, (C, HEAD), 0) % HEAD
    fold = (lane_in == lax.broadcasted_iota(jnp.int32, (C, HEAD), 1)).astype(F32)
    gslice[...] = dot_high(fold, full[3 * C : 3 * C + SLICES], (((0,), (1,)), ((), ())))
    tail = full[3 * C + SLICES : 3 * C + SLICES + 8]
    gtemper[...] = dot_high(tail, fold)[1:2]
    ggain[...] = tail[0:1]


def swap(array, mask):
    n = lax.axis_size("pts")
    return lax.ppermute(array, "pts", [(i, i ^ mask) for i in range(n)])


def quad_sum(x, low, high):
    a = swap(x, low)
    b = swap(x, high)
    c = swap(x, low ^ high)
    return (x + a) + (b + c)


def reduce_first(pay):
    core = lax.rem(lax.axis_index("pts"), 2)
    half = pay.shape[0] // 2
    send = lax.dynamic_slice_in_dim(pay, (1 - core) * half, half, 0)
    keep = lax.dynamic_slice_in_dim(pay, core * half, half, 0)
    x = keep + swap(send, 1)
    x = quad_sum(x, 2, 4)
    x = quad_sum(x, 8, 16)
    x = quad_sum(x, 32, 64)
    other = swap(x, 1)
    return jnp.where(
        core == 0, jnp.concatenate([x, other], 0), jnp.concatenate([other, x], 0)
    )


def groups_of_eight():
    return [[g * 8 + i for i in range(8)] for g in range(16)]


def reduce_second(gpay):
    pieces = gpay.reshape(8, PAY2 // 8, C)
    got = lax.all_to_all(pieces, "pts", 0, 0, tiled=True, axis_index_groups=groups_of_eight())
    x = jnp.sum(got.astype(F32), axis=0)
    for mask in (8, 24, 32, 96):
        x = x + swap(x, mask)
    tiled = jnp.broadcast_to(x.astype(BF)[None], (8, PAY2 // 8, C))
    return lax.all_to_all(tiled, "pts", 0, 0, tiled=True, axis_index_groups=groups_of_eight())


def shifted(array, by):
    n = lax.axis_size("pts")
    return lax.ppermute(array, "pts", [(i, i + by) for i in range(n) if 0 <= i + by < n])


def placement(dest_table, block_counts, rank):
    target = jnp.arange(B_DEV)
    matches = dest_table[None, :] == rank * B_DEV + target[:, None]
    found = jnp.any(matches, axis=1)
    own = jnp.sum(jnp.where(matches, jnp.arange(CAP)[None, :], 0), axis=1)
    from_prev = jnp.sum(~found & (target < HALF))
    from_next = jnp.sum(~found & (target >= HALF))
    left = jnp.sum(jnp.where(jnp.arange(block_counts.shape[0]) == rank - 1, block_counts, 0))
    start = jnp.maximum(left - HALF, 0)
    prev = jnp.clip(left - from_prev + target - start, 0, HALF - 1)
    nxt = jnp.clip(target - (B_DEV - from_next), 0, HALF - 1)
    kind = jnp.where(found, 0, jnp.where(target < HALF, 1, 2))
    return jnp.stack([own, prev, nxt, kind]).astype(jnp.int32)


def whole(shape):
    return pl.BlockSpec(shape, lambda t, *_: (0,) * len(shape))


def rows_spec(width):
    return pl.BlockSpec((BLOCK, width), lambda t, *_: (t, 0))


PARAMS = pltpu.CompilerParams(vmem_limit_bytes=48 * 1024 * 1024)


def per_device(
    loader_points, cotangent, block_counts, dest_table, norm_gain, w_feature, w_middle,
    w_slice, w_temper, attend_weight, w_output,
):
    rank = lax.axis_index("pts")
    count_here = jnp.sum(jnp.where(jnp.arange(block_counts.shape[0]) == rank, block_counts, 0))
    tail_at = jnp.maximum(count_here - HALF, 0) * BLOCK
    tail = lax.dynamic_slice_in_dim(loader_points, tail_at, HALF * BLOCK, 0)
    got_prev = shifted(tail, 1)
    got_next = shifted(loader_points[: HALF * BLOCK], -1)
    sel = placement(dest_table, block_counts, rank)
    gain = norm_gain.reshape(1, C)
    wfm = jnp.concatenate([w_feature, w_middle], axis=1)
    wfmt = wfm.T
    eye = jnp.eye(HEADS, dtype=F32)
    hi = lax.reduce_precision(w_temper, 8, 7)
    mid_part = lax.reduce_precision(w_temper - hi, 8, 7)
    low = w_temper - hi - mid_part
    slice_bd = jnp.kron(eye, w_slice.T.astype(F32))
    bd = jnp.concatenate(
        [slice_bd]
        + [jnp.kron(eye, part[None, :]) for part in (hi, mid_part, low)]
        + [jnp.zeros((8, C), F32)],
        axis=0,
    ).astype(BF)
    bdt = slice_bd.T.astype(BF)
    wcol = jnp.tile(w_temper, HEADS).reshape(C, 1)
    watt = jax.vmap(lambda w: jnp.kron(eye, w))(attend_weight)
    d_mixed = dot(cotangent, w_output, NT).astype(BF)

    wide = jax.ShapeDtypeStruct((ROWS, C), BF)
    ptsb, normed, feat, mid, pay = pl.pallas_call(
        front_kernel,
        grid_spec=pltpu.PrefetchScalarGridSpec(
            num_scalar_prefetch=1,
            grid=(B_DEV,),
            in_specs=[
                pl.BlockSpec((BLOCK, C), lambda t, s: (s[0, t], 0)),
                pl.BlockSpec((BLOCK, C), lambda t, s: (s[1, t], 0)),
                pl.BlockSpec((BLOCK, C), lambda t, s: (s[2, t], 0)),
                rows_spec(C),
                whole((1, C)),
                whole((C, 2 * C)),
                whole((HS + 32, C)),
            ],
            out_specs=[rows_spec(C)] * 4 + [whole((SLICES, PAY1))],
            scratch_shapes=[pltpu.VMEM((HS, 2 * C), F32), pltpu.VMEM((HS, 128), F32)],
        ),
        out_shape=[wide] * 4 + [jax.ShapeDtypeStruct((SLICES, PAY1), F32)],
        compiler_params=PARAMS,
        name="front",
    )(sel, loader_points, got_prev, got_next, d_mixed, gain, wfm, bd)

    pay = reduce_first(pay)

    res, gpay, grad_attend = pl.pallas_call(
        back_kernel,
        grid=(B_DEV,),
        in_specs=[whole((SLICES, PAY1)), whole((3, C, C))]
        + [rows_spec(C)] * 5
        + [
            whole((1, C)),
            whole((2 * C, C)),
            whole((HS + 32, C)),
            whole((C, HS)),
            whole((C, 1)),
        ],
        out_specs=[
            pl.BlockSpec((3 * C, BLOCK), lambda t: (0, t)),
            whole((PAY2, C)),
            whole((3, HEAD, HEAD)),
        ],
        out_shape=[
            jax.ShapeDtypeStruct((3 * C, ROWS), BF),
            jax.ShapeDtypeStruct((PAY2, C), BF),
            jax.ShapeDtypeStruct((3, HEAD, HEAD), F32),
        ],
        scratch_shapes=[
            pltpu.VMEM((HS, 2 * C), BF),
            pltpu.VMEM((2 * C, HS), BF),
            pltpu.VMEM((HS, 1), F32),
            pltpu.VMEM((2 * C, C), F32),
            pltpu.VMEM((C, C), F32),
            pltpu.VMEM((HS + 16, C), F32),
        ],
        compiler_params=PARAMS,
        name="back",
    )(pay, watt, normed, feat, mid, d_mixed, cotangent, gain, wfmt, bd, bdt, wcol)

    layer_out, grad_points = pl.pallas_call(
        out_kernel,
        grid=(B_DEV,),
        in_specs=[
            rows_spec(C),
            rows_spec(C),
            pl.BlockSpec((3 * C, BLOCK), lambda t: (0, t)),
            whole((1, C)),
            whole((2 * C, C)),
            whole((C, C)),
        ],
        out_specs=[rows_spec(C)] * 2,
        out_shape=[wide] * 2,
        compiler_params=PARAMS,
        cost_estimate=pl.CostEstimate(
            flops=2 * ROWS * C * 3 * C, bytes_accessed=7 * ROWS * C * 2, transcendentals=0
        ),
        name="outputs",
    )(ptsb, cotangent, res, gain, wfmt, w_output)

    got = reduce_second(gpay)
    grad_feature, grad_middle, grad_output, grad_slice, grad_temper, grad_gain = pl.pallas_call(
        unpack_kernel,
        out_shape=[
            jax.ShapeDtypeStruct((C, C), F32),
            jax.ShapeDtypeStruct((C, C), F32),
            jax.ShapeDtypeStruct((C, C), F32),
            jax.ShapeDtypeStruct((HEAD, SLICES), F32),
            jax.ShapeDtypeStruct((1, HEAD), F32),
            jax.ShapeDtypeStruct((1, C), F32),
        ],
        compiler_params=PARAMS,
        name="unpack",
    )(got)
    return (
        layer_out,
        grad_points,
        grad_gain.reshape(C),
        grad_feature,
        grad_middle,
        grad_slice,
        grad_temper.reshape(HEAD),
        grad_attend,
        grad_output,
    )


def solution(mesh):
    return jax.shard_map(
        per_device,
        mesh=mesh,
        in_specs=(P("pts", None), P("pts", None), P(), P("pts"), P(), P(), P(), P(), P(), P(), P()),
        out_specs=(P("pts", None), P("pts", None), P(), P(), P(), P(), P(), P(), P()),
        check_vma=False,
    )
```

```python
import math

import jax
import jax.numpy as jnp
from jax import lax
from jax.experimental import pallas as pl
from jax.experimental.pallas import tpu as pltpu
from jax.sharding import PartitionSpec as P

BLOCK = 512
B_DEV = 4
HALF = 2
CAP = 8
C = 256
HEADS = 8
HEAD = 32
SLICES = 64
HS = HEADS * SLICES
ROWS = B_DEV * BLOCK
PAY1 = 640
PAY2 = 896
BF = jnp.bfloat16
F32 = jnp.float32
HIGH = lax.Precision.HIGHEST
NN = (((1,), (0,)), ((), ()))
NT = (((1,), (1,)), ((), ()))
TN = (((0,), (0,)), ((), ()))


def dot(a, b, dims=NN):
    return lax.dot_general(a, b, dims, preferred_element_type=F32)


def dot_high(a, b, dims=NN):
    return lax.dot_general(a, b, dims, precision=HIGH, preferred_element_type=F32)


def head_mask(rows):
    row_head = lax.broadcasted_iota(jnp.int32, (rows, C), 0) // SLICES
    lane_head = lax.broadcasted_iota(jnp.int32, (rows, C), 1) // HEAD
    return row_head == lane_head


def fold_heads(full):
    masked = jnp.where(head_mask(HS), full, 0.0)
    return jnp.sum(masked.reshape(HEADS, SLICES, C), axis=0)


def spread_heads(small):
    tiled = jnp.concatenate([small] * HEADS, axis=0)
    return jnp.where(head_mask(HS), tiled, 0.0)


def normalize(points):
    point_f = points.astype(F32)
    center = point_f - jnp.mean(point_f, axis=-1, keepdims=True)
    inv_std = lax.rsqrt(jnp.mean(center * center, axis=-1, keepdims=True) + 1e-05)
    return center * inv_std, inv_std


def slice_softmax(mid, bd):
    out = dot(bd, mid, NT)
    width = mid.shape[0]
    temper = out[HS : HS + 8] + out[HS + 8 : HS + 16] + out[HS + 16 : HS + 24]
    scale = 0.5 + jnp.maximum(temper, 0.0) + jnp.log1p(jnp.exp(-jnp.abs(temper)))
    inv = 1.0 / scale
    logits = out[:HS].reshape(HEADS, SLICES, width) * inv[:, None, :]
    top = jnp.max(logits, axis=1, keepdims=True)
    e = jnp.exp(logits - top)
    prob = e * (1.0 / jnp.sum(e, axis=1, keepdims=True))
    return temper, inv, logits, prob


def split_halves(core, full, send, keep):
    half = full.shape[0] // 2

    @pl.when(core == 0)
    def _():
        keep[...] = full[:half].astype(keep.dtype)
        send[...] = full[half:].astype(send.dtype)

    @pl.when(core != 0)
    def _():
        keep[...] = full[half:].astype(keep.dtype)
        send[...] = full[:half].astype(send.dtype)


def join_halves(core, mine, other, full):
    half = full.shape[0] // 2

    @pl.when(core == 0)
    def _():
        full[:half] = mine[...].astype(full.dtype)
        full[half:] = other[...].astype(full.dtype)

    @pl.when(core != 0)
    def _():
        full[:half] = other[...].astype(full.dtype)
        full[half:] = mine[...].astype(full.dtype)


def pick_kernel(rank, counts, loader, head, tail, sems):
    start = jnp.maximum(counts[rank[0]] - HALF, 0) * BLOCK
    start = pl.multiple_of(start, BLOCK)
    first = pltpu.make_async_copy(loader.at[pl.ds(0, HALF * BLOCK)], head, sems.at[0])
    last = pltpu.make_async_copy(loader.at[pl.ds(start, HALF * BLOCK)], tail, sems.at[1])
    first.start()
    last.start()
    first.wait()
    last.wait()


def prep_kernel(
    rank, counts, table, cot, wout, wf, wm, ws, wt, attw,
    sel, dmix, wfmt, bd, bdt, wcol, watt,
):
    here = rank[0]
    found, own = [], []
    for t in range(B_DEV):
        slot = jnp.int32(0)
        hit = jnp.int32(0)
        for s in range(CAP):
            same = table[s] == here * B_DEV + t
            slot = jnp.where(same, s, slot)
            hit = jnp.where(same, 1, hit)
        own.append(slot)
        found.append(hit)
    from_prev = 2 - found[0] - found[1]
    from_next = 2 - found[2] - found[3]
    left = counts[jnp.maximum(here - 1, 0)]
    start = jnp.maximum(left - HALF, 0)
    for t in range(B_DEV):
        sel[0, t] = own[t]
        sel[1, t] = jnp.clip(left - from_prev + t - start, 0, HALF - 1)
        sel[2, t] = jnp.clip(t - (B_DEV - from_next), 0, HALF - 1)
        sel[3, t] = jnp.where(found[t] == 1, 0, 1 if t < HALF else 2)

    dmix[...] = dot(cot[...], wout[...], NT).astype(BF)
    wfmt[:C] = wf[...].T
    wfmt[C:] = wm[...].T
    lane_in = lax.broadcasted_iota(jnp.int32, (HEAD, C), 1) % HEAD
    spread = (lax.broadcasted_iota(jnp.int32, (HEAD, C), 0) == lane_in).astype(F32)
    slice_rows = dot(ws[...], spread.astype(BF), TN)
    slice_bd = spread_heads(slice_rows)
    bd[:HS] = slice_bd.astype(BF)
    bdt[...] = slice_bd.T.astype(BF)
    temper = dot_high(wt[...], spread)
    hi = temper.astype(BF).astype(F32)
    middle = (temper - hi).astype(BF).astype(F32)
    low = temper - hi - middle
    row = lax.broadcasted_iota(jnp.int32, (8, C), 0)
    own_head = row == lax.broadcasted_iota(jnp.int32, (8, C), 1) // HEAD
    parts = [jnp.where(own_head, part, 0.0) for part in (hi, middle, low)]
    bd[HS:] = jnp.concatenate(parts + [jnp.zeros((8, C), F32)], axis=0).astype(BF)
    rows = lax.broadcasted_iota(jnp.int32, (C, C), 0)
    cols = lax.broadcasted_iota(jnp.int32, (C, C), 1)
    wcol[...] = jnp.sum(jnp.where(rows == cols, temper, 0.0), axis=1, keepdims=True)
    same_head = rows // HEAD == cols // HEAD
    for i in range(3):
        wide = dot_high(attw[i], spread)
        watt[i] = jnp.where(same_head, jnp.concatenate([wide] * HEADS, axis=0), 0.0)


def front_kernel(
    sel, core, own, prev, nxt, dmix, gain, wf, wm, bd,
    ptsb, normed_out, feat_out, mid_out, send, keep, acc, den, pay
):
    t = pl.program_id(0)
    kind = sel[3, t]

    @pl.when(kind == 0)
    def _():
        ptsb[...] = own[...]

    @pl.when(kind == 1)
    def _():
        ptsb[...] = prev[...]

    @pl.when(kind == 2)
    def _():
        ptsb[...] = nxt[...]

    x_hat, _ = normalize(ptsb[...])
    normed = (x_hat * gain[...]).astype(BF)
    normed_out[...] = normed
    feat = dot(normed, wf[...]).astype(BF)
    mid = dot(normed, wm[...]).astype(BF)
    feat_out[...] = feat
    mid_out[...] = mid
    _, _, _, prob = slice_softmax(mid, bd[...])
    weights = prob.reshape(HS, BLOCK).astype(BF)

    @pl.when(t == 0)
    def _():
        acc[...] = jnp.zeros_like(acc)
        den[...] = jnp.zeros_like(den)

    acc[:, :C] += dot(weights, feat)
    acc[:, C:] += dot(weights, dmix[...])
    wf = weights.astype(F32)
    den[...] += sum(wf[:, i * 128 : (i + 1) * 128] for i in range(BLOCK // 128))

    @pl.when(t == B_DEV - 1)
    def _():
        pay[:, :C] = fold_heads(acc[:, :C])
        pay[:, C : 2 * C] = fold_heads(acc[:, C:])
        total = jnp.sum(den[...], axis=1, keepdims=True)
        row_head = lax.broadcasted_iota(jnp.int32, (HS, 128), 0) // SLICES
        lane = lax.broadcasted_iota(jnp.int32, (HS, 128), 1)
        placed = jnp.where(row_head == lane, total, 0.0)
        pay[:, 2 * C :] = jnp.sum(placed.reshape(HEADS, SLICES, 128), axis=0)
        split_halves(core[0], pay, send, keep)


def attention_step(pay, watt, an, ant, dd, toks):
    numer = pay[:, :C]
    deslice = pay[:, C : 2 * C]
    head_of_lane = lax.broadcasted_iota(jnp.int32, (128, C), 1) // HEAD
    expand = (lax.broadcasted_iota(jnp.int32, (128, C), 0) == head_of_lane).astype(F32)
    inv_den = 1.0 / (dot_high(pay[:, 2 * C :], expand) + 1e-05)
    tokens = numer * inv_den
    mask = head_mask(HS)
    q = dot_high(tokens, watt[0])
    k = dot_high(tokens, watt[1])
    v = dot_high(tokens, watt[2])
    q_bd = spread_heads(q)
    root = 1.0 / math.sqrt(HEAD)
    scores = dot_high(q_bd, k, NT) * root
    top = jnp.max(scores, axis=-1, keepdims=True)
    e = jnp.exp(scores - top)
    att = e / jnp.sum(e, axis=-1, keepdims=True)
    attended = jnp.where(mask, dot_high(att, v), 0.0)
    do_bd = spread_heads(deslice)
    dv = dot_high(att, do_bd, TN)
    d_att = dot_high(do_bd, v, NT)
    ds = att * (d_att - jnp.sum(att * d_att, axis=-1, keepdims=True)) * root
    dq = fold_heads(dot_high(ds, k))
    dk = dot_high(ds, q_bd, TN)
    d_tokens = (
        dot_high(dq, watt[0], NT) + dot_high(dk, watt[1], NT) + dot_high(dv, watt[2], NT)
    )
    d_numer = d_tokens * inv_den
    d_den = -d_numer * tokens
    dd[...] = jnp.sum(spread_heads(d_den), axis=1, keepdims=True)
    d_numer_bd = spread_heads(d_numer)
    an[:, :C] = attended.astype(BF)
    an[:, C:] = d_numer_bd.astype(BF)
    ant[:C] = attended.T.astype(BF)
    ant[C:] = d_numer_bd.T.astype(BF)
    toks[0] = tokens
    toks[1] = dq
    toks[2] = dk
    toks[3] = dv


def attend_gradients(toks, gatt):
    row_head = lax.broadcasted_iota(jnp.int32, (C, C), 0) // HEAD
    col_head = lax.broadcasted_iota(jnp.int32, (C, C), 1) // HEAD
    same = row_head == col_head
    lane_in = lax.broadcasted_iota(jnp.int32, (C, HEAD), 0) % HEAD
    fold = (lane_in == lax.broadcasted_iota(jnp.int32, (C, HEAD), 1)).astype(F32)
    for i in range(3):
        full = jnp.where(same, dot_high(toks[0], toks[i + 1], TN), 0.0)
        packed = dot_high(full, fold)
        gatt[i] = jnp.sum(packed.reshape(HEADS, HEAD, HEAD), axis=0)


def back_kernel(
    core, mine, other, watt, normed, feat, mid, dmix, cot, gain, wfmt, bd, bdt, wcol,
    res, send, keep, toks, an, ant, dd, gfm, gout, gsl, pay, gpay,
):
    t = pl.program_id(0)

    @pl.when(t == 0)
    def _():
        join_halves(core[0], mine, other, pay)
        attention_step(pay, watt, an, ant, dd, toks)
        gfm[...] = jnp.zeros_like(gfm)
        gout[...] = jnp.zeros_like(gout)
        gsl[...] = jnp.zeros_like(gsl)

    mid_here = mid[...]
    temper, inv, logits, prob = slice_softmax(mid_here, bd[...])
    weights = prob.reshape(HS, BLOCK).astype(BF)
    dw = dot(an[:, :C], dmix[...], NT) + dot(an[:, C:], feat[...], NT) + dd[...]
    g = prob * dw.reshape(HEADS, SLICES, BLOCK)
    dl = g - prob * jnp.sum(g, axis=1, keepdims=True)
    d_temper = -jnp.sum(dl * logits, axis=1) * inv * jax.nn.sigmoid(temper)
    d_raw = (dl * inv[:, None, :]).reshape(HS, BLOCK).astype(BF)
    mixed_df = dot(ant[...], weights).astype(BF)
    spread = jnp.broadcast_to(d_temper[:, None, :], (HEADS, HEAD, BLOCK)).reshape(C, BLOCK)
    dm = (dot(bdt[...], d_raw) + spread * wcol[...]).astype(BF)
    res[: 2 * C] = mixed_df
    res[2 * C :] = dm
    normed_here = normed[...]
    gfm[:C] += dot(mixed_df[C:], normed_here)
    gfm[C:] += dot(dm, normed_here)
    gout[...] += dot(mixed_df[:C], cot[...])
    dt_hi = d_temper.astype(BF)
    dt_lo = (d_temper - dt_hi.astype(F32)).astype(BF)
    gsl[:HS] += dot(d_raw, mid_here)
    gsl[HS:] += dot(jnp.concatenate([dt_hi, dt_lo], axis=0), mid_here)

    @pl.when(t == B_DEV - 1)
    def _():
        grad_fm = gfm[...]
        gpay[: 2 * C] = grad_fm
        gpay[2 * C : 3 * C] = gout[...]
        gpay[3 * C : 3 * C + SLICES] = fold_heads(gsl[:HS])
        grad_gain = jnp.sum(grad_fm * wfmt[...].astype(F32), axis=0, keepdims=True) / gain[...]
        both = gsl[HS : HS + 8] + gsl[HS + 8 :]
        row = lax.broadcasted_iota(jnp.int32, (8, C), 0)
        lane_head = lax.broadcasted_iota(jnp.int32, (8, C), 1) // HEAD
        temper_row = jnp.sum(jnp.where(row == lane_head, both, 0.0), axis=0, keepdims=True)
        row = lax.broadcasted_iota(jnp.int32, (SLICES, C), 0)
        tail = jnp.where(row == 0, grad_gain, jnp.where(row == 1, temper_row, 0.0))
        gpay[3 * C + SLICES :] = tail
        split_halves(core[0], gpay, send, keep)


def out_kernel(ptsb, cot, res, gain, wfmt, wout, toks, layer, grad, gatt):
    @pl.when(pl.program_id(0) == 0)
    def _():
        attend_gradients(toks, gatt)

    points = ptsb[...]
    x_hat, inv_std = normalize(points)
    mixed_out = dot(res[:C], wout[...], TN)
    layer[...] = (points.astype(F32) + mixed_out).astype(BF)
    d_normed = dot(res[C:], wfmt[...], TN)
    scaled = d_normed * gain[...]
    mean_g = jnp.mean(scaled, axis=-1, keepdims=True)
    mean_gx = jnp.mean(scaled * x_hat, axis=-1, keepdims=True)
    grad[...] = (cot[...].astype(F32) + (scaled - mean_g - x_hat * mean_gx) * inv_std).astype(BF)


def unpack_kernel(core, mine, other, gfeat, gmid, gout, gslice, gtemper, ggain, full):
    join_halves(core[0], mine, other, full)
    gfeat[...] = full[:C].T
    gmid[...] = full[C : 2 * C].T
    gout[...] = full[2 * C : 3 * C]
    lane_in = lax.broadcasted_iota(jnp.int32, (C, HEAD), 0) % HEAD
    fold = (lane_in == lax.broadcasted_iota(jnp.int32, (C, HEAD), 1)).astype(F32)
    gslice[...] = dot_high(fold, full[3 * C : 3 * C + SLICES], (((0,), (1,)), ((), ())))
    tail = full[3 * C + SLICES : 3 * C + SLICES + 8]
    gtemper[...] = dot_high(tail, fold)[1:2]
    ggain[...] = tail[0:1]


def swap(array, even, odd):
    n = lax.axis_size("pts")
    return lax.ppermute(array, "pts", [(i, i ^ (odd if i % 2 else even)) for i in range(n)])


def quad_sum(x, even, odd, wire):
    w = x.astype(wire)
    a = swap(w, even, odd).astype(F32)
    b = swap(w, 2 * even, 2 * odd).astype(F32)
    c = swap(w, 3 * even, 3 * odd).astype(F32)
    return (w.astype(F32) + a) + (b + c)


def sum_over_chips(send, keep, wire):
    x = keep + swap(send, 1, 1).astype(F32)
    x = quad_sum(x, 2, 8, wire)
    x = quad_sum(x, 8, 32, wire)
    x = quad_sum(x, 32, 2, wire).astype(wire)
    return x, swap(x, 1, 1)


def shifted(array, by):
    n = lax.axis_size("pts")
    return lax.ppermute(array, "pts", [(i, i + by) for i in range(n) if 0 <= i + by < n])


def whole(shape):
    return pl.BlockSpec(shape, lambda t, *_: (0,) * len(shape))


def rows_spec(width):
    return pl.BlockSpec((BLOCK, width), lambda t, *_: (t, 0))


PARAMS = pltpu.CompilerParams(vmem_limit_bytes=24 * 1024 * 1024)
SCALARS = pl.BlockSpec(memory_space=pltpu.SMEM)
HBM = pl.BlockSpec(memory_space=pl.ANY)


def per_device(
    loader_points, cotangent, block_counts, dest_table, norm_gain, w_feature, w_middle,
    w_slice, w_temper, attend_weight, w_output,
):
    rank = lax.axis_index("pts").astype(jnp.int32).reshape(1)
    core = lax.rem(rank, 2)
    edge = jax.ShapeDtypeStruct((HALF * BLOCK, C), BF)
    head, tail = pl.pallas_call(
        pick_kernel,
        in_specs=[SCALARS, SCALARS, HBM],
        out_specs=[HBM, HBM],
        out_shape=[edge, edge],
        scratch_shapes=[pltpu.SemaphoreType.DMA((2,))],
        name="pick",
    )(rank, block_counts, loader_points)
    got_prev = shifted(tail, 1)
    got_next = shifted(head, -1)
    gain = norm_gain.reshape(1, C)
    sel, d_mixed, wfmt, bd, bdt, wcol, watt = pl.pallas_call(
        prep_kernel,
        in_specs=[SCALARS] * 3 + [pl.BlockSpec(memory_space=pltpu.VMEM)] * 7,
        out_specs=[SCALARS] + [pl.BlockSpec(memory_space=pltpu.VMEM)] * 6,
        out_shape=[
            jax.ShapeDtypeStruct((4, B_DEV), jnp.int32),
            jax.ShapeDtypeStruct((ROWS, C), BF),
            jax.ShapeDtypeStruct((2 * C, C), BF),
            jax.ShapeDtypeStruct((HS + 32, C), BF),
            jax.ShapeDtypeStruct((C, HS), BF),
            jax.ShapeDtypeStruct((C, 1), F32),
            jax.ShapeDtypeStruct((3, C, C), F32),
        ],
        compiler_params=PARAMS,
        cost_estimate=pl.CostEstimate(
            flops=2 * ROWS * C * C, bytes_accessed=4 * 1024 * 1024, transcendentals=0
        ),
        name="prep",
    )(
        rank, block_counts, dest_table, cotangent, w_output, w_feature, w_middle, w_slice,
        w_temper.reshape(1, HEAD), attend_weight,
    )

    wide = jax.ShapeDtypeStruct((ROWS, C), BF)
    half1 = jax.ShapeDtypeStruct((SLICES // 2, PAY1), F32)
    ptsb, normed, feat, mid, send, keep = pl.pallas_call(
        front_kernel,
        grid_spec=pltpu.PrefetchScalarGridSpec(
            num_scalar_prefetch=2,
            grid=(B_DEV,),
            in_specs=[
                pl.BlockSpec((BLOCK, C), lambda t, s, c: (s[0, t], 0)),
                pl.BlockSpec((BLOCK, C), lambda t, s, c: (s[1, t], 0)),
                pl.BlockSpec((BLOCK, C), lambda t, s, c: (s[2, t], 0)),
                rows_spec(C),
                whole((1, C)),
                whole((C, C)),
                whole((C, C)),
                whole((HS + 32, C)),
            ],
            out_specs=[rows_spec(C)] * 4 + [whole((SLICES // 2, PAY1))] * 2,
            scratch_shapes=[
                pltpu.VMEM((HS, 2 * C), F32),
                pltpu.VMEM((HS, 128), F32),
                pltpu.VMEM((SLICES, PAY1), F32),
            ],
        ),
        out_shape=[wide] * 4 + [half1] * 2,
        compiler_params=PARAMS,
        name="front",
    )(
        sel, core, loader_points, got_prev, got_next, d_mixed, gain, w_feature, w_middle, bd
    )

    mine, other = sum_over_chips(send, keep, F32)

    res, send, keep, toks = pl.pallas_call(
        back_kernel,
        grid=(B_DEV,),
        in_specs=[SCALARS]
        + [whole((SLICES // 2, PAY1))] * 2
        + [whole((3, C, C))]
        + [rows_spec(C)] * 5
        + [
            whole((1, C)),
            whole((2 * C, C)),
            whole((HS + 32, C)),
            whole((C, HS)),
            whole((C, 1)),
        ],
        out_specs=[
            pl.BlockSpec((3 * C, BLOCK), lambda t: (0, t)),
            whole((PAY2 // 2, C)),
            whole((PAY2 // 2, C)),
            whole((4, SLICES, C)),
        ],
        out_shape=[
            jax.ShapeDtypeStruct((3 * C, ROWS), BF),
            jax.ShapeDtypeStruct((PAY2 // 2, C), BF),
            jax.ShapeDtypeStruct((PAY2 // 2, C), F32),
            jax.ShapeDtypeStruct((4, SLICES, C), F32),
        ],
        scratch_shapes=[
            pltpu.VMEM((HS, 2 * C), BF),
            pltpu.VMEM((2 * C, HS), BF),
            pltpu.VMEM((HS, 1), F32),
            pltpu.VMEM((2 * C, C), F32),
            pltpu.VMEM((C, C), F32),
            pltpu.VMEM((HS + 16, C), F32),
            pltpu.VMEM((SLICES, PAY1), F32),
            pltpu.VMEM((PAY2, C), F32),
        ],
        compiler_params=PARAMS,
        name="back",
    )(
        core, mine, other, watt, normed, feat, mid, d_mixed, cotangent, gain, wfmt, bd, bdt, wcol
    )

    layer_out, grad_points, grad_attend = pl.pallas_call(
        out_kernel,
        grid=(B_DEV,),
        in_specs=[
            rows_spec(C),
            rows_spec(C),
            pl.BlockSpec((3 * C, BLOCK), lambda t: (0, t)),
            whole((1, C)),
            whole((2 * C, C)),
            whole((C, C)),
            whole((4, SLICES, C)),
        ],
        out_specs=[rows_spec(C)] * 2 + [whole((3, HEAD, HEAD))],
        out_shape=[wide] * 2 + [jax.ShapeDtypeStruct((3, HEAD, HEAD), F32)],
        compiler_params=PARAMS,
        cost_estimate=pl.CostEstimate(
            flops=2 * ROWS * C * 3 * C, bytes_accessed=7 * ROWS * C * 2, transcendentals=0
        ),
        name="outputs",
    )(ptsb, cotangent, res, gain, wfmt, w_output, toks)

    mine, other = sum_over_chips(send, keep, BF)
    vmem = pl.BlockSpec(memory_space=pltpu.VMEM)
    grad_feature, grad_middle, grad_output, grad_slice, grad_temper, grad_gain = pl.pallas_call(
        unpack_kernel,
        in_specs=[SCALARS, vmem, vmem],
        out_specs=[vmem] * 6,
        out_shape=[
            jax.ShapeDtypeStruct((C, C), F32),
            jax.ShapeDtypeStruct((C, C), F32),
            jax.ShapeDtypeStruct((C, C), F32),
            jax.ShapeDtypeStruct((HEAD, SLICES), F32),
            jax.ShapeDtypeStruct((1, HEAD), F32),
            jax.ShapeDtypeStruct((1, C), F32),
        ],
        scratch_shapes=[pltpu.VMEM((PAY2, C), F32)],
        compiler_params=PARAMS,
        name="unpack",
    )(core, mine, other)
    return (
        layer_out,
        grad_points,
        grad_gain.reshape(C),
        grad_feature,
        grad_middle,
        grad_slice,
        grad_temper.reshape(HEAD),
        grad_attend,
        grad_output,
    )


def solution(mesh):
    return jax.shard_map(
        per_device,
        mesh=mesh,
        in_specs=(P("pts", None), P("pts", None), P(), P("pts"), P(), P(), P(), P(), P(), P(), P()),
        out_specs=(P("pts", None), P("pts", None), P(), P(), P(), P(), P(), P(), P()),
        check_vma=False,
    )
```

```python
import math

import jax
import jax.numpy as jnp
from jax import lax
from jax.experimental import pallas as pl
from jax.experimental.pallas import tpu as pltpu
from jax.sharding import PartitionSpec as P

BLOCK = 512
B_DEV = 4
HALF = 2
CAP = 8
C = 256
HEADS = 8
HEAD = 32
SLICES = 64
HS = HEADS * SLICES
ROWS = B_DEV * BLOCK
PAY1 = 640
PAY2 = 896
BF = jnp.bfloat16
F32 = jnp.float32
HIGH = lax.Precision.HIGHEST
NN = (((1,), (0,)), ((), ()))
NT = (((1,), (1,)), ((), ()))
TN = (((0,), (0,)), ((), ()))


def dot(a, b, dims=NN):
    return lax.dot_general(a, b, dims, preferred_element_type=F32)


def dot_high(a, b, dims=NN):
    return lax.dot_general(a, b, dims, precision=HIGH, preferred_element_type=F32)


def head_mask(rows):
    row_head = lax.broadcasted_iota(jnp.int32, (rows, C), 0) // SLICES
    lane_head = lax.broadcasted_iota(jnp.int32, (rows, C), 1) // HEAD
    return row_head == lane_head


def fold_heads(full):
    masked = jnp.where(head_mask(HS), full, 0.0)
    return jnp.sum(masked.reshape(HEADS, SLICES, C), axis=0)


def spread_heads(small):
    tiled = jnp.concatenate([small] * HEADS, axis=0)
    return jnp.where(head_mask(HS), tiled, 0.0)


def normalize(points):
    point_f = points.astype(F32)
    center = point_f - jnp.mean(point_f, axis=-1, keepdims=True)
    inv_std = lax.rsqrt(jnp.mean(center * center, axis=-1, keepdims=True) + 1e-05)
    return center * inv_std, inv_std


def slice_softmax(mid, bd):
    out = dot(bd, mid, NT)
    width = mid.shape[0]
    temper = out[HS : HS + 8] + out[HS + 8 : HS + 16] + out[HS + 16 : HS + 24]
    scale = 0.5 + jnp.maximum(temper, 0.0) + jnp.log1p(jnp.exp(-jnp.abs(temper)))
    inv = 1.0 / scale
    logits = out[:HS].reshape(HEADS, SLICES, width) * inv[:, None, :]
    top = jnp.max(logits, axis=1, keepdims=True)
    e = jnp.exp(logits - top)
    prob = e * (1.0 / jnp.sum(e, axis=1, keepdims=True))
    return temper, inv, logits, prob


def split_halves(core, full, send, keep):
    half = full.shape[0] // 2

    @pl.when(core == 0)
    def _():
        keep[...] = full[:half].astype(keep.dtype)
        send[...] = full[half:].astype(send.dtype)

    @pl.when(core != 0)
    def _():
        keep[...] = full[half:].astype(keep.dtype)
        send[...] = full[:half].astype(send.dtype)


def join_halves(core, mine, other, full):
    half = full.shape[0] // 2

    @pl.when(core == 0)
    def _():
        full[:half] = mine[...].astype(full.dtype)
        full[half:] = other[...].astype(full.dtype)

    @pl.when(core != 0)
    def _():
        full[:half] = other[...].astype(full.dtype)
        full[half:] = mine[...].astype(full.dtype)


def pick_kernel(rank, counts, first, last, head, tail):
    head[...] = first[...]
    tail[...] = last[...]


def prep_kernel(
    rank, counts, table, cot, wout, wf, wm, ws, wt, attw,
    sel, dmix, wfmt, bd, bdt, wcol, watt,
):
    here = rank[0]
    found, own = [], []
    for t in range(B_DEV):
        slot = jnp.int32(0)
        hit = jnp.int32(0)
        for s in range(CAP):
            same = table[s] == here * B_DEV + t
            slot = jnp.where(same, s, slot)
            hit = jnp.where(same, 1, hit)
        own.append(slot)
        found.append(hit)
    from_prev = 2 - found[0] - found[1]
    from_next = 2 - found[2] - found[3]
    left = counts[jnp.maximum(here - 1, 0)]
    start = jnp.maximum(left - HALF, 0)
    for t in range(B_DEV):
        sel[0, t] = own[t]
        sel[1, t] = jnp.clip(left - from_prev + t - start, 0, HALF - 1)
        sel[2, t] = jnp.clip(t - (B_DEV - from_next), 0, HALF - 1)
        sel[3, t] = jnp.where(found[t] == 1, 0, 1 if t < HALF else 2)

    dmix[...] = dot(cot[...], wout[...], NT).astype(BF)
    wfmt[:C] = wf[...].T
    wfmt[C:] = wm[...].T
    lane_in = lax.broadcasted_iota(jnp.int32, (HEAD, C), 1) % HEAD
    spread = (lax.broadcasted_iota(jnp.int32, (HEAD, C), 0) == lane_in).astype(F32)
    slice_rows = dot(ws[...], spread.astype(BF), TN)
    slice_bd = spread_heads(slice_rows)
    bd[:HS] = slice_bd.astype(BF)
    bdt[...] = slice_bd.T.astype(BF)
    temper = dot_high(wt[...], spread)
    hi = temper.astype(BF).astype(F32)
    middle = (temper - hi).astype(BF).astype(F32)
    low = temper - hi - middle
    row = lax.broadcasted_iota(jnp.int32, (8, C), 0)
    own_head = row == lax.broadcasted_iota(jnp.int32, (8, C), 1) // HEAD
    parts = [jnp.where(own_head, part, 0.0) for part in (hi, middle, low)]
    bd[HS:] = jnp.concatenate(parts + [jnp.zeros((8, C), F32)], axis=0).astype(BF)
    rows = lax.broadcasted_iota(jnp.int32, (C, C), 0)
    cols = lax.broadcasted_iota(jnp.int32, (C, C), 1)
    wcol[...] = jnp.sum(jnp.where(rows == cols, temper, 0.0), axis=1, keepdims=True)
    same_head = rows // HEAD == cols // HEAD
    for i in range(3):
        wide = dot_high(attw[i], spread)
        watt[i] = jnp.where(same_head, jnp.concatenate([wide] * HEADS, axis=0), 0.0)


def front_kernel(
    sel, core, own, prev, nxt, dmix, gain, wf, wm, bd,
    ptsb, normed_out, feat_out, mid_out, send, keep, acc, den, pay
):
    t = pl.program_id(0)
    kind = sel[3, t]

    @pl.when(kind == 0)
    def _():
        ptsb[...] = own[...]

    @pl.when(kind == 1)
    def _():
        ptsb[...] = prev[...]

    @pl.when(kind == 2)
    def _():
        ptsb[...] = nxt[...]

    x_hat, _ = normalize(ptsb[...])
    normed = (x_hat * gain[...]).astype(BF)
    normed_out[...] = normed
    feat = dot(normed, wf[...]).astype(BF)
    mid = dot(normed, wm[...]).astype(BF)
    feat_out[...] = feat
    mid_out[...] = mid
    _, _, _, prob = slice_softmax(mid, bd[...])
    weights = prob.reshape(HS, BLOCK).astype(BF)

    @pl.when(t == 0)
    def _():
        acc[...] = jnp.zeros_like(acc)
        den[...] = jnp.zeros_like(den)

    acc[:, :C] += dot(weights, feat)
    acc[:, C:] += dot(weights, dmix[...])
    wf = weights.astype(F32)
    den[...] += sum(wf[:, i * 128 : (i + 1) * 128] for i in range(BLOCK // 128))

    @pl.when(t == B_DEV - 1)
    def _():
        pay[:, :C] = fold_heads(acc[:, :C])
        pay[:, C : 2 * C] = fold_heads(acc[:, C:])
        total = jnp.sum(den[...], axis=1, keepdims=True)
        row_head = lax.broadcasted_iota(jnp.int32, (HS, 128), 0) // SLICES
        lane = lax.broadcasted_iota(jnp.int32, (HS, 128), 1)
        placed = jnp.where(row_head == lane, total, 0.0)
        pay[:, 2 * C :] = jnp.sum(placed.reshape(HEADS, SLICES, 128), axis=0)
        split_halves(core[0], pay, send, keep)


def attention_step(pay, watt, an, ant, dd, toks):
    numer = pay[:, :C]
    deslice = pay[:, C : 2 * C]
    head_of_lane = lax.broadcasted_iota(jnp.int32, (128, C), 1) // HEAD
    expand = (lax.broadcasted_iota(jnp.int32, (128, C), 0) == head_of_lane).astype(F32)
    inv_den = 1.0 / (dot_high(pay[:, 2 * C :], expand) + 1e-05)
    tokens = numer * inv_den
    mask = head_mask(HS)
    q = dot_high(tokens, watt[0])
    k = dot_high(tokens, watt[1])
    v = dot_high(tokens, watt[2])
    q_bd = spread_heads(q)
    root = 1.0 / math.sqrt(HEAD)
    scores = dot_high(q_bd, k, NT) * root
    top = jnp.max(scores, axis=-1, keepdims=True)
    e = jnp.exp(scores - top)
    att = e / jnp.sum(e, axis=-1, keepdims=True)
    attended = jnp.where(mask, dot_high(att, v), 0.0)
    do_bd = spread_heads(deslice)
    dv = dot_high(att, do_bd, TN)
    d_att = dot_high(do_bd, v, NT)
    ds = att * (d_att - jnp.sum(att * d_att, axis=-1, keepdims=True)) * root
    dq = fold_heads(dot_high(ds, k))
    dk = dot_high(ds, q_bd, TN)
    d_tokens = (
        dot_high(dq, watt[0], NT) + dot_high(dk, watt[1], NT) + dot_high(dv, watt[2], NT)
    )
    d_numer = d_tokens * inv_den
    d_den = -d_numer * tokens
    dd[...] = jnp.sum(spread_heads(d_den), axis=1, keepdims=True)
    d_numer_bd = spread_heads(d_numer)
    an[:, :C] = attended.astype(BF)
    an[:, C:] = d_numer_bd.astype(BF)
    ant[:C] = attended.T.astype(BF)
    ant[C:] = d_numer_bd.T.astype(BF)
    toks[0] = tokens
    toks[1] = dq
    toks[2] = dk
    toks[3] = dv


def attend_gradients(toks, gatt):
    row_head = lax.broadcasted_iota(jnp.int32, (C, C), 0) // HEAD
    col_head = lax.broadcasted_iota(jnp.int32, (C, C), 1) // HEAD
    same = row_head == col_head
    lane_in = lax.broadcasted_iota(jnp.int32, (C, HEAD), 0) % HEAD
    fold = (lane_in == lax.broadcasted_iota(jnp.int32, (C, HEAD), 1)).astype(F32)
    for i in range(3):
        full = jnp.where(same, dot_high(toks[0], toks[i + 1], TN), 0.0)
        packed = dot_high(full, fold)
        gatt[i] = jnp.sum(packed.reshape(HEADS, HEAD, HEAD), axis=0)


def back_kernel(
    core, mine, other, watt, normed, feat, mid, dmix, cot, gain, wfmt, bd, bdt, wcol,
    res, send, keep, toks, an, ant, dd, gfm, gout, gsl, pay, gpay,
):
    t = pl.program_id(0)

    @pl.when(t == 0)
    def _():
        join_halves(core[0], mine, other, pay)
        attention_step(pay, watt, an, ant, dd, toks)
        gfm[...] = jnp.zeros_like(gfm)
        gout[...] = jnp.zeros_like(gout)
        gsl[...] = jnp.zeros_like(gsl)

    mid_here = mid[...]
    temper, inv, logits, prob = slice_softmax(mid_here, bd[...])
    weights = prob.reshape(HS, BLOCK).astype(BF)
    dw = dot(an[:, :C], dmix[...], NT) + dot(an[:, C:], feat[...], NT) + dd[...]
    g = prob * dw.reshape(HEADS, SLICES, BLOCK)
    dl = g - prob * jnp.sum(g, axis=1, keepdims=True)
    d_temper = -jnp.sum(dl * logits, axis=1) * inv * jax.nn.sigmoid(temper)
    d_raw = (dl * inv[:, None, :]).reshape(HS, BLOCK).astype(BF)
    mixed_df = dot(ant[...], weights).astype(BF)
    spread = jnp.broadcast_to(d_temper[:, None, :], (HEADS, HEAD, BLOCK)).reshape(C, BLOCK)
    dm = (dot(bdt[...], d_raw) + spread * wcol[...]).astype(BF)
    res[: 2 * C] = mixed_df
    res[2 * C :] = dm
    normed_here = normed[...]
    gfm[:C] += dot(mixed_df[C:], normed_here)
    gfm[C:] += dot(dm, normed_here)
    gout[...] += dot(mixed_df[:C], cot[...])
    dt_hi = d_temper.astype(BF)
    dt_lo = (d_temper - dt_hi.astype(F32)).astype(BF)
    gsl[:HS] += dot(d_raw, mid_here)
    gsl[HS:] += dot(jnp.concatenate([dt_hi, dt_lo], axis=0), mid_here)

    @pl.when(t == B_DEV - 1)
    def _():
        grad_fm = gfm[...]
        gpay[: 2 * C] = grad_fm
        gpay[2 * C : 3 * C] = gout[...]
        gpay[3 * C : 3 * C + SLICES] = fold_heads(gsl[:HS])
        grad_gain = jnp.sum(grad_fm * wfmt[...].astype(F32), axis=0, keepdims=True) / gain[...]
        both = gsl[HS : HS + 8] + gsl[HS + 8 :]
        row = lax.broadcasted_iota(jnp.int32, (8, C), 0)
        lane_head = lax.broadcasted_iota(jnp.int32, (8, C), 1) // HEAD
        temper_row = jnp.sum(jnp.where(row == lane_head, both, 0.0), axis=0, keepdims=True)
        row = lax.broadcasted_iota(jnp.int32, (SLICES, C), 0)
        tail = jnp.where(row == 0, grad_gain, jnp.where(row == 1, temper_row, 0.0))
        gpay[3 * C + SLICES :] = tail
        split_halves(core[0], gpay, send, keep)


def out_kernel(ptsb, cot, res, gain, wfmt, wout, layer, grad):
    points = ptsb[...]
    x_hat, inv_std = normalize(points)
    mixed_out = dot(res[:C], wout[...], TN)
    layer[...] = (points.astype(F32) + mixed_out).astype(BF)
    d_normed = dot(res[C:], wfmt[...], TN)
    scaled = d_normed * gain[...]
    mean_g = jnp.mean(scaled, axis=-1, keepdims=True)
    mean_gx = jnp.mean(scaled * x_hat, axis=-1, keepdims=True)
    grad[...] = (cot[...].astype(F32) + (scaled - mean_g - x_hat * mean_gx) * inv_std).astype(BF)


def unpack_kernel(core, mine, other, gfeat, gmid, gout, gslice, gtemper, ggain, full):
    join_halves(core[0], mine, other, full)
    gfeat[...] = full[:C].T
    gmid[...] = full[C : 2 * C].T
    gout[...] = full[2 * C : 3 * C]
    lane_in = lax.broadcasted_iota(jnp.int32, (C, HEAD), 0) % HEAD
    fold = (lane_in == lax.broadcasted_iota(jnp.int32, (C, HEAD), 1)).astype(F32)
    gslice[...] = dot_high(fold, full[3 * C : 3 * C + SLICES], (((0,), (1,)), ((), ())))
    tail = full[3 * C + SLICES : 3 * C + SLICES + 8]
    gtemper[...] = dot_high(tail, fold)[1:2]
    ggain[...] = tail[0:1]


def swap(array, even, odd):
    n = lax.axis_size("pts")
    return lax.ppermute(array, "pts", [(i, i ^ (odd if i % 2 else even)) for i in range(n)])


def quad_sum(x, even, odd, wire):
    w = x.astype(wire)
    a = swap(w, even, odd).astype(F32)
    b = swap(w, 2 * even, 2 * odd).astype(F32)
    c = swap(w, 3 * even, 3 * odd).astype(F32)
    return (w.astype(F32) + a) + (b + c)


def sum_over_chips(send, keep, wire, beside=()):
    x = keep + swap(send, 1, 1).astype(F32)
    done = []
    for i, (even, odd) in enumerate(((2, 8), (8, 32), (32, 2))):
        x = quad_sum(x, even, odd, wire)
        for at, arrays in beside:
            if at == i:
                x, arrays = lax.optimization_barrier((x, arrays))
                done.append(arrays)
    x = x.astype(wire)
    return x, swap(x, 1, 1), done


def shifted(array, by):
    n = lax.axis_size("pts")
    return lax.ppermute(array, "pts", [(i, i + by) for i in range(n) if 0 <= i + by < n])


def whole(shape):
    return pl.BlockSpec(shape, lambda t, *_: (0,) * len(shape))


def rows_spec(width):
    return pl.BlockSpec((BLOCK, width), lambda t, *_: (t, 0))


PARAMS = pltpu.CompilerParams(vmem_limit_bytes=24 * 1024 * 1024)
SCALARS = pl.BlockSpec(memory_space=pltpu.SMEM)
HBM = pl.BlockSpec(memory_space=pl.ANY)


def per_device(
    loader_points, cotangent, block_counts, dest_table, norm_gain, w_feature, w_middle,
    w_slice, w_temper, attend_weight, w_output,
):
    rank = lax.axis_index("pts").astype(jnp.int32).reshape(1)
    core = lax.rem(rank, 2)
    edge = jax.ShapeDtypeStruct((HALF * BLOCK, C), BF)

    def last_slots(t, rank, counts):
        return (jnp.maximum(counts[rank[0]] - HALF, 0) + t, 0)

    head, tail = pl.pallas_call(
        pick_kernel,
        grid_spec=pltpu.PrefetchScalarGridSpec(
            num_scalar_prefetch=2,
            grid=(HALF,),
            in_specs=[rows_spec(C), pl.BlockSpec((BLOCK, C), last_slots)],
            out_specs=[rows_spec(C)] * 2,
        ),
        out_shape=[edge, edge],
        name="pick",
    )(rank, block_counts, loader_points, loader_points)
    got_prev = shifted(tail, 1)
    got_next = shifted(head, -1)
    gain = norm_gain.reshape(1, C)
    sel, d_mixed, wfmt, bd, bdt, wcol, watt = pl.pallas_call(
        prep_kernel,
        grid=(1,),
        in_specs=[SCALARS] * 3
        + [
            whole((ROWS, C)),
            whole((C, C)),
            whole((C, C)),
            whole((C, C)),
            whole((HEAD, SLICES)),
            whole((1, HEAD)),
            whole((3, HEAD, HEAD)),
        ],
        out_specs=[
            SCALARS,
            whole((ROWS, C)),
            whole((2 * C, C)),
            whole((HS + 32, C)),
            whole((C, HS)),
            whole((C, 1)),
            whole((3, C, C)),
        ],
        out_shape=[
            jax.ShapeDtypeStruct((4, B_DEV), jnp.int32),
            jax.ShapeDtypeStruct((ROWS, C), BF),
            jax.ShapeDtypeStruct((2 * C, C), BF),
            jax.ShapeDtypeStruct((HS + 32, C), BF),
            jax.ShapeDtypeStruct((C, HS), BF),
            jax.ShapeDtypeStruct((C, 1), F32),
            jax.ShapeDtypeStruct((3, C, C), F32),
        ],
        compiler_params=PARAMS,
        cost_estimate=pl.CostEstimate(
            flops=2 * ROWS * C * C, bytes_accessed=4 * 1024 * 1024, transcendentals=0
        ),
        name="prep",
    )(
        rank, block_counts, dest_table, cotangent, w_output, w_feature, w_middle, w_slice,
        w_temper.reshape(1, HEAD), attend_weight,
    )

    wide = jax.ShapeDtypeStruct((ROWS, C), BF)
    half1 = jax.ShapeDtypeStruct((SLICES // 2, PAY1), F32)
    ptsb, normed, feat, mid, send, keep = pl.pallas_call(
        front_kernel,
        grid_spec=pltpu.PrefetchScalarGridSpec(
            num_scalar_prefetch=2,
            grid=(B_DEV,),
            in_specs=[
                pl.BlockSpec((BLOCK, C), lambda t, s, c: (s[0, t], 0)),
                pl.BlockSpec((BLOCK, C), lambda t, s, c: (s[1, t], 0)),
                pl.BlockSpec((BLOCK, C), lambda t, s, c: (s[2, t], 0)),
                rows_spec(C),
                whole((1, C)),
                whole((C, C)),
                whole((C, C)),
                whole((HS + 32, C)),
            ],
            out_specs=[rows_spec(C)] * 4 + [whole((SLICES // 2, PAY1))] * 2,
            scratch_shapes=[
                pltpu.VMEM((HS, 2 * C), F32),
                pltpu.VMEM((HS, 128), F32),
                pltpu.VMEM((SLICES, PAY1), F32),
            ],
        ),
        out_shape=[wide] * 4 + [half1] * 2,
        compiler_params=PARAMS,
        name="front",
    )(
        sel, core, loader_points, got_prev, got_next, d_mixed, gain, w_feature, w_middle, bd
    )

    mine, other, _ = sum_over_chips(send, keep, F32)

    res, send, keep, toks = pl.pallas_call(
        back_kernel,
        grid=(B_DEV,),
        in_specs=[SCALARS]
        + [whole((SLICES // 2, PAY1))] * 2
        + [whole((3, C, C))]
        + [rows_spec(C)] * 5
        + [
            whole((1, C)),
            whole((2 * C, C)),
            whole((HS + 32, C)),
            whole((C, HS)),
            whole((C, 1)),
        ],
        out_specs=[
            pl.BlockSpec((3 * C, BLOCK), lambda t: (0, t)),
            whole((PAY2 // 2, C)),
            whole((PAY2 // 2, C)),
            whole((4, SLICES, C)),
        ],
        out_shape=[
            jax.ShapeDtypeStruct((3 * C, ROWS), BF),
            jax.ShapeDtypeStruct((PAY2 // 2, C), BF),
            jax.ShapeDtypeStruct((PAY2 // 2, C), F32),
            jax.ShapeDtypeStruct((4, SLICES, C), F32),
        ],
        scratch_shapes=[
            pltpu.VMEM((HS, 2 * C), BF),
            pltpu.VMEM((2 * C, HS), BF),
            pltpu.VMEM((HS, 1), F32),
            pltpu.VMEM((2 * C, C), F32),
            pltpu.VMEM((C, C), F32),
            pltpu.VMEM((HS + 16, C), F32),
            pltpu.VMEM((SLICES, PAY1), F32),
            pltpu.VMEM((PAY2, C), F32),
        ],
        compiler_params=PARAMS,
        name="back",
    )(
        core, mine, other, watt, normed, feat, mid, d_mixed, cotangent, gain, wfmt, bd, bdt, wcol
    )

    layer_out, grad_points = pl.pallas_call(
        out_kernel,
        grid=(B_DEV,),
        in_specs=[
            rows_spec(C),
            rows_spec(C),
            pl.BlockSpec((3 * C, BLOCK), lambda t: (0, t)),
            whole((1, C)),
            whole((2 * C, C)),
            whole((C, C)),
        ],
        out_specs=[rows_spec(C)] * 2,
        out_shape=[wide] * 2,
        compiler_params=PARAMS,
        cost_estimate=pl.CostEstimate(
            flops=2 * ROWS * C * 3 * C, bytes_accessed=7 * ROWS * C * 2, transcendentals=0
        ),
        name="outputs",
    )(ptsb, cotangent, res, gain, wfmt, w_output)

    grad_attend = pl.pallas_call(
        attend_gradients,
        out_shape=jax.ShapeDtypeStruct((3, HEAD, HEAD), F32),
        compiler_params=PARAMS,
        name="attend_grads",
    )(toks)

    beside = ((0, (layer_out, grad_points)), (1, grad_attend))
    mine, other, done = sum_over_chips(send, keep, BF, beside)
    (layer_out, grad_points), grad_attend = done
    vmem = pl.BlockSpec(memory_space=pltpu.VMEM)
    grad_feature, grad_middle, grad_output, grad_slice, grad_temper, grad_gain = pl.pallas_call(
        unpack_kernel,
        in_specs=[SCALARS, vmem, vmem],
        out_specs=[vmem] * 6,
        out_shape=[
            jax.ShapeDtypeStruct((C, C), F32),
            jax.ShapeDtypeStruct((C, C), F32),
            jax.ShapeDtypeStruct((C, C), F32),
            jax.ShapeDtypeStruct((HEAD, SLICES), F32),
            jax.ShapeDtypeStruct((1, HEAD), F32),
            jax.ShapeDtypeStruct((1, C), F32),
        ],
        scratch_shapes=[pltpu.VMEM((PAY2, C), F32)],
        compiler_params=PARAMS,
        name="unpack",
    )(core, mine, other)
    return (
        layer_out,
        grad_points,
        grad_gain.reshape(C),
        grad_feature,
        grad_middle,
        grad_slice,
        grad_temper.reshape(HEAD),
        grad_attend,
        grad_output,
    )


def solution(mesh):
    return jax.shard_map(
        per_device,
        mesh=mesh,
        in_specs=(P("pts", None), P("pts", None), P(), P("pts"), P(), P(), P(), P(), P(), P(), P()),
        out_specs=(P("pts", None), P("pts", None), P(), P(), P(), P(), P(), P(), P()),
        check_vma=False,
    )
```

```python
import math

import jax
import jax.numpy as jnp
from jax import lax
from jax.experimental import pallas as pl
from jax.experimental.pallas import tpu as pltpu
from jax.sharding import PartitionSpec as P

BLOCK = 512
B_DEV = 4
HALF = 2
CAP = 8
C = 256
HEADS = 8
HEAD = 32
SLICES = 64
HS = HEADS * SLICES
ROWS = B_DEV * BLOCK
PAY1 = 640
PAY2 = 896
BF = jnp.bfloat16
F32 = jnp.float32
HIGH = lax.Precision.HIGH
G = C // 2
GS = HS // 2
NN = (((1,), (0,)), ((), ()))
NT = (((1,), (1,)), ((), ()))
TN = (((0,), (0,)), ((), ()))


def dot(a, b, dims=NN):
    return lax.dot_general(a, b, dims, preferred_element_type=F32)


def dot_high(a, b, dims=NN):
    return lax.dot_general(a, b, dims, precision=HIGH, preferred_element_type=F32)


def head_mask(rows):
    row_head = lax.broadcasted_iota(jnp.int32, (rows, C), 0) // SLICES
    lane_head = lax.broadcasted_iota(jnp.int32, (rows, C), 1) // HEAD
    return row_head == lane_head


def fold_heads(full):
    masked = jnp.where(head_mask(HS), full, 0.0)
    return jnp.sum(masked.reshape(HEADS, SLICES, C), axis=0)


def spread_heads(small):
    tiled = jnp.concatenate([small] * HEADS, axis=0)
    return jnp.where(head_mask(HS), tiled, 0.0)


def normalize(points):
    point_f = points.astype(F32)
    center = point_f - jnp.mean(point_f, axis=-1, keepdims=True)
    inv_std = lax.rsqrt(jnp.mean(center * center, axis=-1, keepdims=True) + 1e-05)
    return center * inv_std, inv_std


def slice_softmax(mid_t, bd):
    out = dot(bd, mid_t)
    width = mid_t.shape[1]
    temper = out[HS : HS + 8] + out[HS + 8 : HS + 16] + out[HS + 16 : HS + 24]
    scale = 0.5 + jnp.maximum(temper, 0.0) + jnp.log1p(jnp.exp(-jnp.abs(temper)))
    inv = 1.0 / scale
    powers = out[:HS].reshape(HEADS, SLICES, width) * (inv * math.log2(math.e))[:, None, :]
    top = jnp.max(powers, axis=1, keepdims=True)
    e = jnp.exp2(powers - top)
    prob = e * (1.0 / jnp.sum(e, axis=1, keepdims=True))
    return temper, inv, prob


def split_halves(core, full, send, keep):
    half = full.shape[0] // 2

    @pl.when(core == 0)
    def _():
        keep[...] = full[:half].astype(keep.dtype)
        send[...] = full[half:].astype(send.dtype)

    @pl.when(core != 0)
    def _():
        keep[...] = full[half:].astype(keep.dtype)
        send[...] = full[:half].astype(send.dtype)


def join_halves(core, mine, other, full):
    half = full.shape[0] // 2

    @pl.when(core == 0)
    def _():
        full[:half] = mine[...].astype(full.dtype)
        full[half:] = other[...].astype(full.dtype)

    @pl.when(core != 0)
    def _():
        full[:half] = other[...].astype(full.dtype)
        full[half:] = mine[...].astype(full.dtype)


def pick_kernel(rank, counts, inner, outer, inner_out, outer_out):
    inner_out[...] = inner[...]
    outer_out[...] = outer[...]


def prep_kernel(
    rank, counts, table, cot, wout, wf, wm, ws, wt, attw,
    sel, dmix, wfmt, bd, bdt, wcol, watt,
):
    here = rank[0]
    found, own = [], []
    for t in range(B_DEV):
        slot = jnp.int32(0)
        hit = jnp.int32(0)
        for s in range(CAP):
            same = table[s] == here * B_DEV + t
            slot = jnp.where(same, s, slot)
            hit = jnp.where(same, 1, hit)
        own.append(slot)
        found.append(hit)
    from_prev = 2 - found[0] - found[1]
    from_next = 2 - found[2] - found[3]
    left = counts[jnp.maximum(here - 1, 0)]
    start = jnp.maximum(left - HALF, 0)
    for t in range(B_DEV):
        sel[0, t] = own[t]
        place = left - from_prev + t - start if t < HALF else t - (B_DEV - from_next)
        sel[1, t] = jnp.clip(place, 0, HALF - 1)
        sel[2, t] = found[t]

    dmix[...] = dot(cot[...], wout[...], NT).astype(BF)
    wfmt[:C] = wf[...].T
    wfmt[C:] = wm[...].T
    lane_in = lax.broadcasted_iota(jnp.int32, (HEAD, C), 1) % HEAD
    spread = (lax.broadcasted_iota(jnp.int32, (HEAD, C), 0) == lane_in).astype(F32)
    slice_rows = dot(ws[...], spread.astype(BF), TN)
    slice_bd = spread_heads(slice_rows)
    bd[:HS] = slice_bd.astype(BF)
    bdt[...] = slice_bd.T.astype(BF)
    temper = dot_high(wt[...], spread)
    hi = temper.astype(BF).astype(F32)
    middle = (temper - hi).astype(BF).astype(F32)
    low = temper - hi - middle
    row = lax.broadcasted_iota(jnp.int32, (8, C), 0)
    own_head = row == lax.broadcasted_iota(jnp.int32, (8, C), 1) // HEAD
    parts = [jnp.where(own_head, part, 0.0) for part in (hi, middle, low)]
    bd[HS:] = jnp.concatenate(parts + [jnp.zeros((8, C), F32)], axis=0).astype(BF)
    rows = lax.broadcasted_iota(jnp.int32, (C, C), 0)
    cols = lax.broadcasted_iota(jnp.int32, (C, C), 1)
    wcol[...] = jnp.sum(jnp.where(rows == cols, temper, 0.0), axis=1, keepdims=True)
    same_head = rows // HEAD == cols // HEAD
    for i in range(3):
        wide = dot_high(attw[i], spread)
        watt[i] = jnp.where(same_head, jnp.concatenate([wide] * HEADS, axis=0), 0.0)


def first_tile(t, core):
    return t + HALF * (1 - core[0])


def second_tile(t, core):
    return t + HALF * core[0]


def front_first(sel, core, own, other, dmix, gain, wf, wmt, bd, *outs):
    *arrays, pay, acc, den = outs
    tile = first_tile(pl.program_id(0), core)
    front_tile(sel[2, tile], own, other, dmix, gain, wf, wmt, bd, *arrays, acc, den)

    @pl.when(pl.program_id(0) == HALF - 1)
    def _():
        fold_sums(acc, den, pay)


def front_second(sel, core, own, other, dmix, gain, wf, wmt, bd, pay_first, *rest):
    *arrays, send, keep, acc, den, pay = rest[6:]
    tile = second_tile(pl.program_id(0), core)
    front_tile(sel[2, tile], own, other, dmix, gain, wf, wmt, bd, *arrays, acc, den)

    @pl.when(pl.program_id(0) == HALF - 1)
    def _():
        fold_sums(acc, den, pay)
        pay[...] += pay_first[...]
        split_halves(core[0], pay, send, keep)


def front_tile(
    found, own, other, dmix, gain, wf, wmt, bd,
    ptsb, normed_out, feat_out, mid_out, prob_out, aux, acc, den,
):
    t = pl.program_id(0)

    @pl.when(found == 1)
    def _():
        ptsb[...] = own[...]

    @pl.when(found != 1)
    def _():
        ptsb[...] = other[...]

    x_hat, _ = normalize(ptsb[...])
    normed = (x_hat * gain[...]).astype(BF)
    normed_out[...] = normed
    feat = dot(normed, wf[...]).astype(BF)
    mid_t = dot(wmt[...], normed, NT).astype(BF)
    feat_out[...] = feat
    mid_out[...] = mid_t
    temper, inv, prob = slice_softmax(mid_t, bd[...])
    prob_out[...] = prob.reshape(HS, BLOCK)
    aux[:HEADS] = inv
    aux[HEADS:] = inv * jax.nn.sigmoid(temper)
    weights = prob.reshape(HS, BLOCK).astype(BF)

    @pl.when(t == 0)
    def _():
        acc[...] = jnp.zeros_like(acc)
        den[...] = jnp.zeros_like(den)

    grad = dmix[...]
    for i in range(2):
        both = jnp.concatenate([feat[:, i * G : (i + 1) * G], grad[:, i * G : (i + 1) * G]], axis=1)
        acc[i * GS : (i + 1) * GS] += dot(weights[i * GS : (i + 1) * GS], both)
    den[...] += dot(weights, jnp.ones((BLOCK, 128), BF))


def fold_sums(acc, den, pay):
    row_head = lax.broadcasted_iota(jnp.int32, (GS, C), 0) // SLICES
    lane_head = lax.broadcasted_iota(jnp.int32, (GS, C), 1) % G // HEAD
    for i in range(2):
        own_part = jnp.where(row_head == lane_head, acc[i * GS : (i + 1) * GS], 0.0)
        folded = jnp.sum(own_part.reshape(HEADS // 2, SLICES, C), axis=0)
        pay[:, i * G : (i + 1) * G] = folded[:, :G]
        pay[:, C + i * G : C + (i + 1) * G] = folded[:, G:]
    row_head = lax.broadcasted_iota(jnp.int32, (HS, 128), 0) // SLICES
    lane = lax.broadcasted_iota(jnp.int32, (HS, 128), 1)
    placed = jnp.where(row_head == lane, den[...], 0.0)
    pay[:, 2 * C :] = jnp.sum(placed.reshape(HEADS, SLICES, 128), axis=0)


def attention_step(pay, watt, an, ant, dd, toks):
    numer = pay[:, :C]
    deslice = pay[:, C : 2 * C]
    head_of_lane = lax.broadcasted_iota(jnp.int32, (128, C), 1) // HEAD
    expand = (lax.broadcasted_iota(jnp.int32, (128, C), 0) == head_of_lane).astype(F32)
    inv_den = 1.0 / (dot_high(pay[:, 2 * C :], expand) + 1e-05)
    tokens = numer * inv_den
    mask = head_mask(HS)
    q = dot_high(tokens, watt[0])
    k = dot_high(tokens, watt[1])
    v = dot_high(tokens, watt[2])
    q_bd = spread_heads(q)
    root = 1.0 / math.sqrt(HEAD)
    scores = dot_high(q_bd, k, NT) * root
    top = jnp.max(scores, axis=-1, keepdims=True)
    e = jnp.exp(scores - top)
    att = e / jnp.sum(e, axis=-1, keepdims=True)
    attended = jnp.where(mask, dot_high(att, v), 0.0)
    do_bd = spread_heads(deslice)
    dv = dot_high(att, do_bd, TN)
    d_att = dot_high(do_bd, v, NT)
    ds = att * (d_att - jnp.sum(att * d_att, axis=-1, keepdims=True)) * root
    dq = fold_heads(dot_high(ds, k))
    dk = dot_high(ds, q_bd, TN)
    d_tokens = (
        dot_high(dq, watt[0], NT) + dot_high(dk, watt[1], NT) + dot_high(dv, watt[2], NT)
    )
    d_numer = d_tokens * inv_den
    d_den = -d_numer * tokens
    dd[...] = jnp.sum(spread_heads(d_den), axis=1, keepdims=True)
    d_numer_bd = spread_heads(d_numer)
    for i in range(2):
        rows = slice(i * GS, (i + 1) * GS)
        lanes = slice(i * G, (i + 1) * G)
        both = jnp.concatenate([attended[rows, lanes], d_numer_bd[rows, lanes]], axis=1)
        an[i] = both.astype(BF)
        ant[i] = both.T.astype(BF)
    toks[0] = tokens
    toks[1] = dq
    toks[2] = dk
    toks[3] = dv


def attend_gradients(toks, gatt):
    row_head = lax.broadcasted_iota(jnp.int32, (C, C), 0) // HEAD
    col_head = lax.broadcasted_iota(jnp.int32, (C, C), 1) // HEAD
    same = row_head == col_head
    lane_in = lax.broadcasted_iota(jnp.int32, (C, HEAD), 0) % HEAD
    fold = (lane_in == lax.broadcasted_iota(jnp.int32, (C, HEAD), 1)).astype(F32)
    for i in range(3):
        full = jnp.where(same, dot_high(toks[0], toks[i + 1], TN), 0.0)
        packed = dot_high(full, fold)
        gatt[i] = jnp.sum(packed.reshape(HEADS, HEAD, HEAD), axis=0)


def back_kernel(
    core, mine, other, watt, normed, feat, mid, prob_in, aux, dmix, cot, gain, wfmt, bdt, wcol,
    res, send, keep, toks, an, ant, dd, gfm, gout, gsl, pay, gpay,
):
    t = pl.program_id(0)

    @pl.when(t == 0)
    def _():
        join_halves(core[0], mine, other, pay)
        attention_step(pay, watt, an, ant, dd, toks)
        gfm[...] = jnp.zeros_like(gfm)
        gout[...] = jnp.zeros_like(gout)
        gsl[...] = jnp.zeros_like(gsl)

    mid_t = mid[...]
    weights = prob_in[...].astype(BF)
    prob = prob_in[...].reshape(HEADS, SLICES, BLOCK)
    inv = aux[:HEADS]
    groups = []
    for i in range(2):
        lanes = slice(i * G, (i + 1) * G)
        groups.append(dot(an[i], jnp.concatenate([dmix[:, lanes], feat[:, lanes]], axis=1), NT))
    dw = jnp.concatenate(groups, axis=0) + dd[...]
    dw = dw.reshape(HEADS, SLICES, BLOCK)
    dl = prob * (dw - jnp.sum(prob * dw, axis=1, keepdims=True))
    d_raw = (dl * inv[:, None, :]).reshape(HS, BLOCK).astype(BF)
    direct = dot(bdt[...], d_raw)
    inner = (mid_t.astype(F32) * direct).reshape(HEADS, HEAD, BLOCK)
    d_temper = -jnp.sum(inner, axis=1) * aux[HEADS:]
    low = dot(ant[0], weights[:GS]).astype(BF)
    high = dot(ant[1], weights[GS:]).astype(BF)
    mixed_df = jnp.concatenate([low[:G], high[:G], low[G:], high[G:]], axis=0)
    spread = jnp.broadcast_to(d_temper[:, None, :], (HEADS, HEAD, BLOCK)).reshape(C, BLOCK)
    dm = (direct + spread * wcol[...]).astype(BF)
    res[: 2 * C] = mixed_df
    res[2 * C :] = dm
    normed_here = normed[...]
    gfm[:C] += dot(mixed_df[C:], normed_here)
    gfm[C:] += dot(dm, normed_here)
    gout[...] += dot(mixed_df[:C], cot[...])
    dt_hi = d_temper.astype(BF)
    dt_lo = (d_temper - dt_hi.astype(F32)).astype(BF)
    gsl[:HS] += dot(d_raw, mid_t, NT)
    gsl[HS:] += dot(jnp.concatenate([dt_hi, dt_lo], axis=0), mid_t, NT)

    @pl.when(t == B_DEV - 1)
    def _():
        grad_fm = gfm[...]
        gpay[: 2 * C] = grad_fm
        gpay[2 * C : 3 * C] = gout[...]
        gpay[3 * C : 3 * C + SLICES] = fold_heads(gsl[:HS])
        grad_gain = jnp.sum(grad_fm * wfmt[...].astype(F32), axis=0, keepdims=True) / gain[...]
        both = gsl[HS : HS + 8] + gsl[HS + 8 :]
        row = lax.broadcasted_iota(jnp.int32, (8, C), 0)
        lane_head = lax.broadcasted_iota(jnp.int32, (8, C), 1) // HEAD
        temper_row = jnp.sum(jnp.where(row == lane_head, both, 0.0), axis=0, keepdims=True)
        row = lax.broadcasted_iota(jnp.int32, (SLICES, C), 0)
        tail = jnp.where(row == 0, grad_gain, jnp.where(row == 1, temper_row, 0.0))
        gpay[3 * C + SLICES :] = tail
        split_halves(core[0], gpay, send, keep)


def out_kernel(ptsb, cot, res, gain, wfmt, wout, layer, grad):
    points = ptsb[...]
    x_hat, inv_std = normalize(points)
    mixed_out = dot(res[:C], wout[...], TN)
    layer[...] = (points.astype(F32) + mixed_out).astype(BF)
    d_normed = dot(res[C:], wfmt[...], TN)
    scaled = d_normed * gain[...]
    mean_g = jnp.mean(scaled, axis=-1, keepdims=True)
    mean_gx = jnp.mean(scaled * x_hat, axis=-1, keepdims=True)
    grad[...] = (cot[...].astype(F32) + (scaled - mean_g - x_hat * mean_gx) * inv_std).astype(BF)


def unpack_kernel(core, mine, other, gfeat, gmid, gout, gslice, gtemper, ggain, full):
    join_halves(core[0], mine, other, full)
    gfeat[...] = full[:C].T
    gmid[...] = full[C : 2 * C].T
    gout[...] = full[2 * C : 3 * C]
    lane_in = lax.broadcasted_iota(jnp.int32, (C, HEAD), 0) % HEAD
    fold = (lane_in == lax.broadcasted_iota(jnp.int32, (C, HEAD), 1)).astype(F32)
    gslice[...] = dot_high(fold, full[3 * C : 3 * C + SLICES], (((0,), (1,)), ((), ())))
    tail = full[3 * C + SLICES : 3 * C + SLICES + 8]
    gtemper[...] = dot_high(tail, fold)[1:2]
    ggain[...] = tail[0:1]


def swap(array, even, odd):
    n = lax.axis_size("pts")
    return lax.ppermute(array, "pts", [(i, i ^ (odd if i % 2 else even)) for i in range(n)])


def quad_sum(x, even, odd, wire):
    w = x.astype(wire)
    a = swap(w, even, odd).astype(F32)
    b = swap(w, 2 * even, 2 * odd).astype(F32)
    c = swap(w, 3 * even, 3 * odd).astype(F32)
    return (w.astype(F32) + a) + (b + c)


def sum_over_chips(send, keep, wire, beside=()):
    x = keep + swap(send, 1, 1).astype(F32)
    done = []
    for i, (even, odd) in enumerate(((2, 8), (8, 32), (32, 2))):
        x = quad_sum(x, even, odd, wire)
        for at, arrays in beside:
            if at == i:
                x, arrays = lax.optimization_barrier((x, arrays))
                done.append(arrays)
    x = x.astype(wire)
    return x, swap(x, 1, 1), done


def neighbour_blocks(inner, outer):
    n = lax.axis_size("pts")
    edges = [(i, i + 1) for i in range(1, n - 1, 2)]
    got_outer = lax.ppermute(outer, "pts", edges + [(j, i) for i, j in edges])
    return swap(inner, 1, 1), got_outer


def whole(shape):
    return pl.BlockSpec(shape, lambda t, *_: (0,) * len(shape))


def rows_spec(width):
    return pl.BlockSpec((BLOCK, width), lambda t, *_: (t, 0))


PARAMS = pltpu.CompilerParams(vmem_limit_bytes=24 * 1024 * 1024)
SCALARS = pl.BlockSpec(memory_space=pltpu.SMEM)
HBM = pl.BlockSpec(memory_space=pl.ANY)


def per_device(
    loader_points, cotangent, block_counts, dest_table, norm_gain, w_feature, w_middle,
    w_slice, w_temper, attend_weight, w_output,
):
    rank = lax.axis_index("pts").astype(jnp.int32).reshape(1)
    core = lax.rem(rank, 2)
    edge = jax.ShapeDtypeStruct((HALF * BLOCK, C), BF)

    def tail_slot(t, rank, counts):
        return jnp.maximum(counts[rank[0]] - HALF, 0) + t

    def inner_slot(t, rank, counts):
        return (jnp.where(rank[0] % 2 == 0, tail_slot(t, rank, counts), t), 0)

    def outer_slot(t, rank, counts):
        return (jnp.where(rank[0] % 2 == 0, t, tail_slot(t, rank, counts)), 0)

    inner, outer = pl.pallas_call(
        pick_kernel,
        grid_spec=pltpu.PrefetchScalarGridSpec(
            num_scalar_prefetch=2,
            grid=(HALF,),
            in_specs=[pl.BlockSpec((BLOCK, C), inner_slot), pl.BlockSpec((BLOCK, C), outer_slot)],
            out_specs=[rows_spec(C)] * 2,
        ),
        out_shape=[edge, edge],
        name="pick",
    )(rank, block_counts, loader_points, loader_points)
    got_inner, got_outer = neighbour_blocks(inner, outer)
    gain = norm_gain.reshape(1, C)
    sel, d_mixed, wfmt, bd, bdt, wcol, watt = pl.pallas_call(
        prep_kernel,
        grid=(1,),
        in_specs=[SCALARS] * 3
        + [
            whole((ROWS, C)),
            whole((C, C)),
            whole((C, C)),
            whole((C, C)),
            whole((HEAD, SLICES)),
            whole((1, HEAD)),
            whole((3, HEAD, HEAD)),
        ],
        out_specs=[
            SCALARS,
            whole((ROWS, C)),
            whole((2 * C, C)),
            whole((HS + 32, C)),
            whole((C, HS)),
            whole((C, 1)),
            whole((3, C, C)),
        ],
        out_shape=[
            jax.ShapeDtypeStruct((3, B_DEV), jnp.int32),
            jax.ShapeDtypeStruct((ROWS, C), BF),
            jax.ShapeDtypeStruct((2 * C, C), BF),
            jax.ShapeDtypeStruct((HS + 32, C), BF),
            jax.ShapeDtypeStruct((C, HS), BF),
            jax.ShapeDtypeStruct((C, 1), F32),
            jax.ShapeDtypeStruct((3, C, C), F32),
        ],
        compiler_params=PARAMS,
        cost_estimate=pl.CostEstimate(
            flops=2 * ROWS * C * C, bytes_accessed=4 * 1024 * 1024, transcendentals=0
        ),
        name="prep",
    )(
        rank, block_counts, dest_table, cotangent, w_output, w_feature, w_middle, w_slice,
        w_temper.reshape(1, HEAD), attend_weight,
    )

    wide = jax.ShapeDtypeStruct((ROWS, C), BF)
    half1 = jax.ShapeDtypeStruct((SLICES // 2, PAY1), F32)
    cols_of = lambda rows: pl.BlockSpec((rows, BLOCK), lambda t, *_: (0, t))
    arrays = [wide] * 3 + [
        jax.ShapeDtypeStruct((C, ROWS), BF),
        jax.ShapeDtypeStruct((HS, ROWS), F32),
        jax.ShapeDtypeStruct((2 * HEADS, ROWS), F32),
    ]

    def front_specs(tile):
        rows = pl.BlockSpec((BLOCK, C), lambda t, s, c: (tile(t, c), 0))
        cols = lambda n: pl.BlockSpec((n, BLOCK), lambda t, s, c: (0, tile(t, c)))
        ins = [
            pl.BlockSpec((BLOCK, C), lambda t, s, c: (s[0, tile(t, c)], 0)),
            pl.BlockSpec((BLOCK, C), lambda t, s, c: (s[1, tile(t, c)], 0)),
            rows,
            whole((1, C)),
            whole((C, C)),
            pl.BlockSpec((C, C), lambda t, s, c: (1, 0)),
            whole((HS + 32, C)),
        ]
        return ins, [rows] * 3 + [cols(C), cols(HS), cols(2 * HEADS)]

    sums = [pltpu.VMEM((HS, C), F32), pltpu.VMEM((HS, 128), F32)]
    ins, outs = front_specs(first_tile)
    *first, pay = pl.pallas_call(
        front_first,
        grid_spec=pltpu.PrefetchScalarGridSpec(
            num_scalar_prefetch=2,
            grid=(HALF,),
            in_specs=ins,
            out_specs=outs + [whole((SLICES, PAY1))],
            scratch_shapes=sums,
        ),
        out_shape=arrays + [jax.ShapeDtypeStruct((SLICES, PAY1), F32)],
        compiler_params=PARAMS,
        cost_estimate=pl.CostEstimate(
            flops=2 * ROWS * C * 3 * C, bytes_accessed=6 * 1024 * 1024, transcendentals=0
        ),
        name="front_first",
    )(sel, core, loader_points, got_inner, d_mixed, gain, w_feature, wfmt, bd)
    ins, outs = front_specs(second_tile)
    *first, send, keep = pl.pallas_call(
        front_second,
        grid_spec=pltpu.PrefetchScalarGridSpec(
            num_scalar_prefetch=2,
            grid=(HALF,),
            in_specs=ins + [whole((SLICES, PAY1))] + [HBM] * 6,
            out_specs=outs + [whole((SLICES // 2, PAY1))] * 2,
            scratch_shapes=sums + [pltpu.VMEM((SLICES, PAY1), F32)],
        ),
        out_shape=arrays + [half1] * 2,
        input_output_aliases={10 + i: i for i in range(6)},
        compiler_params=PARAMS,
        name="front_second",
    )(sel, core, loader_points, got_outer, d_mixed, gain, w_feature, wfmt, bd, pay, *first)
    ptsb, normed, feat, mid, prob, aux = first

    mine, other, _ = sum_over_chips(send, keep, F32)

    res, send, keep, toks = pl.pallas_call(
        back_kernel,
        grid=(B_DEV,),
        in_specs=[SCALARS]
        + [whole((SLICES // 2, PAY1))] * 2
        + [whole((3, C, C))]
        + [rows_spec(C)] * 2
        + [cols_of(C), cols_of(HS), cols_of(2 * HEADS)]
        + [rows_spec(C)] * 2
        + [
            whole((1, C)),
            whole((2 * C, C)),
            whole((C, HS)),
            whole((C, 1)),
        ],
        out_specs=[
            pl.BlockSpec((3 * C, BLOCK), lambda t: (0, t)),
            whole((PAY2 // 2, C)),
            whole((PAY2 // 2, C)),
            whole((4, SLICES, C)),
        ],
        out_shape=[
            jax.ShapeDtypeStruct((3 * C, ROWS), BF),
            jax.ShapeDtypeStruct((PAY2 // 2, C), BF),
            jax.ShapeDtypeStruct((PAY2 // 2, C), F32),
            jax.ShapeDtypeStruct((4, SLICES, C), F32),
        ],
        scratch_shapes=[
            pltpu.VMEM((2, GS, C), BF),
            pltpu.VMEM((2, C, GS), BF),
            pltpu.VMEM((HS, 1), F32),
            pltpu.VMEM((2 * C, C), F32),
            pltpu.VMEM((C, C), F32),
            pltpu.VMEM((HS + 16, C), F32),
            pltpu.VMEM((SLICES, PAY1), F32),
            pltpu.VMEM((PAY2, C), F32),
        ],
        compiler_params=PARAMS,
        name="back",
    )(
        core, mine, other, watt, normed, feat, mid, prob, aux, d_mixed, cotangent, gain, wfmt,
        bdt, wcol,
    )

    layer_out, grad_points = pl.pallas_call(
        out_kernel,
        grid=(B_DEV,),
        in_specs=[
            rows_spec(C),
            rows_spec(C),
            pl.BlockSpec((3 * C, BLOCK), lambda t: (0, t)),
            whole((1, C)),
            whole((2 * C, C)),
            whole((C, C)),
        ],
        out_specs=[rows_spec(C)] * 2,
        out_shape=[wide] * 2,
        compiler_params=PARAMS,
        cost_estimate=pl.CostEstimate(
            flops=2 * ROWS * C * 3 * C, bytes_accessed=7 * ROWS * C * 2, transcendentals=0
        ),
        name="outputs",
    )(ptsb, cotangent, res, gain, wfmt, w_output)

    grad_attend = pl.pallas_call(
        attend_gradients,
        out_shape=jax.ShapeDtypeStruct((3, HEAD, HEAD), F32),
        compiler_params=PARAMS,
        name="attend_grads",
    )(toks)

    beside = ((0, (layer_out, grad_points)), (1, grad_attend))
    mine, other, done = sum_over_chips(send, keep, BF, beside)
    (layer_out, grad_points), grad_attend = done
    vmem = pl.BlockSpec(memory_space=pltpu.VMEM)
    grad_feature, grad_middle, grad_output, grad_slice, grad_temper, grad_gain = pl.pallas_call(
        unpack_kernel,
        in_specs=[SCALARS, vmem, vmem],
        out_specs=[vmem] * 6,
        out_shape=[
            jax.ShapeDtypeStruct((C, C), F32),
            jax.ShapeDtypeStruct((C, C), F32),
            jax.ShapeDtypeStruct((C, C), F32),
            jax.ShapeDtypeStruct((HEAD, SLICES), F32),
            jax.ShapeDtypeStruct((1, HEAD), F32),
            jax.ShapeDtypeStruct((1, C), F32),
        ],
        scratch_shapes=[pltpu.VMEM((PAY2, C), F32)],
        compiler_params=PARAMS,
        name="unpack",
    )(core, mine, other)
    return (
        layer_out,
        grad_points,
        grad_gain.reshape(C),
        grad_feature,
        grad_middle,
        grad_slice,
        grad_temper.reshape(HEAD),
        grad_attend,
        grad_output,
    )


def solution(mesh):
    return jax.shard_map(
        per_device,
        mesh=mesh,
        in_specs=(P("pts", None), P("pts", None), P(), P("pts"), P(), P(), P(), P(), P(), P(), P()),
        out_specs=(P("pts", None), P("pts", None), P(), P(), P(), P(), P(), P(), P()),
        check_vma=False,
    )
```

```python
import math

import jax
import jax.numpy as jnp
from jax import lax
from jax.experimental import pallas as pl
from jax.experimental.pallas import tpu as pltpu
from jax.sharding import PartitionSpec as P

BLOCK = 512
B_DEV = 4
HALF = 2
CAP = 8
C = 256
HEADS = 8
HEAD = 32
SLICES = 64
HS = HEADS * SLICES
ROWS = B_DEV * BLOCK
PAY1 = 640
PAY2 = 800
ORDER = (1, 2, 3)
FT = 512
SUB = BLOCK // FT
BF = jnp.bfloat16
F32 = jnp.float32
HIGH = lax.Precision.HIGH
G = C // 2
GS = HS // 2
NN = (((1,), (0,)), ((), ()))
NT = (((1,), (1,)), ((), ()))
TN = (((0,), (0,)), ((), ()))


def dot(a, b, dims=NN):
    return lax.dot_general(a, b, dims, preferred_element_type=F32)


def dot_high(a, b, dims=NN):
    return lax.dot_general(a, b, dims, precision=HIGH, preferred_element_type=F32)


def dot_full(a, b):
    return lax.dot_general(a, b, NN, precision=lax.Precision.HIGHEST, preferred_element_type=F32)


def head_mask(rows):
    row_head = lax.broadcasted_iota(jnp.int32, (rows, C), 0) // SLICES
    lane_head = lax.broadcasted_iota(jnp.int32, (rows, C), 1) // HEAD
    return row_head == lane_head


def fold_heads(full):
    masked = jnp.where(head_mask(HS), full, 0.0)
    return jnp.sum(masked.reshape(HEADS, SLICES, C), axis=0)


def spread_heads(small):
    tiled = jnp.concatenate([small] * HEADS, axis=0)
    return jnp.where(head_mask(HS), tiled, 0.0)


def normalize(points):
    point_f = points.astype(F32)
    center = point_f - jnp.mean(point_f, axis=-1, keepdims=True)
    inv_std = lax.rsqrt(jnp.mean(center * center, axis=-1, keepdims=True) + 1e-05)
    return center * inv_std, inv_std


def slice_softmax(mid_t, bd):
    out = dot(bd, mid_t)
    width = mid_t.shape[1]
    temper = out[HS : HS + 8] + out[HS + 8 : HS + 16] + out[HS + 16 : HS + 24]
    scale = 0.5 + jnp.maximum(temper, 0.0) + jnp.log1p(jnp.exp(-jnp.abs(temper)))
    inv = 1.0 / scale
    powers = out[:HS].reshape(HEADS, SLICES, width) * (inv * math.log2(math.e))[:, None, :]
    top = jnp.max(powers, axis=1, keepdims=True)
    e = jnp.exp2(powers - top)
    prob = e * (1.0 / jnp.sum(e, axis=1, keepdims=True))
    raw_top = top[:, 0] * (scale * math.log(2.0))
    return temper, inv, raw_top, prob


def split_halves(core, full, send, keep):
    half = full.shape[0] // 2

    @pl.when(core == 0)
    def _():
        keep[...] = full[:half].astype(keep.dtype)
        send[...] = full[half:].astype(send.dtype)

    @pl.when(core != 0)
    def _():
        keep[...] = full[half:].astype(keep.dtype)
        send[...] = full[:half].astype(send.dtype)


def join_halves(core, mine, other, full):
    half = full.shape[0] // 2

    @pl.when(core == 0)
    def _():
        full[:half] = mine[...].astype(full.dtype)
        full[half:] = other[...].astype(full.dtype)

    @pl.when(core != 0)
    def _():
        full[:half] = other[...].astype(full.dtype)
        full[half:] = mine[...].astype(full.dtype)


def pick_kernel(rank, counts, table, inner, outer, sel, inner_out, outer_out):
    inner_out[...] = inner[...]
    outer_out[...] = outer[...]

    @pl.when(pl.program_id(0) == 0)
    def _():
        place_blocks(rank, counts, table, sel)


def place_blocks(rank, counts, table, sel):
    here = rank[0]
    found, own = [], []
    for t in range(B_DEV):
        slot = jnp.int32(0)
        hit = jnp.int32(0)
        for s in range(CAP):
            same = table[s] == here * B_DEV + t
            slot = jnp.where(same, s, slot)
            hit = jnp.where(same, 1, hit)
        own.append(slot)
        found.append(hit)
    from_prev = 2 - found[0] - found[1]
    from_next = 2 - found[2] - found[3]
    left = counts[jnp.maximum(here - 1, 0)]
    start = jnp.maximum(left - HALF, 0)
    for t in range(B_DEV):
        sel[0, t] = own[t]
        place = left - from_prev + t - start if t < HALF else t - (B_DEV - from_next)
        sel[1, t] = jnp.clip(place, 0, HALF - 1)
        sel[2, t] = found[t]


def prep_kernel(cot, wout, wf, wm, ws, wt, dmix, wfmt, bd):
    dmix[...] = dot(cot[...], wout[...], NT).astype(BF)
    wfmt[:C] = wf[...].T
    wfmt[C:] = wm[...].T
    spread = spread_matrix()
    slice_rows = dot(ws[...], spread.astype(BF), TN)
    bd[:HS] = spread_heads(slice_rows).astype(BF)
    temper = dot_full(wt[...], spread)
    hi = temper.astype(BF).astype(F32)
    middle = (temper - hi).astype(BF).astype(F32)
    low = temper - hi - middle
    row = lax.broadcasted_iota(jnp.int32, (8, C), 0)
    own_head = row == lax.broadcasted_iota(jnp.int32, (8, C), 1) // HEAD
    parts = [jnp.where(own_head, part, 0.0) for part in (hi, middle, low)]
    bd[HS:] = jnp.concatenate(parts + [jnp.zeros((8, C), F32)], axis=0).astype(BF)


def spread_matrix():
    lane_in = lax.broadcasted_iota(jnp.int32, (HEAD, C), 1) % HEAD
    return (lax.broadcasted_iota(jnp.int32, (HEAD, C), 0) == lane_in).astype(F32)


def prep_back_kernel(bd, wt, attw, bdt, wcol, watt):
    spread = spread_matrix()
    bdt[:C] = bd[...].astype(F32).T.astype(BF)
    row = lax.broadcasted_iota(jnp.int32, (16, HS), 0)
    bdt[C:] = (row == lax.broadcasted_iota(jnp.int32, (16, HS), 1) // SLICES).astype(BF)
    temper = dot_full(wt[...], spread)
    rows = lax.broadcasted_iota(jnp.int32, (C, C), 0)
    cols = lax.broadcasted_iota(jnp.int32, (C, C), 1)
    wcol[...] = jnp.sum(jnp.where(rows == cols, temper, 0.0), axis=1, keepdims=True)
    same_head = rows // HEAD == cols // HEAD
    for i in range(3):
        wide = dot_full(attw[i], spread)
        watt[i] = jnp.where(same_head, jnp.concatenate([wide] * HEADS, axis=0), 0.0)


def first_tile(t, core):
    return t + HALF * SUB * (1 - core[0])


def second_tile(t, core):
    return t + HALF * SUB * core[0]


def front_first(sel, core, own, other, dmix, gain, wf, wmt, bd, *outs):
    *arrays, pay, acc, den = outs
    tile = first_tile(pl.program_id(0), core)
    front_tile(sel[2, tile // SUB], own, other, dmix, gain, wf, wmt, bd, *arrays, acc, den)

    @pl.when(pl.program_id(0) == HALF * SUB - 1)
    def _():
        fold_sums(acc, den, pay)


def front_second(sel, core, own, other, dmix, gain, wf, wmt, bd, pay_first, *rest):
    *arrays, send, keep, acc, den, pay = rest[6:]
    tile = second_tile(pl.program_id(0), core)
    front_tile(sel[2, tile // SUB], own, other, dmix, gain, wf, wmt, bd, *arrays, acc, den)

    @pl.when(pl.program_id(0) == HALF * SUB - 1)
    def _():
        fold_sums(acc, den, pay)
        pay[...] += pay_first[...]
        split_halves(core[0], pay, send, keep)


def front_tile(
    found, own, other, dmix, gain, wf, wmt, bd,
    ptsb, normed_out, feat_out, mid_out, prob_out, aux, acc, den,
):
    t = pl.program_id(0)

    @pl.when(found == 1)
    def _():
        ptsb[...] = own[...]

    @pl.when(found != 1)
    def _():
        ptsb[...] = other[...]

    x_hat, _ = normalize(ptsb[...])
    normed = (x_hat * gain[...]).astype(BF)
    normed_out[...] = normed
    feat = dot(normed, wf[...]).astype(BF)
    mid_t = dot(wmt[...], normed, NT).astype(BF)
    feat_out[...] = feat
    mid_out[...] = mid_t
    temper, inv, raw_top, prob = slice_softmax(mid_t, bd[...])
    prob_out[...] = prob.reshape(HS, FT)
    aux[:HEADS] = inv
    aux[HEADS : 2 * HEADS] = inv * jax.nn.sigmoid(temper)
    aux[2 * HEADS :] = raw_top
    weights = prob.reshape(HS, FT).astype(BF)

    @pl.when(t == 0)
    def _():
        acc[...] = jnp.zeros_like(acc)
        den[...] = jnp.zeros_like(den)

    grad = dmix[...]
    for i in range(2):
        both = jnp.concatenate([feat[:, i * G : (i + 1) * G], grad[:, i * G : (i + 1) * G]], axis=1)
        acc[i * GS : (i + 1) * GS] += dot(weights[i * GS : (i + 1) * GS], both)
    den[...] += dot(weights, jnp.ones((FT, 128), BF))


def fold_sums(acc, den, pay):
    row_head = lax.broadcasted_iota(jnp.int32, (GS, C), 0) // SLICES
    lane_head = lax.broadcasted_iota(jnp.int32, (GS, C), 1) % G // HEAD
    for i in range(2):
        own_part = jnp.where(row_head == lane_head, acc[i * GS : (i + 1) * GS], 0.0)
        folded = jnp.sum(own_part.reshape(HEADS // 2, SLICES, C), axis=0)
        pay[:, i * G : (i + 1) * G] = folded[:, :G]
        pay[:, C + i * G : C + (i + 1) * G] = folded[:, G:]
    row_head = lax.broadcasted_iota(jnp.int32, (HS, 128), 0) // SLICES
    lane = lax.broadcasted_iota(jnp.int32, (HS, 128), 1)
    placed = jnp.where(row_head == lane, den[...], 0.0)
    pay[:, 2 * C :] = jnp.sum(placed.reshape(HEADS, SLICES, 128), axis=0)


def packed_mask():
    row = lax.broadcasted_iota(jnp.int32, (SLICES, C), 0)
    return lax.broadcasted_iota(jnp.int32, (SLICES, C), 1) // HEAD == row % 8


def attention_step(pay, watt, an, ant, dd, toks):
    numer = pay[:, :C]
    deslice = pay[:, C : 2 * C]
    head_of_lane = lax.broadcasted_iota(jnp.int32, (128, C), 1) // HEAD
    expand = (lax.broadcasted_iota(jnp.int32, (128, C), 0) == head_of_lane).astype(F32)
    inv_den = 1.0 / (dot_high(pay[:, 2 * C :], expand) + 1e-05)
    tokens = numer * inv_den
    mask = head_mask(HS)
    q = dot_high(tokens, watt[0])
    k = dot_high(tokens, watt[1])
    v = dot_high(tokens, watt[2])
    q_bd = spread_heads(q)
    root = 1.0 / math.sqrt(HEAD)
    scores = dot_high(q_bd, k, NT) * root
    top = jnp.max(scores, axis=-1, keepdims=True)
    e = jnp.exp(scores - top)
    att = e / jnp.sum(e, axis=-1, keepdims=True)
    attended = jnp.where(mask, dot_high(att, v), 0.0)
    do_bd = spread_heads(deslice)
    dv = dot_high(att, do_bd, TN)
    d_att = dot_high(do_bd, v, NT)
    ds = att * (d_att - jnp.sum(att * d_att, axis=-1, keepdims=True)) * root
    dq = fold_heads(dot_high(ds, k))
    dk = dot_high(ds, q_bd, TN)
    d_tokens = (
        dot_high(dq, watt[0], NT) + dot_high(dk, watt[1], NT) + dot_high(dv, watt[2], NT)
    )
    d_numer = d_tokens * inv_den
    d_den = -d_numer * tokens
    dd[...] = jnp.sum(spread_heads(d_den), axis=1, keepdims=True)
    d_numer_bd = spread_heads(d_numer)
    for i in range(2):
        rows = slice(i * GS, (i + 1) * GS)
        lanes = slice(i * G, (i + 1) * G)
        both = jnp.concatenate([attended[rows, lanes], d_numer_bd[rows, lanes]], axis=1)
        an[i] = both.astype(BF)
        ant[i] = both.T.astype(BF)
    toks[0] = tokens
    toks[1] = dq
    toks[2] = dk
    toks[3] = dv


def attend_gradients(toks, gatt):
    row_head = lax.broadcasted_iota(jnp.int32, (C, C), 0) // HEAD
    col_head = lax.broadcasted_iota(jnp.int32, (C, C), 1) // HEAD
    same = row_head == col_head
    lane_in = lax.broadcasted_iota(jnp.int32, (C, HEAD), 0) % HEAD
    fold = (lane_in == lax.broadcasted_iota(jnp.int32, (C, HEAD), 1)).astype(F32)
    for i in range(3):
        full = jnp.where(same, dot_high(toks[0], toks[i + 1], TN), 0.0)
        packed = dot_high(full, fold)
        gatt[i] = jnp.sum(packed.reshape(HEADS, HEAD, HEAD), axis=0)


def back_kernel(
    core, mine, other, watt, normed, feat, mid, prob_in, aux, dmix, cot, gain, wfmt, bdt, wcol,
    res, send, keep, toks, an, ant, dd, gfm, gout, gsl, pay, gpay,
):
    t = pl.program_id(0)

    @pl.when(t == 0)
    def _():
        join_halves(core[0], mine, other, pay)
        attention_step(pay, watt, an, ant, dd, toks)
        gfm[...] = jnp.zeros_like(gfm)
        gout[...] = jnp.zeros_like(gout)
        gsl[...] = jnp.zeros_like(gsl)

    mid_t = mid[...]
    weights = prob_in[...].astype(BF)
    prob = prob_in[...].reshape(HEADS, SLICES, BLOCK)
    inv = aux[:HEADS]
    groups = []
    for i in range(2):
        lanes = slice(i * G, (i + 1) * G)
        groups.append(dot(an[i], jnp.concatenate([dmix[:, lanes], feat[:, lanes]], axis=1), NT))
    dw = jnp.concatenate(groups, axis=0) + dd[...]
    dw = dw.reshape(HEADS, SLICES, BLOCK)
    dl = prob * (dw - jnp.sum(prob * dw, axis=1, keepdims=True))
    d_raw = (dl * inv[:, None, :]).reshape(HS, BLOCK).astype(BF)
    direct = dot(bdt[...], d_raw)
    inner = (mid_t.astype(F32) * direct[:C]).reshape(HEADS, HEAD, BLOCK)
    against_top = jnp.sum(inner, axis=1) - aux[2 * HEADS :] * direct[C : C + HEADS]
    d_temper = -against_top * aux[HEADS : 2 * HEADS]
    low = dot(ant[0], weights[:GS]).astype(BF)
    high = dot(ant[1], weights[GS:]).astype(BF)
    mixed_df = jnp.concatenate([low[:G], high[:G], low[G:], high[G:]], axis=0)
    spread = jnp.broadcast_to(d_temper[:, None, :], (HEADS, HEAD, BLOCK)).reshape(C, BLOCK)
    dm = (direct[:C] + spread * wcol[...]).astype(BF)
    res[: 2 * C] = mixed_df
    res[2 * C :] = dm
    normed_here = normed[...]
    gfm[:C] += dot(mixed_df[C:], normed_here)
    gfm[C:] += dot(dm, normed_here)
    gout[...] += dot(mixed_df[:C], cot[...])
    dt_hi = d_temper.astype(BF)
    dt_lo = (d_temper - dt_hi.astype(F32)).astype(BF)
    gsl[:HS] += dot(d_raw, mid_t, NT)
    gsl[HS:] += dot(jnp.concatenate([dt_hi, dt_lo], axis=0), mid_t, NT)

    @pl.when(t == B_DEV - 1)
    def _():
        grad_fm = gfm[...]
        gpay[: 2 * C] = grad_fm
        gpay[2 * C : 3 * C] = gout[...]
        rows = lax.broadcasted_iota(jnp.int32, (C, C), 0)
        cols = lax.broadcasted_iota(jnp.int32, (C, C), 1)
        over_heads = (rows % HEAD == cols % HEAD).astype(F32)
        packed = jnp.where(packed_mask(), dot_high(fold_heads(gsl[:HS]), over_heads), 0.0)
        gpay[3 * C : 3 * C + 8] = jnp.sum(packed.reshape(8, 8, C), axis=1)
        grad_gain = jnp.sum(grad_fm * wfmt[...].astype(F32), axis=0, keepdims=True) / gain[...]
        both = gsl[HS : HS + 8] + gsl[HS + 8 :]
        row = lax.broadcasted_iota(jnp.int32, (8, C), 0)
        lane_head = lax.broadcasted_iota(jnp.int32, (8, C), 1) // HEAD
        temper_row = jnp.sum(jnp.where(row == lane_head, both, 0.0), axis=0, keepdims=True)
        row = lax.broadcasted_iota(jnp.int32, (PAY2 - 3 * C - 8, C), 0)
        tail = jnp.where(row == 0, grad_gain, jnp.where(row == 1, temper_row, 0.0))
        gpay[3 * C + 8 :] = tail
        split_halves(core[0], gpay, send, keep)


def out_kernel(ptsb, cot, res, gain, wfmt, wout, layer, grad):
    points = ptsb[...]
    x_hat, inv_std = normalize(points)
    mixed_out = dot(res[:C], wout[...], TN)
    layer[...] = (points.astype(F32) + mixed_out).astype(BF)
    d_normed = dot(res[C:], wfmt[...], TN)
    scaled = d_normed * gain[...]
    mean_g = jnp.mean(scaled, axis=-1, keepdims=True)
    mean_gx = jnp.mean(scaled * x_hat, axis=-1, keepdims=True)
    grad[...] = (cot[...].astype(F32) + (scaled - mean_g - x_hat * mean_gx) * inv_std).astype(BF)


def unpack_kernel(core, mine, other, gfeat, gmid, gout, gslice, gtemper, ggain, full):
    join_halves(core[0], mine, other, full)
    gfeat[...] = full[:C].T
    gmid[...] = full[C : 2 * C].T
    gout[...] = full[2 * C : 3 * C]
    lane_in = lax.broadcasted_iota(jnp.int32, (C, HEAD), 0) % HEAD
    fold = (lane_in == lax.broadcasted_iota(jnp.int32, (C, HEAD), 1)).astype(F32)
    rows = jnp.broadcast_to(full[3 * C : 3 * C + 8].reshape(8, 1, C), (8, 8, C))
    spread = jnp.where(packed_mask(), rows.reshape(SLICES, C), 0.0)
    gslice[...] = dot_high(fold, spread, (((0,), (1,)), ((), ())))
    tail = full[3 * C + 8 : 3 * C + 16]
    gtemper[...] = dot_high(tail, fold)[1:2]
    ggain[...] = tail[0:1]


def swap(array, even, odd):
    n = lax.axis_size("pts")
    return lax.ppermute(array, "pts", [(i, i ^ (odd if i % 2 else even)) for i in range(n)])


def quad_sum(x, even, odd, wire):
    w = x.astype(wire)
    got = {k: swap(w, k * even, k * odd).astype(F32) for k in ORDER}
    return (w.astype(F32) + got[1]) + (got[2] + got[3])


def sum_over_chips(send, keep, wire, beside=()):
    x = keep + swap(send, 1, 1).astype(F32)
    done = []
    for i, (even, odd) in enumerate(((2, 8), (8, 32), (32, 2))):
        x = quad_sum(x, even, odd, wire)
        for at, arrays in beside:
            if at == i:
                x, arrays = lax.optimization_barrier((x, arrays))
                done.append(arrays)
    x = x.astype(wire)
    return x, swap(x, 1, 1), done


def neighbour_blocks(inner, outer):
    n = lax.axis_size("pts")
    edges = [(i, i + 1) for i in range(1, n - 1, 2)]
    got_outer = lax.ppermute(outer, "pts", edges + [(j, i) for i, j in edges])
    return swap(inner, 1, 1), got_outer


def whole(shape):
    return pl.BlockSpec(shape, lambda t, *_: (0,) * len(shape))


def rows_spec(width):
    return pl.BlockSpec((BLOCK, width), lambda t, *_: (t, 0))


PARAMS = pltpu.CompilerParams(vmem_limit_bytes=24 * 1024 * 1024)
SCALARS = pl.BlockSpec(memory_space=pltpu.SMEM)
HBM = pl.BlockSpec(memory_space=pl.ANY)


def per_device(
    loader_points, cotangent, block_counts, dest_table, norm_gain, w_feature, w_middle,
    w_slice, w_temper, attend_weight, w_output,
):
    rank = lax.axis_index("pts").astype(jnp.int32).reshape(1)
    core = lax.rem(rank, 2)
    edge = jax.ShapeDtypeStruct((HALF * BLOCK, C), BF)

    def tail_slot(t, rank, counts):
        return jnp.maximum(counts[rank[0]] - HALF, 0) + t

    def inner_slot(t, rank, counts, table):
        return (jnp.where(rank[0] % 2 == 0, tail_slot(t, rank, counts), t), 0)

    def outer_slot(t, rank, counts, table):
        return (jnp.where(rank[0] % 2 == 0, t, tail_slot(t, rank, counts)), 0)

    sel, inner, outer = pl.pallas_call(
        pick_kernel,
        grid_spec=pltpu.PrefetchScalarGridSpec(
            num_scalar_prefetch=3,
            grid=(HALF,),
            in_specs=[pl.BlockSpec((BLOCK, C), inner_slot), pl.BlockSpec((BLOCK, C), outer_slot)],
            out_specs=[SCALARS] + [rows_spec(C)] * 2,
        ),
        out_shape=[jax.ShapeDtypeStruct((3, B_DEV), jnp.int32), edge, edge],
        name="pick",
    )(rank, block_counts, dest_table, loader_points, loader_points)
    got_inner, got_outer = neighbour_blocks(inner, outer)
    gain = norm_gain.reshape(1, C)
    d_mixed, wfmt, bd = pl.pallas_call(
        prep_kernel,
        grid=(1,),
        in_specs=[whole((ROWS, C))] + [whole((C, C))] * 3 + [whole((HEAD, SLICES)), whole((1, HEAD))],
        out_specs=[whole((ROWS, C)), whole((2 * C, C)), whole((HS + 32, C))],
        out_shape=[
            jax.ShapeDtypeStruct((ROWS, C), BF),
            jax.ShapeDtypeStruct((2 * C, C), BF),
            jax.ShapeDtypeStruct((HS + 32, C), BF),
        ],
        compiler_params=PARAMS,
        cost_estimate=pl.CostEstimate(
            flops=2 * ROWS * C * C, bytes_accessed=4 * 1024 * 1024, transcendentals=0
        ),
        name="prep",
    )(cotangent, w_output, w_feature, w_middle, w_slice, w_temper.reshape(1, HEAD))

    back_weights = pl.pallas_call(
        prep_back_kernel,
        grid=(1,),
        in_specs=[whole((HS, C)), whole((1, HEAD)), whole((3, HEAD, HEAD))],
        out_specs=[whole((C + 16, HS)), whole((C, 1)), whole((3, C, C))],
        out_shape=[
            jax.ShapeDtypeStruct((C + 16, HS), BF),
            jax.ShapeDtypeStruct((C, 1), F32),
            jax.ShapeDtypeStruct((3, C, C), F32),
        ],
        compiler_params=PARAMS,
        cost_estimate=pl.CostEstimate(
            flops=C * C * C, bytes_accessed=2 * 1024 * 1024, transcendentals=0
        ),
        name="prep_back",
    )(bd, w_temper.reshape(1, HEAD), attend_weight)

    wide = jax.ShapeDtypeStruct((ROWS, C), BF)
    half1 = jax.ShapeDtypeStruct((SLICES // 2, PAY1), F32)
    cols_of = lambda rows: pl.BlockSpec((rows, BLOCK), lambda t, *_: (0, t))
    arrays = [wide] * 3 + [
        jax.ShapeDtypeStruct((C, ROWS), BF),
        jax.ShapeDtypeStruct((HS, ROWS), F32),
        jax.ShapeDtypeStruct((3 * HEADS, ROWS), F32),
    ]

    def front_specs(tile):
        rows = pl.BlockSpec((FT, C), lambda t, s, c: (tile(t, c), 0))
        cols = lambda n: pl.BlockSpec((n, FT), lambda t, s, c: (0, tile(t, c)))
        ins = [
            pl.BlockSpec((FT, C), lambda t, s, c: (s[0, tile(t, c) // SUB] * SUB + t % SUB, 0)),
            pl.BlockSpec((FT, C), lambda t, s, c: (s[1, tile(t, c) // SUB] * SUB + t % SUB, 0)),
            rows,
            whole((1, C)),
            whole((C, C)),
            pl.BlockSpec((C, C), lambda t, s, c: (1, 0)),
            whole((HS + 32, C)),
        ]
        return ins, [rows] * 3 + [cols(C), cols(HS), cols(3 * HEADS)]

    sums = [pltpu.VMEM((HS, C), F32), pltpu.VMEM((HS, 128), F32)]
    ins, outs = front_specs(first_tile)
    *first, pay = pl.pallas_call(
        front_first,
        grid_spec=pltpu.PrefetchScalarGridSpec(
            num_scalar_prefetch=2,
            grid=(HALF * SUB,),
            in_specs=ins,
            out_specs=outs + [whole((SLICES, PAY1))],
            scratch_shapes=sums,
        ),
        out_shape=arrays + [jax.ShapeDtypeStruct((SLICES, PAY1), F32)],
        compiler_params=PARAMS,
        cost_estimate=pl.CostEstimate(
            flops=2 * ROWS * C * 3 * C, bytes_accessed=6 * 1024 * 1024, transcendentals=0
        ),
        name="front_first",
    )(sel, core, loader_points, got_inner, d_mixed, gain, w_feature, wfmt, bd)
    pay, (bdt, wcol, watt) = lax.optimization_barrier((pay, back_weights))
    ins, outs = front_specs(second_tile)
    *first, send, keep = pl.pallas_call(
        front_second,
        grid_spec=pltpu.PrefetchScalarGridSpec(
            num_scalar_prefetch=2,
            grid=(HALF * SUB,),
            in_specs=ins + [whole((SLICES, PAY1))] + [HBM] * 6,
            out_specs=outs + [whole((SLICES // 2, PAY1))] * 2,
            scratch_shapes=sums + [pltpu.VMEM((SLICES, PAY1), F32)],
        ),
        out_shape=arrays + [half1] * 2,
        input_output_aliases={10 + i: i for i in range(6)},
        compiler_params=PARAMS,
        name="front_second",
    )(sel, core, loader_points, got_outer, d_mixed, gain, w_feature, wfmt, bd, pay, *first)
    ptsb, normed, feat, mid, prob, aux = first

    mine, other, _ = sum_over_chips(send, keep, F32)

    res, send, keep, toks = pl.pallas_call(
        back_kernel,
        grid=(B_DEV,),
        in_specs=[SCALARS]
        + [whole((SLICES // 2, PAY1))] * 2
        + [whole((3, C, C))]
        + [rows_spec(C)] * 2
        + [cols_of(C), cols_of(HS), cols_of(3 * HEADS)]
        + [rows_spec(C)] * 2
        + [
            whole((1, C)),
            whole((2 * C, C)),
            whole((C + 16, HS)),
            whole((C, 1)),
        ],
        out_specs=[
            pl.BlockSpec((3 * C, BLOCK), lambda t: (0, t)),
            whole((PAY2 // 2, C)),
            whole((PAY2 // 2, C)),
            whole((4, SLICES, C)),
        ],
        out_shape=[
            jax.ShapeDtypeStruct((3 * C, ROWS), BF),
            jax.ShapeDtypeStruct((PAY2 // 2, C), BF),
            jax.ShapeDtypeStruct((PAY2 // 2, C), F32),
            jax.ShapeDtypeStruct((4, SLICES, C), F32),
        ],
        scratch_shapes=[
            pltpu.VMEM((2, GS, C), BF),
            pltpu.VMEM((2, C, GS), BF),
            pltpu.VMEM((HS, 1), F32),
            pltpu.VMEM((2 * C, C), F32),
            pltpu.VMEM((C, C), F32),
            pltpu.VMEM((HS + 16, C), F32),
            pltpu.VMEM((SLICES, PAY1), F32),
            pltpu.VMEM((PAY2, C), F32),
        ],
        compiler_params=PARAMS,
        name="back",
    )(
        core, mine, other, watt, normed, feat, mid, prob, aux, d_mixed, cotangent, gain, wfmt,
        bdt, wcol,
    )

    layer_out, grad_points = pl.pallas_call(
        out_kernel,
        grid=(B_DEV,),
        in_specs=[
            rows_spec(C),
            rows_spec(C),
            pl.BlockSpec((3 * C, BLOCK), lambda t: (0, t)),
            whole((1, C)),
            whole((2 * C, C)),
            whole((C, C)),
        ],
        out_specs=[rows_spec(C)] * 2,
        out_shape=[wide] * 2,
        compiler_params=PARAMS,
        cost_estimate=pl.CostEstimate(
            flops=2 * ROWS * C * 3 * C, bytes_accessed=7 * ROWS * C * 2, transcendentals=0
        ),
        name="outputs",
    )(ptsb, cotangent, res, gain, wfmt, w_output)

    grad_attend = pl.pallas_call(
        attend_gradients,
        out_shape=jax.ShapeDtypeStruct((3, HEAD, HEAD), F32),
        compiler_params=PARAMS,
        name="attend_grads",
    )(toks)

    beside = ((0, (layer_out, grad_points)), (1, grad_attend))
    mine, other, done = sum_over_chips(send, keep, BF, beside)
    (layer_out, grad_points), grad_attend = done
    vmem = pl.BlockSpec(memory_space=pltpu.VMEM)
    grad_feature, grad_middle, grad_output, grad_slice, grad_temper, grad_gain = pl.pallas_call(
        unpack_kernel,
        in_specs=[SCALARS, vmem, vmem],
        out_specs=[vmem] * 6,
        out_shape=[
            jax.ShapeDtypeStruct((C, C), F32),
            jax.ShapeDtypeStruct((C, C), F32),
            jax.ShapeDtypeStruct((C, C), F32),
            jax.ShapeDtypeStruct((HEAD, SLICES), F32),
            jax.ShapeDtypeStruct((1, HEAD), F32),
            jax.ShapeDtypeStruct((1, C), F32),
        ],
        scratch_shapes=[pltpu.VMEM((PAY2, C), F32)],
        compiler_params=PARAMS,
        name="unpack",
    )(core, mine, other)
    return (
        layer_out,
        grad_points,
        grad_gain.reshape(C),
        grad_feature,
        grad_middle,
        grad_slice,
        grad_temper.reshape(HEAD),
        grad_attend,
        grad_output,
    )


def solution(mesh):
    return jax.shard_map(
        per_device,
        mesh=mesh,
        in_specs=(P("pts", None), P("pts", None), P(), P("pts"), P(), P(), P(), P(), P(), P(), P()),
        out_specs=(P("pts", None), P("pts", None), P(), P(), P(), P(), P(), P(), P()),
        check_vma=False,
    )
```

```python
import math

import jax
import jax.numpy as jnp
from jax import lax
from jax.experimental import pallas as pl
from jax.experimental.pallas import tpu as pltpu
from jax.sharding import PartitionSpec as P

BLOCK = 512
B_DEV = 4
HALF = 2
CAP = 8
C = 256
HEADS = 8
HEAD = 32
SLICES = 64
HS = HEADS * SLICES
ROWS = B_DEV * BLOCK
PAY1 = 640
PAY2 = 800
ORDER = (1, 2, 3)
FT = HALF * BLOCK
BT = 1024
BF = jnp.bfloat16
F32 = jnp.float32
HIGH = lax.Precision.HIGH
G = C // 2
GS = HS // 2
NN = (((1,), (0,)), ((), ()))
NT = (((1,), (1,)), ((), ()))
TN = (((0,), (0,)), ((), ()))


def dot(a, b, dims=NN):
    return lax.dot_general(a, b, dims, preferred_element_type=F32)


def dot_high(a, b, dims=NN):
    return lax.dot_general(a, b, dims, precision=HIGH, preferred_element_type=F32)


def dot_full(a, b):
    return lax.dot_general(a, b, NN, precision=lax.Precision.HIGHEST, preferred_element_type=F32)


def head_mask(rows):
    row_head = lax.broadcasted_iota(jnp.int32, (rows, C), 0) // SLICES
    lane_head = lax.broadcasted_iota(jnp.int32, (rows, C), 1) // HEAD
    return row_head == lane_head


def fold_heads(full):
    masked = jnp.where(head_mask(HS), full, 0.0)
    return jnp.sum(masked.reshape(HEADS, SLICES, C), axis=0)


def spread_heads(small):
    tiled = jnp.concatenate([small] * HEADS, axis=0)
    return jnp.where(head_mask(HS), tiled, 0.0)


def normalize(points):
    point_f = points.astype(F32)
    center = point_f - jnp.mean(point_f, axis=-1, keepdims=True)
    inv_std = lax.rsqrt(jnp.mean(center * center, axis=-1, keepdims=True) + 1e-05)
    return center * inv_std, inv_std


def slice_softmax(mid_t, bd):
    out = dot(bd, mid_t)
    width = mid_t.shape[1]
    temper = out[HS : HS + 8] + out[HS + 8 : HS + 16] + out[HS + 16 : HS + 24]
    scale = 0.5 + jnp.maximum(temper, 0.0) + jnp.log1p(jnp.exp(-jnp.abs(temper)))
    inv = 1.0 / scale
    powers = out[:HS].reshape(HEADS, SLICES, width) * (inv * math.log2(math.e))[:, None, :]
    top = jnp.max(powers, axis=1, keepdims=True)
    e = jnp.exp2(powers - top)
    prob = e * (1.0 / jnp.sum(e, axis=1, keepdims=True))
    raw_top = top[:, 0] * (scale * math.log(2.0))
    return temper, inv, raw_top, prob


def split_halves(core, full, send, keep):
    half = full.shape[0] // 2

    @pl.when(core == 0)
    def _():
        keep[...] = full[:half].astype(keep.dtype)
        send[...] = full[half:].astype(send.dtype)

    @pl.when(core != 0)
    def _():
        keep[...] = full[half:].astype(keep.dtype)
        send[...] = full[:half].astype(send.dtype)


def join_halves(core, mine, other, full):
    half = full.shape[0] // 2

    @pl.when(core == 0)
    def _():
        full[:half] = mine[...].astype(full.dtype)
        full[half:] = other[...].astype(full.dtype)

    @pl.when(core != 0)
    def _():
        full[:half] = other[...].astype(full.dtype)
        full[half:] = mine[...].astype(full.dtype)


def pick_kernel(rank, counts, table, inner, outer, sel, inner_out, outer_out):
    inner_out[...] = inner[...]
    outer_out[...] = outer[...]

    @pl.when(pl.program_id(0) == 0)
    def _():
        place_blocks(rank, counts, table, sel)


def place_blocks(rank, counts, table, sel):
    here = rank[0]
    found, own = [], []
    for t in range(B_DEV):
        slot = jnp.int32(0)
        hit = jnp.int32(0)
        for s in range(CAP):
            same = table[s] == here * B_DEV + t
            slot = jnp.where(same, s, slot)
            hit = jnp.where(same, 1, hit)
        own.append(slot)
        found.append(hit)
    from_prev = 2 - found[0] - found[1]
    from_next = 2 - found[2] - found[3]
    left = counts[jnp.maximum(here - 1, 0)]
    start = jnp.maximum(left - HALF, 0)
    for t in range(B_DEV):
        sel[0, t] = own[t]
        place = left - from_prev + t - start if t < HALF else t - (B_DEV - from_next)
        sel[1, t] = jnp.clip(place, 0, HALF - 1)
        sel[2, t] = found[t]


def prep_kernel(cot, wout, wf, wm, ws, wt, dmix, wfmt, bd):
    dmix[...] = dot(cot[...], wout[...], NT).astype(BF)
    wfmt[:C] = wf[...].T
    wfmt[C:] = wm[...].T
    spread = spread_matrix()
    slice_rows = dot(ws[...], spread.astype(BF), TN)
    bd[:HS] = spread_heads(slice_rows).astype(BF)
    temper = dot_full(wt[...], spread)
    hi = temper.astype(BF).astype(F32)
    middle = (temper - hi).astype(BF).astype(F32)
    low = temper - hi - middle
    row = lax.broadcasted_iota(jnp.int32, (8, C), 0)
    own_head = row == lax.broadcasted_iota(jnp.int32, (8, C), 1) // HEAD
    parts = [jnp.where(own_head, part, 0.0) for part in (hi, middle, low)]
    bd[HS:] = jnp.concatenate(parts + [jnp.zeros((8, C), F32)], axis=0).astype(BF)


def spread_matrix():
    lane_in = lax.broadcasted_iota(jnp.int32, (HEAD, C), 1) % HEAD
    return (lax.broadcasted_iota(jnp.int32, (HEAD, C), 0) == lane_in).astype(F32)


def prep_back_kernel(bd, wt, attw, bdt, wcol, watt):
    spread = spread_matrix()
    bdt[:C] = bd[...].astype(F32).T.astype(BF)
    row = lax.broadcasted_iota(jnp.int32, (16, HS), 0)
    bdt[C:] = (row == lax.broadcasted_iota(jnp.int32, (16, HS), 1) // SLICES).astype(BF)
    temper = dot_full(wt[...], spread)
    rows = lax.broadcasted_iota(jnp.int32, (C, C), 0)
    cols = lax.broadcasted_iota(jnp.int32, (C, C), 1)
    wcol[...] = jnp.sum(jnp.where(rows == cols, temper, 0.0), axis=1, keepdims=True)
    same_head = rows // HEAD == cols // HEAD
    for i in range(3):
        wide = dot_full(attw[i], spread)
        watt[i] = jnp.where(same_head, jnp.concatenate([wide] * HEADS, axis=0), 0.0)


def first_half(core):
    return 1 - core[0]


def second_half(core):
    return core[0]


def front_first(sel, core, *refs):
    *arrays, pay, acc, den = refs
    front_rows(sel, first_half(core), *arrays, acc, den)
    fold_sums(acc, den, pay)


def front_second(sel, core, *refs):
    ins, pay_first, rest = refs[:9], refs[9], refs[16:]
    *arrays, send, keep, acc, den, pay = rest
    front_rows(sel, second_half(core), *ins, *arrays, acc, den)
    fold_sums(acc, den, pay)
    pay[...] += pay_first[...]
    split_halves(core[0], pay, send, keep)


def front_rows(
    sel, half, own_a, own_b, other_a, other_b, dmix, gain, wf, wmt, bd,
    ptsb, normed_out, feat_out, mid_out, prob_out, aux, acc, den,
):
    for i, (own, other) in enumerate(((own_a, other_a), (own_b, other_b))):
        found = sel[2, HALF * half + i]
        place = slice(i * BLOCK, (i + 1) * BLOCK)

        @pl.when(found == 1)
        def _(own=own, place=place):
            ptsb[place] = own[...]

        @pl.when(found != 1)
        def _(other=other, place=place):
            ptsb[place] = other[...]

    x_hat, _ = normalize(ptsb[...])
    normed = (x_hat * gain[...]).astype(BF)
    normed_out[...] = normed
    feat = dot(normed, wf[...]).astype(BF)
    mid_t = dot(wmt[...], normed, NT).astype(BF)
    feat_out[...] = feat
    mid_out[...] = mid_t
    temper, inv, raw_top, prob = slice_softmax(mid_t, bd[...])
    prob_out[...] = prob.reshape(HS, FT)
    aux[:HEADS] = inv
    aux[HEADS : 2 * HEADS] = inv * jax.nn.sigmoid(temper)
    aux[2 * HEADS :] = raw_top
    weights = prob.reshape(HS, FT).astype(BF)

    grad = dmix[...]
    for i in range(2):
        both = jnp.concatenate([feat[:, i * G : (i + 1) * G], grad[:, i * G : (i + 1) * G]], axis=1)
        acc[i * GS : (i + 1) * GS] = dot(weights[i * GS : (i + 1) * GS], both)
    den[...] = dot(weights, jnp.ones((FT, 128), BF))


def fold_sums(acc, den, pay):
    row_head = lax.broadcasted_iota(jnp.int32, (GS, C), 0) // SLICES
    lane_head = lax.broadcasted_iota(jnp.int32, (GS, C), 1) % G // HEAD
    for i in range(2):
        own_part = jnp.where(row_head == lane_head, acc[i * GS : (i + 1) * GS], 0.0)
        folded = jnp.sum(own_part.reshape(HEADS // 2, SLICES, C), axis=0)
        pay[:, i * G : (i + 1) * G] = folded[:, :G]
        pay[:, C + i * G : C + (i + 1) * G] = folded[:, G:]
    row_head = lax.broadcasted_iota(jnp.int32, (HS, 128), 0) // SLICES
    lane = lax.broadcasted_iota(jnp.int32, (HS, 128), 1)
    placed = jnp.where(row_head == lane, den[...], 0.0)
    pay[:, 2 * C :] = jnp.sum(placed.reshape(HEADS, SLICES, 128), axis=0)


def packed_mask():
    row = lax.broadcasted_iota(jnp.int32, (SLICES, C), 0)
    return lax.broadcasted_iota(jnp.int32, (SLICES, C), 1) // HEAD == row % 8


def attention_step(pay, watt, an, ant, dd, toks):
    numer = pay[:, :C]
    deslice = pay[:, C : 2 * C]
    head_of_lane = lax.broadcasted_iota(jnp.int32, (128, C), 1) // HEAD
    expand = (lax.broadcasted_iota(jnp.int32, (128, C), 0) == head_of_lane).astype(F32)
    inv_den = 1.0 / (dot_high(pay[:, 2 * C :], expand) + 1e-05)
    tokens = numer * inv_den
    mask = head_mask(HS)
    q = dot_high(tokens, watt[0])
    k = dot_high(tokens, watt[1])
    v = dot_high(tokens, watt[2])
    q_bd = spread_heads(q)
    root = 1.0 / math.sqrt(HEAD)
    scores = dot_high(q_bd, k, NT) * root
    top = jnp.max(scores, axis=-1, keepdims=True)
    e = jnp.exp(scores - top)
    att = e / jnp.sum(e, axis=-1, keepdims=True)
    attended = jnp.where(mask, dot_high(att, v), 0.0)
    do_bd = spread_heads(deslice)
    dv = dot_high(att, do_bd, TN)
    d_att = dot_high(do_bd, v, NT)
    ds = att * (d_att - jnp.sum(att * d_att, axis=-1, keepdims=True)) * root
    dq = fold_heads(dot_high(ds, k))
    dk = dot_high(ds, q_bd, TN)
    d_tokens = (
        dot_high(dq, watt[0], NT) + dot_high(dk, watt[1], NT) + dot_high(dv, watt[2], NT)
    )
    d_numer = d_tokens * inv_den
    d_den = -d_numer * tokens
    dd[...] = jnp.sum(spread_heads(d_den), axis=1, keepdims=True)
    d_numer_bd = spread_heads(d_numer)
    for i in range(2):
        rows = slice(i * GS, (i + 1) * GS)
        lanes = slice(i * G, (i + 1) * G)
        both = jnp.concatenate([attended[rows, lanes], d_numer_bd[rows, lanes]], axis=1)
        an[i] = both.astype(BF)
        ant[i] = both.T.astype(BF)
    toks[0] = tokens
    toks[1] = dq
    toks[2] = dk
    toks[3] = dv


def attend_gradients(toks, gatt):
    row_head = lax.broadcasted_iota(jnp.int32, (C, C), 0) // HEAD
    col_head = lax.broadcasted_iota(jnp.int32, (C, C), 1) // HEAD
    same = row_head == col_head
    lane_in = lax.broadcasted_iota(jnp.int32, (C, HEAD), 0) % HEAD
    fold = (lane_in == lax.broadcasted_iota(jnp.int32, (C, HEAD), 1)).astype(F32)
    for i in range(3):
        full = jnp.where(same, dot_high(toks[0], toks[i + 1], TN), 0.0)
        packed = dot_high(full, fold)
        gatt[i] = jnp.sum(packed.reshape(HEADS, HEAD, HEAD), axis=0)


def back_kernel(
    core, mine, other, watt, normed, feat, mid, prob_in, aux, dmix, cot, gain, wfmt, bdt, wcol,
    res, send, keep, toks, an, ant, dd, gfm, gout, gsl, pay, gpay,
):
    t = pl.program_id(0)

    @pl.when(t == 0)
    def _():
        join_halves(core[0], mine, other, pay)
        attention_step(pay, watt, an, ant, dd, toks)
        gfm[...] = jnp.zeros_like(gfm)
        gout[...] = jnp.zeros_like(gout)
        gsl[...] = jnp.zeros_like(gsl)

    mid_t = mid[...]
    weights = prob_in[...].astype(BF)
    prob = prob_in[...].reshape(HEADS, SLICES, BT)
    inv = aux[:HEADS]
    groups = []
    for i in range(2):
        lanes = slice(i * G, (i + 1) * G)
        groups.append(dot(an[i], jnp.concatenate([dmix[:, lanes], feat[:, lanes]], axis=1), NT))
    dw = jnp.concatenate(groups, axis=0) + dd[...]
    dw = dw.reshape(HEADS, SLICES, BT)
    dl = prob * (dw - jnp.sum(prob * dw, axis=1, keepdims=True))
    d_raw = (dl * inv[:, None, :]).reshape(HS, BT).astype(BF)
    direct = dot(bdt[...], d_raw)
    inner = (mid_t.astype(F32) * direct[:C]).reshape(HEADS, HEAD, BT)
    against_top = jnp.sum(inner, axis=1) - aux[2 * HEADS :] * direct[C : C + HEADS]
    d_temper = -against_top * aux[HEADS : 2 * HEADS]
    low = dot(ant[0], weights[:GS]).astype(BF)
    high = dot(ant[1], weights[GS:]).astype(BF)
    mixed_df = jnp.concatenate([low[:G], high[:G], low[G:], high[G:]], axis=0)
    spread = jnp.broadcast_to(d_temper[:, None, :], (HEADS, HEAD, BT)).reshape(C, BT)
    dm = (direct[:C] + spread * wcol[...]).astype(BF)
    res[: 2 * C] = mixed_df
    res[2 * C :] = dm
    normed_here = normed[...]
    gfm[:C] += dot(mixed_df[C:], normed_here)
    gfm[C:] += dot(dm, normed_here)
    gout[...] += dot(mixed_df[:C], cot[...])
    dt_hi = d_temper.astype(BF)
    dt_lo = (d_temper - dt_hi.astype(F32)).astype(BF)
    gsl[:HS] += dot(d_raw, mid_t, NT)
    gsl[HS:] += dot(jnp.concatenate([dt_hi, dt_lo], axis=0), mid_t, NT)

    @pl.when(t == ROWS // BT - 1)
    def _():
        grad_fm = gfm[...]
        gpay[: 2 * C] = grad_fm
        gpay[2 * C : 3 * C] = gout[...]
        rows = lax.broadcasted_iota(jnp.int32, (C, C), 0)
        cols = lax.broadcasted_iota(jnp.int32, (C, C), 1)
        over_heads = (rows % HEAD == cols % HEAD).astype(F32)
        packed = jnp.where(packed_mask(), dot_high(fold_heads(gsl[:HS]), over_heads), 0.0)
        gpay[3 * C : 3 * C + 8] = jnp.sum(packed.reshape(8, 8, C), axis=1)
        grad_gain = jnp.sum(grad_fm * wfmt[...].astype(F32), axis=0, keepdims=True) / gain[...]
        both = gsl[HS : HS + 8] + gsl[HS + 8 :]
        row = lax.broadcasted_iota(jnp.int32, (8, C), 0)
        lane_head = lax.broadcasted_iota(jnp.int32, (8, C), 1) // HEAD
        temper_row = jnp.sum(jnp.where(row == lane_head, both, 0.0), axis=0, keepdims=True)
        row = lax.broadcasted_iota(jnp.int32, (PAY2 - 3 * C - 8, C), 0)
        tail = jnp.where(row == 0, grad_gain, jnp.where(row == 1, temper_row, 0.0))
        gpay[3 * C + 8 :] = tail
        split_halves(core[0], gpay, send, keep)


def out_kernel(ptsb, cot, res, gain, wfmt, wout, layer, grad):
    points = ptsb[...]
    x_hat, inv_std = normalize(points)
    mixed_out = dot(res[:C], wout[...], TN)
    layer[...] = (points.astype(F32) + mixed_out).astype(BF)
    d_normed = dot(res[C:], wfmt[...], TN)
    scaled = d_normed * gain[...]
    mean_g = jnp.mean(scaled, axis=-1, keepdims=True)
    mean_gx = jnp.mean(scaled * x_hat, axis=-1, keepdims=True)
    grad[...] = (cot[...].astype(F32) + (scaled - mean_g - x_hat * mean_gx) * inv_std).astype(BF)


def unpack_kernel(core, mine, other, gfeat, gmid, gout, gslice, gtemper, ggain, full):
    join_halves(core[0], mine, other, full)
    gfeat[...] = full[:C].T
    gmid[...] = full[C : 2 * C].T
    gout[...] = full[2 * C : 3 * C]
    lane_in = lax.broadcasted_iota(jnp.int32, (C, HEAD), 0) % HEAD
    fold = (lane_in == lax.broadcasted_iota(jnp.int32, (C, HEAD), 1)).astype(F32)
    rows = jnp.broadcast_to(full[3 * C : 3 * C + 8].reshape(8, 1, C), (8, 8, C))
    spread = jnp.where(packed_mask(), rows.reshape(SLICES, C), 0.0)
    gslice[...] = dot_high(fold, spread, (((0,), (1,)), ((), ())))
    tail = full[3 * C + 8 : 3 * C + 16]
    gtemper[...] = dot_high(tail, fold)[1:2]
    ggain[...] = tail[0:1]


def swap(array, even, odd):
    n = lax.axis_size("pts")
    return lax.ppermute(array, "pts", [(i, i ^ (odd if i % 2 else even)) for i in range(n)])


def quad_sum(x, even, odd, wire):
    w = x.astype(wire)
    got = {k: swap(w, k * even, k * odd).astype(F32) for k in ORDER}
    return (w.astype(F32) + got[1]) + (got[2] + got[3])


def sum_over_chips(send, keep, wire, beside=()):
    x = keep + swap(send, 1, 1).astype(F32)
    done = []
    for i, (even, odd) in enumerate(((2, 8), (8, 32), (32, 2))):
        x = quad_sum(x, even, odd, wire)
        for at, arrays in beside:
            if at == i:
                x, arrays = lax.optimization_barrier((x, arrays))
                done.append(arrays)
    x = x.astype(wire)
    return x, swap(x, 1, 1), done


def neighbour_blocks(inner, outer):
    n = lax.axis_size("pts")
    edges = [(i, i + 1) for i in range(1, n - 1, 2)]
    got_outer = lax.ppermute(outer, "pts", edges + [(j, i) for i, j in edges])
    return swap(inner, 1, 1), got_outer


def whole(shape):
    return pl.BlockSpec(shape, lambda t, *_: (0,) * len(shape))


def rows_spec(width):
    return pl.BlockSpec((BLOCK, width), lambda t, *_: (t, 0))


PARAMS = pltpu.CompilerParams(vmem_limit_bytes=24 * 1024 * 1024)
BACK_PARAMS = pltpu.CompilerParams(vmem_limit_bytes=32 * 1024 * 1024)
SCALARS = pl.BlockSpec(memory_space=pltpu.SMEM)
HBM = pl.BlockSpec(memory_space=pl.ANY)


def per_device(
    loader_points, cotangent, block_counts, dest_table, norm_gain, w_feature, w_middle,
    w_slice, w_temper, attend_weight, w_output,
):
    rank = lax.axis_index("pts").astype(jnp.int32).reshape(1)
    core = lax.rem(rank, 2)
    edge = jax.ShapeDtypeStruct((HALF * BLOCK, C), BF)

    def tail_slot(t, rank, counts):
        return jnp.maximum(counts[rank[0]] - HALF, 0) + t

    def inner_slot(t, rank, counts, table):
        return (jnp.where(rank[0] % 2 == 0, tail_slot(t, rank, counts), t), 0)

    def outer_slot(t, rank, counts, table):
        return (jnp.where(rank[0] % 2 == 0, t, tail_slot(t, rank, counts)), 0)

    sel, inner, outer = pl.pallas_call(
        pick_kernel,
        grid_spec=pltpu.PrefetchScalarGridSpec(
            num_scalar_prefetch=3,
            grid=(HALF,),
            in_specs=[pl.BlockSpec((BLOCK, C), inner_slot), pl.BlockSpec((BLOCK, C), outer_slot)],
            out_specs=[SCALARS] + [rows_spec(C)] * 2,
        ),
        out_shape=[jax.ShapeDtypeStruct((3, B_DEV), jnp.int32), edge, edge],
        name="pick",
    )(rank, block_counts, dest_table, loader_points, loader_points)
    got_inner, got_outer = neighbour_blocks(inner, outer)
    gain = norm_gain.reshape(1, C)
    d_mixed, wfmt, bd = pl.pallas_call(
        prep_kernel,
        grid=(1,),
        in_specs=[whole((ROWS, C))] + [whole((C, C))] * 3 + [whole((HEAD, SLICES)), whole((1, HEAD))],
        out_specs=[whole((ROWS, C)), whole((2 * C, C)), whole((HS + 32, C))],
        out_shape=[
            jax.ShapeDtypeStruct((ROWS, C), BF),
            jax.ShapeDtypeStruct((2 * C, C), BF),
            jax.ShapeDtypeStruct((HS + 32, C), BF),
        ],
        compiler_params=PARAMS,
        cost_estimate=pl.CostEstimate(
            flops=2 * ROWS * C * C, bytes_accessed=4 * 1024 * 1024, transcendentals=0
        ),
        name="prep",
    )(cotangent, w_output, w_feature, w_middle, w_slice, w_temper.reshape(1, HEAD))

    back_weights = pl.pallas_call(
        prep_back_kernel,
        grid=(1,),
        in_specs=[whole((HS, C)), whole((1, HEAD)), whole((3, HEAD, HEAD))],
        out_specs=[whole((C + 16, HS)), whole((C, 1)), whole((3, C, C))],
        out_shape=[
            jax.ShapeDtypeStruct((C + 16, HS), BF),
            jax.ShapeDtypeStruct((C, 1), F32),
            jax.ShapeDtypeStruct((3, C, C), F32),
        ],
        compiler_params=PARAMS,
        cost_estimate=pl.CostEstimate(
            flops=C * C * C, bytes_accessed=2 * 1024 * 1024, transcendentals=0
        ),
        name="prep_back",
    )(bd, w_temper.reshape(1, HEAD), attend_weight)

    wide = jax.ShapeDtypeStruct((ROWS, C), BF)
    half1 = jax.ShapeDtypeStruct((SLICES // 2, PAY1), F32)
    arrays = [wide] * 3 + [
        jax.ShapeDtypeStruct((C, ROWS), BF),
        jax.ShapeDtypeStruct((HS, ROWS), F32),
        jax.ShapeDtypeStruct((3 * HEADS, ROWS), F32),
    ]

    def front_specs(half):
        rows = pl.BlockSpec((FT, C), lambda t, s, c: (half(c), 0))
        cols = lambda n: pl.BlockSpec((n, FT), lambda t, s, c: (0, half(c)))
        block = lambda row, i: pl.BlockSpec(
            (BLOCK, C), lambda t, s, c: (s[row, HALF * half(c) + i], 0)
        )
        ins = [
            block(0, 0),
            block(0, 1),
            block(1, 0),
            block(1, 1),
            rows,
            whole((1, C)),
            whole((C, C)),
            pl.BlockSpec((C, C), lambda t, s, c: (1, 0)),
            whole((HS + 32, C)),
        ]
        return ins, [rows] * 3 + [cols(C), cols(HS), cols(3 * HEADS)]

    sums = [pltpu.VMEM((HS, C), F32), pltpu.VMEM((HS, 128), F32)]
    ins, outs = front_specs(first_half)
    *first, pay = pl.pallas_call(
        front_first,
        grid_spec=pltpu.PrefetchScalarGridSpec(
            num_scalar_prefetch=2,
            grid=(1,),
            in_specs=ins,
            out_specs=outs + [whole((SLICES, PAY1))],
            scratch_shapes=sums,
        ),
        out_shape=arrays + [jax.ShapeDtypeStruct((SLICES, PAY1), F32)],
        compiler_params=PARAMS,
        cost_estimate=pl.CostEstimate(
            flops=2 * ROWS * C * 3 * C, bytes_accessed=6 * 1024 * 1024, transcendentals=0
        ),
        name="front_first",
    )(sel, core, loader_points, loader_points, got_inner, got_inner, d_mixed, gain, w_feature, wfmt, bd)
    pay, (bdt, wcol, watt) = lax.optimization_barrier((pay, back_weights))
    ins, outs = front_specs(second_half)
    *first, send, keep = pl.pallas_call(
        front_second,
        grid_spec=pltpu.PrefetchScalarGridSpec(
            num_scalar_prefetch=2,
            grid=(1,),
            in_specs=ins + [whole((SLICES, PAY1))] + [HBM] * 6,
            out_specs=outs + [whole((SLICES // 2, PAY1))] * 2,
            scratch_shapes=sums + [pltpu.VMEM((SLICES, PAY1), F32)],
        ),
        out_shape=arrays + [half1] * 2,
        input_output_aliases={12 + i: i for i in range(6)},
        compiler_params=PARAMS,
        name="front_second",
    )(
        sel, core, loader_points, loader_points, got_outer, got_outer, d_mixed, gain, w_feature,
        wfmt, bd, pay, *first,
    )
    ptsb, normed, feat, mid, prob, aux = first

    mine, other, _ = sum_over_chips(send, keep, F32)

    back_rows = pl.BlockSpec((BT, C), lambda t: (t, 0))
    back_cols = lambda rows: pl.BlockSpec((rows, BT), lambda t: (0, t))
    res, send, keep, toks = pl.pallas_call(
        back_kernel,
        grid=(ROWS // BT,),
        in_specs=[SCALARS]
        + [whole((SLICES // 2, PAY1))] * 2
        + [whole((3, C, C))]
        + [back_rows] * 2
        + [back_cols(C), back_cols(HS), back_cols(3 * HEADS)]
        + [back_rows] * 2
        + [
            whole((1, C)),
            whole((2 * C, C)),
            whole((C + 16, HS)),
            whole((C, 1)),
        ],
        out_specs=[
            back_cols(3 * C),
            whole((PAY2 // 2, C)),
            whole((PAY2 // 2, C)),
            whole((4, SLICES, C)),
        ],
        out_shape=[
            jax.ShapeDtypeStruct((3 * C, ROWS), BF),
            jax.ShapeDtypeStruct((PAY2 // 2, C), BF),
            jax.ShapeDtypeStruct((PAY2 // 2, C), F32),
            jax.ShapeDtypeStruct((4, SLICES, C), F32),
        ],
        scratch_shapes=[
            pltpu.VMEM((2, GS, C), BF),
            pltpu.VMEM((2, C, GS), BF),
            pltpu.VMEM((HS, 1), F32),
            pltpu.VMEM((2 * C, C), F32),
            pltpu.VMEM((C, C), F32),
            pltpu.VMEM((HS + 16, C), F32),
            pltpu.VMEM((SLICES, PAY1), F32),
            pltpu.VMEM((PAY2, C), F32),
        ],
        compiler_params=BACK_PARAMS,
        name="back",
    )(
        core, mine, other, watt, normed, feat, mid, prob, aux, d_mixed, cotangent, gain, wfmt,
        bdt, wcol,
    )

    layer_out, grad_points = pl.pallas_call(
        out_kernel,
        grid=(B_DEV,),
        in_specs=[
            rows_spec(C),
            rows_spec(C),
            pl.BlockSpec((3 * C, BLOCK), lambda t: (0, t)),
            whole((1, C)),
            whole((2 * C, C)),
            whole((C, C)),
        ],
        out_specs=[rows_spec(C)] * 2,
        out_shape=[wide] * 2,
        compiler_params=PARAMS,
        cost_estimate=pl.CostEstimate(
            flops=2 * ROWS * C * 3 * C, bytes_accessed=7 * ROWS * C * 2, transcendentals=0
        ),
        name="outputs",
    )(ptsb, cotangent, res, gain, wfmt, w_output)

    grad_attend = pl.pallas_call(
        attend_gradients,
        out_shape=jax.ShapeDtypeStruct((3, HEAD, HEAD), F32),
        compiler_params=PARAMS,
        name="attend_grads",
    )(toks)

    beside = ((0, (layer_out, grad_points)), (1, grad_attend))
    mine, other, done = sum_over_chips(send, keep, BF, beside)
    (layer_out, grad_points), grad_attend = done
    vmem = pl.BlockSpec(memory_space=pltpu.VMEM)
    grad_feature, grad_middle, grad_output, grad_slice, grad_temper, grad_gain = pl.pallas_call(
        unpack_kernel,
        in_specs=[SCALARS, vmem, vmem],
        out_specs=[vmem] * 6,
        out_shape=[
            jax.ShapeDtypeStruct((C, C), F32),
            jax.ShapeDtypeStruct((C, C), F32),
            jax.ShapeDtypeStruct((C, C), F32),
            jax.ShapeDtypeStruct((HEAD, SLICES), F32),
            jax.ShapeDtypeStruct((1, HEAD), F32),
            jax.ShapeDtypeStruct((1, C), F32),
        ],
        scratch_shapes=[pltpu.VMEM((PAY2, C), F32)],
        compiler_params=PARAMS,
        name="unpack",
    )(core, mine, other)
    return (
        layer_out,
        grad_points,
        grad_gain.reshape(C),
        grad_feature,
        grad_middle,
        grad_slice,
        grad_temper.reshape(HEAD),
        grad_attend,
        grad_output,
    )


def solution(mesh):
    return jax.shard_map(
        per_device,
        mesh=mesh,
        in_specs=(P("pts", None), P("pts", None), P(), P("pts"), P(), P(), P(), P(), P(), P(), P()),
        out_specs=(P("pts", None), P("pts", None), P(), P(), P(), P(), P(), P(), P()),
        check_vma=False,
    )
```

```python
import math

import jax
import jax.numpy as jnp
from jax import lax
from jax.experimental import pallas as pl
from jax.experimental.pallas import tpu as pltpu
from jax.sharding import PartitionSpec as P

BLOCK = 512
B_DEV = 4
HALF = 2
CAP = 8
C = 256
HEADS = 8
HEAD = 32
SLICES = 64
HS = HEADS * SLICES
ROWS = B_DEV * BLOCK
PAY1 = 640
PAY2 = 800
ORDER = (1, 2, 3)
FT = HALF * BLOCK
BT = ROWS
BF = jnp.bfloat16
F32 = jnp.float32
HIGH = lax.Precision.HIGH
G = C // 2
GS = HS // 2
NN = (((1,), (0,)), ((), ()))
NT = (((1,), (1,)), ((), ()))
TN = (((0,), (0,)), ((), ()))


def dot(a, b, dims=NN):
    return lax.dot_general(a, b, dims, preferred_element_type=F32)


def dot_high(a, b, dims=NN):
    return lax.dot_general(a, b, dims, precision=HIGH, preferred_element_type=F32)


def dot_full(a, b):
    return lax.dot_general(a, b, NN, precision=lax.Precision.HIGHEST, preferred_element_type=F32)


def head_mask(rows):
    row_head = lax.broadcasted_iota(jnp.int32, (rows, C), 0) // SLICES
    lane_head = lax.broadcasted_iota(jnp.int32, (rows, C), 1) // HEAD
    return row_head == lane_head


def fold_heads(full):
    masked = jnp.where(head_mask(HS), full, 0.0)
    return jnp.sum(masked.reshape(HEADS, SLICES, C), axis=0)


def spread_heads(small):
    tiled = jnp.concatenate([small] * HEADS, axis=0)
    return jnp.where(head_mask(HS), tiled, 0.0)


def normalize(points):
    point_f = points.astype(F32)
    center = point_f - jnp.mean(point_f, axis=-1, keepdims=True)
    inv_std = lax.rsqrt(jnp.mean(center * center, axis=-1, keepdims=True) + 1e-05)
    return center * inv_std, inv_std


def slice_softmax(mid_t, bd):
    out = dot(bd, mid_t)
    width = mid_t.shape[1]
    temper = out[HS : HS + 8] + out[HS + 8 : HS + 16] + out[HS + 16 : HS + 24]
    scale = 0.5 + jnp.maximum(temper, 0.0) + jnp.log1p(jnp.exp(-jnp.abs(temper)))
    inv = 1.0 / scale
    powers = out[:HS].reshape(HEADS, SLICES, width) * (inv * math.log2(math.e))[:, None, :]
    top = jnp.max(powers, axis=1, keepdims=True)
    e = jnp.exp2(powers - top)
    prob = e * (1.0 / jnp.sum(e, axis=1, keepdims=True))
    raw_top = top[:, 0] * (scale * math.log(2.0))
    return temper, inv, raw_top, prob


def split_halves(core, full, send, keep):
    half = full.shape[0] // 2

    @pl.when(core == 0)
    def _():
        keep[...] = full[:half].astype(keep.dtype)
        send[...] = full[half:].astype(send.dtype)

    @pl.when(core != 0)
    def _():
        keep[...] = full[half:].astype(keep.dtype)
        send[...] = full[:half].astype(send.dtype)


def join_halves(core, mine, other, full):
    half = full.shape[0] // 2

    @pl.when(core == 0)
    def _():
        full[:half] = mine[...].astype(full.dtype)
        full[half:] = other[...].astype(full.dtype)

    @pl.when(core != 0)
    def _():
        full[:half] = other[...].astype(full.dtype)
        full[half:] = mine[...].astype(full.dtype)


def pick_kernel(rank, counts, table, inner, outer, sel, inner_out, outer_out):
    inner_out[...] = inner[...]
    outer_out[...] = outer[...]

    @pl.when(pl.program_id(0) == 0)
    def _():
        place_blocks(rank, counts, table, sel)


def place_blocks(rank, counts, table, sel):
    here = rank[0]
    found, own = [], []
    for t in range(B_DEV):
        slot = jnp.int32(0)
        hit = jnp.int32(0)
        for s in range(CAP):
            same = table[s] == here * B_DEV + t
            slot = jnp.where(same, s, slot)
            hit = jnp.where(same, 1, hit)
        own.append(slot)
        found.append(hit)
    from_prev = 2 - found[0] - found[1]
    from_next = 2 - found[2] - found[3]
    left = counts[jnp.maximum(here - 1, 0)]
    start = jnp.maximum(left - HALF, 0)
    for t in range(B_DEV):
        sel[0, t] = own[t]
        place = left - from_prev + t - start if t < HALF else t - (B_DEV - from_next)
        sel[1, t] = jnp.clip(place, 0, HALF - 1)
        sel[2, t] = found[t]


def prep_kernel(cot, wout, wf, wm, ws, wt, dmix, wfmt, bd):
    dmix[...] = dot(cot[...], wout[...], NT).astype(BF)
    wfmt[:C] = wf[...].T
    wfmt[C:] = wm[...].T
    spread = spread_matrix()
    slice_rows = dot(ws[...], spread.astype(BF), TN)
    bd[:HS] = spread_heads(slice_rows).astype(BF)
    temper = dot_full(wt[...], spread)
    hi = temper.astype(BF).astype(F32)
    middle = (temper - hi).astype(BF).astype(F32)
    low = temper - hi - middle
    row = lax.broadcasted_iota(jnp.int32, (8, C), 0)
    own_head = row == lax.broadcasted_iota(jnp.int32, (8, C), 1) // HEAD
    parts = [jnp.where(own_head, part, 0.0) for part in (hi, middle, low)]
    bd[HS:] = jnp.concatenate(parts + [jnp.zeros((8, C), F32)], axis=0).astype(BF)


def spread_matrix():
    lane_in = lax.broadcasted_iota(jnp.int32, (HEAD, C), 1) % HEAD
    return (lax.broadcasted_iota(jnp.int32, (HEAD, C), 0) == lane_in).astype(F32)


def prep_back_kernel(bd, wt, attw, bdt, wcol, watt):
    spread = spread_matrix()
    bdt[:C] = bd[...].astype(F32).T.astype(BF)
    row = lax.broadcasted_iota(jnp.int32, (16, HS), 0)
    bdt[C:] = (row == lax.broadcasted_iota(jnp.int32, (16, HS), 1) // SLICES).astype(BF)
    temper = dot_full(wt[...], spread)
    rows = lax.broadcasted_iota(jnp.int32, (C, C), 0)
    cols = lax.broadcasted_iota(jnp.int32, (C, C), 1)
    wcol[...] = jnp.sum(jnp.where(rows == cols, temper, 0.0), axis=1, keepdims=True)
    same_head = rows // HEAD == cols // HEAD
    for i in range(3):
        wide = dot_full(attw[i], spread)
        watt[i] = jnp.where(same_head, jnp.concatenate([wide] * HEADS, axis=0), 0.0)


def first_half(core):
    return 1 - core[0]


def second_half(core):
    return core[0]


def front_first(sel, core, *refs):
    *arrays, pay, acc, den = refs
    front_rows(sel, first_half(core), *arrays, acc, den)
    fold_sums(acc, den, pay)


def front_second(sel, core, *refs):
    ins, pay_first, rest = refs[:9], refs[9], refs[16:]
    *arrays, send, keep, acc, den, pay = rest
    front_rows(sel, second_half(core), *ins, *arrays, acc, den)
    fold_sums(acc, den, pay)
    pay[...] += pay_first[...]
    split_halves(core[0], pay, send, keep)


def front_rows(
    sel, half, own_a, own_b, other_a, other_b, dmix, gain, wf, wmt, bd,
    ptsb, normed_out, feat_out, mid_out, prob_out, aux, acc, den,
):
    for i, (own, other) in enumerate(((own_a, other_a), (own_b, other_b))):
        found = sel[2, HALF * half + i]
        place = slice(i * BLOCK, (i + 1) * BLOCK)

        @pl.when(found == 1)
        def _(own=own, place=place):
            ptsb[place] = own[...]

        @pl.when(found != 1)
        def _(other=other, place=place):
            ptsb[place] = other[...]

    x_hat, _ = normalize(ptsb[...])
    normed = (x_hat * gain[...]).astype(BF)
    normed_out[...] = normed
    feat = dot(normed, wf[...]).astype(BF)
    mid_t = dot(wmt[...], normed, NT).astype(BF)
    feat_out[...] = feat
    mid_out[...] = mid_t
    temper, inv, raw_top, prob = slice_softmax(mid_t, bd[...])
    prob_out[...] = prob.reshape(HS, FT)
    aux[:HEADS] = inv
    aux[HEADS : 2 * HEADS] = inv * jax.nn.sigmoid(temper)
    aux[2 * HEADS :] = raw_top
    weights = prob.reshape(HS, FT).astype(BF)

    grad = dmix[...]
    for i in range(2):
        both = jnp.concatenate([feat[:, i * G : (i + 1) * G], grad[:, i * G : (i + 1) * G]], axis=1)
        acc[i * GS : (i + 1) * GS] = dot(weights[i * GS : (i + 1) * GS], both)
    den[...] = dot(weights, jnp.ones((FT, 128), BF))


def fold_sums(acc, den, pay):
    row_head = lax.broadcasted_iota(jnp.int32, (GS, C), 0) // SLICES
    lane_head = lax.broadcasted_iota(jnp.int32, (GS, C), 1) % G // HEAD
    for i in range(2):
        own_part = jnp.where(row_head == lane_head, acc[i * GS : (i + 1) * GS], 0.0)
        folded = jnp.sum(own_part.reshape(HEADS // 2, SLICES, C), axis=0)
        pay[:, i * G : (i + 1) * G] = folded[:, :G]
        pay[:, C + i * G : C + (i + 1) * G] = folded[:, G:]
    row_head = lax.broadcasted_iota(jnp.int32, (HS, 128), 0) // SLICES
    lane = lax.broadcasted_iota(jnp.int32, (HS, 128), 1)
    placed = jnp.where(row_head == lane, den[...], 0.0)
    pay[:, 2 * C :] = jnp.sum(placed.reshape(HEADS, SLICES, 128), axis=0)


def packed_mask():
    row = lax.broadcasted_iota(jnp.int32, (SLICES, C), 0)
    return lax.broadcasted_iota(jnp.int32, (SLICES, C), 1) // HEAD == row % 8


def attention_step(pay, watt, an, ant, dd, toks):
    numer = pay[:, :C]
    deslice = pay[:, C : 2 * C]
    head_of_lane = lax.broadcasted_iota(jnp.int32, (128, C), 1) // HEAD
    expand = (lax.broadcasted_iota(jnp.int32, (128, C), 0) == head_of_lane).astype(F32)
    inv_den = 1.0 / (dot_high(pay[:, 2 * C :], expand) + 1e-05)
    tokens = numer * inv_den
    mask = head_mask(HS)
    q = dot_high(tokens, watt[0])
    k = dot_high(tokens, watt[1])
    v = dot_high(tokens, watt[2])
    q_bd = spread_heads(q)
    root = 1.0 / math.sqrt(HEAD)
    scores = dot_high(q_bd, k, NT) * root
    top = jnp.max(scores, axis=-1, keepdims=True)
    e = jnp.exp(scores - top)
    att = e / jnp.sum(e, axis=-1, keepdims=True)
    attended = jnp.where(mask, dot_high(att, v), 0.0)
    do_bd = spread_heads(deslice)
    dv = dot_high(att, do_bd, TN)
    d_att = dot_high(do_bd, v, NT)
    ds = att * (d_att - jnp.sum(att * d_att, axis=-1, keepdims=True)) * root
    dq = fold_heads(dot_high(ds, k))
    dk = dot_high(ds, q_bd, TN)
    d_tokens = (
        dot_high(dq, watt[0], NT) + dot_high(dk, watt[1], NT) + dot_high(dv, watt[2], NT)
    )
    d_numer = d_tokens * inv_den
    d_den = -d_numer * tokens
    dd[...] = jnp.sum(spread_heads(d_den), axis=1, keepdims=True)
    d_numer_bd = spread_heads(d_numer)
    for i in range(2):
        rows = slice(i * GS, (i + 1) * GS)
        lanes = slice(i * G, (i + 1) * G)
        both = jnp.concatenate([attended[rows, lanes], d_numer_bd[rows, lanes]], axis=1)
        an[i] = both.astype(BF)
        ant[i] = both.T.astype(BF)
    toks[0] = tokens
    toks[1] = dq
    toks[2] = dk
    toks[3] = dv


def attend_gradients(toks, gatt):
    row_head = lax.broadcasted_iota(jnp.int32, (C, C), 0) // HEAD
    col_head = lax.broadcasted_iota(jnp.int32, (C, C), 1) // HEAD
    same = row_head == col_head
    lane_in = lax.broadcasted_iota(jnp.int32, (C, HEAD), 0) % HEAD
    fold = (lane_in == lax.broadcasted_iota(jnp.int32, (C, HEAD), 1)).astype(F32)
    for i in range(3):
        full = jnp.where(same, dot_high(toks[0], toks[i + 1], TN), 0.0)
        packed = dot_high(full, fold)
        gatt[i] = jnp.sum(packed.reshape(HEADS, HEAD, HEAD), axis=0)


def back_kernel(
    core, mine, other, watt, normed, feat, mid, prob_in, aux, dmix, cot, gain, wfmt, bdt, wcol,
    res, send, keep, toks, an, ant, dd, gfm, gout, gsl, pay, gpay,
):
    join_halves(core[0], mine, other, pay)
    attention_step(pay, watt, an, ant, dd, toks)
    mid_t = mid[...]
    weights = prob_in[...].astype(BF)
    prob = prob_in[...].reshape(HEADS, SLICES, BT)
    inv = aux[:HEADS]
    groups = []
    for i in range(2):
        lanes = slice(i * G, (i + 1) * G)
        groups.append(dot(an[i], jnp.concatenate([dmix[:, lanes], feat[:, lanes]], axis=1), NT))
    dw = jnp.concatenate(groups, axis=0) + dd[...]
    dw = dw.reshape(HEADS, SLICES, BT)
    dl = prob * (dw - jnp.sum(prob * dw, axis=1, keepdims=True))
    d_raw = (dl * inv[:, None, :]).reshape(HS, BT).astype(BF)
    direct = dot(bdt[...], d_raw)
    inner = (mid_t.astype(F32) * direct[:C]).reshape(HEADS, HEAD, BT)
    against_top = jnp.sum(inner, axis=1) - aux[2 * HEADS :] * direct[C : C + HEADS]
    d_temper = -against_top * aux[HEADS : 2 * HEADS]
    low = dot(ant[0], weights[:GS]).astype(BF)
    high = dot(ant[1], weights[GS:]).astype(BF)
    mixed_df = jnp.concatenate([low[:G], high[:G], low[G:], high[G:]], axis=0)
    spread = jnp.broadcast_to(d_temper[:, None, :], (HEADS, HEAD, BT)).reshape(C, BT)
    dm = (direct[:C] + spread * wcol[...]).astype(BF)
    res[: 2 * C] = mixed_df
    res[2 * C :] = dm
    normed_here = normed[...]
    gfm[:C] = dot(mixed_df[C:], normed_here)
    gfm[C:] = dot(dm, normed_here)
    gout[...] = dot(mixed_df[:C], cot[...])
    dt_hi = d_temper.astype(BF)
    dt_lo = (d_temper - dt_hi.astype(F32)).astype(BF)
    gsl[:HS] = dot(d_raw, mid_t, NT)
    gsl[HS:] = dot(jnp.concatenate([dt_hi, dt_lo], axis=0), mid_t, NT)

    grad_fm = gfm[...]
    gpay[: 2 * C] = grad_fm
    gpay[2 * C : 3 * C] = gout[...]
    rows = lax.broadcasted_iota(jnp.int32, (C, C), 0)
    cols = lax.broadcasted_iota(jnp.int32, (C, C), 1)
    over_heads = (rows % HEAD == cols % HEAD).astype(F32)
    packed = jnp.where(packed_mask(), dot_high(fold_heads(gsl[:HS]), over_heads), 0.0)
    gpay[3 * C : 3 * C + 8] = jnp.sum(packed.reshape(8, 8, C), axis=1)
    grad_gain = jnp.sum(grad_fm * wfmt[...].astype(F32), axis=0, keepdims=True) / gain[...]
    both = gsl[HS : HS + 8] + gsl[HS + 8 :]
    row = lax.broadcasted_iota(jnp.int32, (8, C), 0)
    lane_head = lax.broadcasted_iota(jnp.int32, (8, C), 1) // HEAD
    temper_row = jnp.sum(jnp.where(row == lane_head, both, 0.0), axis=0, keepdims=True)
    row = lax.broadcasted_iota(jnp.int32, (PAY2 - 3 * C - 8, C), 0)
    tail = jnp.where(row == 0, grad_gain, jnp.where(row == 1, temper_row, 0.0))
    gpay[3 * C + 8 :] = tail
    split_halves(core[0], gpay, send, keep)


def out_kernel(ptsb, cot, res, gain, wfmt, wout, layer, grad):
    points = ptsb[...]
    x_hat, inv_std = normalize(points)
    mixed_out = dot(res[:C], wout[...], TN)
    layer[...] = (points.astype(F32) + mixed_out).astype(BF)
    d_normed = dot(res[C:], wfmt[...], TN)
    scaled = d_normed * gain[...]
    mean_g = jnp.mean(scaled, axis=-1, keepdims=True)
    mean_gx = jnp.mean(scaled * x_hat, axis=-1, keepdims=True)
    grad[...] = (cot[...].astype(F32) + (scaled - mean_g - x_hat * mean_gx) * inv_std).astype(BF)


def unpack_kernel(core, mine, other, gfeat, gmid, gout, gslice, gtemper, ggain, full):
    join_halves(core[0], mine, other, full)
    gfeat[...] = full[:C].T
    gmid[...] = full[C : 2 * C].T
    gout[...] = full[2 * C : 3 * C]
    lane_in = lax.broadcasted_iota(jnp.int32, (C, HEAD), 0) % HEAD
    fold = (lane_in == lax.broadcasted_iota(jnp.int32, (C, HEAD), 1)).astype(F32)
    rows = jnp.broadcast_to(full[3 * C : 3 * C + 8].reshape(8, 1, C), (8, 8, C))
    spread = jnp.where(packed_mask(), rows.reshape(SLICES, C), 0.0)
    gslice[...] = dot_high(fold, spread, (((0,), (1,)), ((), ())))
    tail = full[3 * C + 8 : 3 * C + 16]
    gtemper[...] = dot_high(tail, fold)[1:2]
    ggain[...] = tail[0:1]


def swap(array, even, odd):
    n = lax.axis_size("pts")
    return lax.ppermute(array, "pts", [(i, i ^ (odd if i % 2 else even)) for i in range(n)])


def quad_sum(x, even, odd, wire):
    w = x.astype(wire)
    got = {k: swap(w, k * even, k * odd).astype(F32) for k in ORDER}
    return (w.astype(F32) + got[1]) + (got[2] + got[3])


def sum_over_chips(send, keep, wire, beside=()):
    x = keep + swap(send, 1, 1).astype(F32)
    done = []
    for i, (even, odd) in enumerate(((2, 8), (8, 32), (32, 2))):
        x = quad_sum(x, even, odd, wire)
        for at, arrays in beside:
            if at == i:
                x, arrays = lax.optimization_barrier((x, arrays))
                done.append(arrays)
    x = x.astype(wire)
    return x, swap(x, 1, 1), done


def neighbour_blocks(inner, outer):
    n = lax.axis_size("pts")
    edges = [(i, i + 1) for i in range(1, n - 1, 2)]
    got_outer = lax.ppermute(outer, "pts", edges + [(j, i) for i, j in edges])
    return swap(inner, 1, 1), got_outer


def whole(shape):
    return pl.BlockSpec(shape, lambda t, *_: (0,) * len(shape))


def rows_spec(width):
    return pl.BlockSpec((BLOCK, width), lambda t, *_: (t, 0))


PARAMS = pltpu.CompilerParams(vmem_limit_bytes=24 * 1024 * 1024)
BACK_PARAMS = pltpu.CompilerParams(vmem_limit_bytes=36 * 1024 * 1024)
SCALARS = pl.BlockSpec(memory_space=pltpu.SMEM)
HBM = pl.BlockSpec(memory_space=pl.ANY)


def per_device(
    loader_points, cotangent, block_counts, dest_table, norm_gain, w_feature, w_middle,
    w_slice, w_temper, attend_weight, w_output,
):
    rank = lax.axis_index("pts").astype(jnp.int32).reshape(1)
    core = lax.rem(rank, 2)
    edge = jax.ShapeDtypeStruct((HALF * BLOCK, C), BF)

    def tail_slot(t, rank, counts):
        return jnp.maximum(counts[rank[0]] - HALF, 0) + t

    def inner_slot(t, rank, counts, table):
        return (jnp.where(rank[0] % 2 == 0, tail_slot(t, rank, counts), t), 0)

    def outer_slot(t, rank, counts, table):
        return (jnp.where(rank[0] % 2 == 0, t, tail_slot(t, rank, counts)), 0)

    sel, inner, outer = pl.pallas_call(
        pick_kernel,
        grid_spec=pltpu.PrefetchScalarGridSpec(
            num_scalar_prefetch=3,
            grid=(HALF,),
            in_specs=[pl.BlockSpec((BLOCK, C), inner_slot), pl.BlockSpec((BLOCK, C), outer_slot)],
            out_specs=[SCALARS] + [rows_spec(C)] * 2,
        ),
        out_shape=[jax.ShapeDtypeStruct((3, B_DEV), jnp.int32), edge, edge],
        name="pick",
    )(rank, block_counts, dest_table, loader_points, loader_points)
    got_inner, got_outer = neighbour_blocks(inner, outer)
    gain = norm_gain.reshape(1, C)
    d_mixed, wfmt, bd = pl.pallas_call(
        prep_kernel,
        grid=(1,),
        in_specs=[whole((ROWS, C))] + [whole((C, C))] * 3 + [whole((HEAD, SLICES)), whole((1, HEAD))],
        out_specs=[whole((ROWS, C)), whole((2 * C, C)), whole((HS + 32, C))],
        out_shape=[
            jax.ShapeDtypeStruct((ROWS, C), BF),
            jax.ShapeDtypeStruct((2 * C, C), BF),
            jax.ShapeDtypeStruct((HS + 32, C), BF),
        ],
        compiler_params=PARAMS,
        cost_estimate=pl.CostEstimate(
            flops=2 * ROWS * C * C, bytes_accessed=4 * 1024 * 1024, transcendentals=0
        ),
        name="prep",
    )(cotangent, w_output, w_feature, w_middle, w_slice, w_temper.reshape(1, HEAD))

    back_weights = pl.pallas_call(
        prep_back_kernel,
        grid=(1,),
        in_specs=[whole((HS, C)), whole((1, HEAD)), whole((3, HEAD, HEAD))],
        out_specs=[whole((C + 16, HS)), whole((C, 1)), whole((3, C, C))],
        out_shape=[
            jax.ShapeDtypeStruct((C + 16, HS), BF),
            jax.ShapeDtypeStruct((C, 1), F32),
            jax.ShapeDtypeStruct((3, C, C), F32),
        ],
        compiler_params=PARAMS,
        cost_estimate=pl.CostEstimate(
            flops=C * C * C, bytes_accessed=2 * 1024 * 1024, transcendentals=0
        ),
        name="prep_back",
    )(bd, w_temper.reshape(1, HEAD), attend_weight)

    wide = jax.ShapeDtypeStruct((ROWS, C), BF)
    half1 = jax.ShapeDtypeStruct((SLICES // 2, PAY1), F32)
    arrays = [wide] * 3 + [
        jax.ShapeDtypeStruct((C, ROWS), BF),
        jax.ShapeDtypeStruct((HS, ROWS), F32),
        jax.ShapeDtypeStruct((3 * HEADS, ROWS), F32),
    ]

    def front_specs(half):
        rows = pl.BlockSpec((FT, C), lambda t, s, c: (half(c), 0))
        cols = lambda n: pl.BlockSpec((n, FT), lambda t, s, c: (0, half(c)))
        block = lambda row, i: pl.BlockSpec(
            (BLOCK, C), lambda t, s, c: (s[row, HALF * half(c) + i], 0)
        )
        ins = [
            block(0, 0),
            block(0, 1),
            block(1, 0),
            block(1, 1),
            rows,
            whole((1, C)),
            whole((C, C)),
            pl.BlockSpec((C, C), lambda t, s, c: (1, 0)),
            whole((HS + 32, C)),
        ]
        return ins, [rows] * 3 + [cols(C), cols(HS), cols(3 * HEADS)]

    sums = [pltpu.VMEM((HS, C), F32), pltpu.VMEM((HS, 128), F32)]
    ins, outs = front_specs(first_half)
    *first, pay = pl.pallas_call(
        front_first,
        grid_spec=pltpu.PrefetchScalarGridSpec(
            num_scalar_prefetch=2,
            grid=(1,),
            in_specs=ins,
            out_specs=outs + [whole((SLICES, PAY1))],
            scratch_shapes=sums,
        ),
        out_shape=arrays + [jax.ShapeDtypeStruct((SLICES, PAY1), F32)],
        compiler_params=PARAMS,
        cost_estimate=pl.CostEstimate(
            flops=2 * ROWS * C * 3 * C, bytes_accessed=6 * 1024 * 1024, transcendentals=0
        ),
        name="front_first",
    )(sel, core, loader_points, loader_points, got_inner, got_inner, d_mixed, gain, w_feature, wfmt, bd)
    pay, (bdt, wcol, watt) = lax.optimization_barrier((pay, back_weights))
    ins, outs = front_specs(second_half)
    *first, send, keep = pl.pallas_call(
        front_second,
        grid_spec=pltpu.PrefetchScalarGridSpec(
            num_scalar_prefetch=2,
            grid=(1,),
            in_specs=ins + [whole((SLICES, PAY1))] + [HBM] * 6,
            out_specs=outs + [whole((SLICES // 2, PAY1))] * 2,
            scratch_shapes=sums + [pltpu.VMEM((SLICES, PAY1), F32)],
        ),
        out_shape=arrays + [half1] * 2,
        input_output_aliases={12 + i: i for i in range(6)},
        compiler_params=PARAMS,
        name="front_second",
    )(
        sel, core, loader_points, loader_points, got_outer, got_outer, d_mixed, gain, w_feature,
        wfmt, bd, pay, *first,
    )
    ptsb, normed, feat, mid, prob, aux = first

    mine, other, _ = sum_over_chips(send, keep, F32)

    back_rows = pl.BlockSpec((BT, C), lambda t: (t, 0))
    back_cols = lambda rows: pl.BlockSpec((rows, BT), lambda t: (0, t))
    res, send, keep, toks = pl.pallas_call(
        back_kernel,
        grid=(ROWS // BT,),
        in_specs=[SCALARS]
        + [whole((SLICES // 2, PAY1))] * 2
        + [whole((3, C, C))]
        + [back_rows] * 2
        + [back_cols(C), back_cols(HS), back_cols(3 * HEADS)]
        + [back_rows] * 2
        + [
            whole((1, C)),
            whole((2 * C, C)),
            whole((C + 16, HS)),
            whole((C, 1)),
        ],
        out_specs=[
            back_cols(3 * C),
            whole((PAY2 // 2, C)),
            whole((PAY2 // 2, C)),
            whole((4, SLICES, C)),
        ],
        out_shape=[
            jax.ShapeDtypeStruct((3 * C, ROWS), BF),
            jax.ShapeDtypeStruct((PAY2 // 2, C), BF),
            jax.ShapeDtypeStruct((PAY2 // 2, C), F32),
            jax.ShapeDtypeStruct((4, SLICES, C), F32),
        ],
        scratch_shapes=[
            pltpu.VMEM((2, GS, C), BF),
            pltpu.VMEM((2, C, GS), BF),
            pltpu.VMEM((HS, 1), F32),
            pltpu.VMEM((2 * C, C), F32),
            pltpu.VMEM((C, C), F32),
            pltpu.VMEM((HS + 16, C), F32),
            pltpu.VMEM((SLICES, PAY1), F32),
            pltpu.VMEM((PAY2, C), F32),
        ],
        compiler_params=BACK_PARAMS,
        name="back",
    )(
        core, mine, other, watt, normed, feat, mid, prob, aux, d_mixed, cotangent, gain, wfmt,
        bdt, wcol,
    )

    layer_out, grad_points = pl.pallas_call(
        out_kernel,
        grid=(B_DEV,),
        in_specs=[
            rows_spec(C),
            rows_spec(C),
            pl.BlockSpec((3 * C, BLOCK), lambda t: (0, t)),
            whole((1, C)),
            whole((2 * C, C)),
            whole((C, C)),
        ],
        out_specs=[rows_spec(C)] * 2,
        out_shape=[wide] * 2,
        compiler_params=PARAMS,
        cost_estimate=pl.CostEstimate(
            flops=2 * ROWS * C * 3 * C, bytes_accessed=7 * ROWS * C * 2, transcendentals=0
        ),
        name="outputs",
    )(ptsb, cotangent, res, gain, wfmt, w_output)

    grad_attend = pl.pallas_call(
        attend_gradients,
        out_shape=jax.ShapeDtypeStruct((3, HEAD, HEAD), F32),
        compiler_params=PARAMS,
        name="attend_grads",
    )(toks)

    beside = ((0, (layer_out, grad_points)), (1, grad_attend))
    mine, other, done = sum_over_chips(send, keep, BF, beside)
    (layer_out, grad_points), grad_attend = done
    vmem = pl.BlockSpec(memory_space=pltpu.VMEM)
    grad_feature, grad_middle, grad_output, grad_slice, grad_temper, grad_gain = pl.pallas_call(
        unpack_kernel,
        in_specs=[SCALARS, vmem, vmem],
        out_specs=[vmem] * 6,
        out_shape=[
            jax.ShapeDtypeStruct((C, C), F32),
            jax.ShapeDtypeStruct((C, C), F32),
            jax.ShapeDtypeStruct((C, C), F32),
            jax.ShapeDtypeStruct((HEAD, SLICES), F32),
            jax.ShapeDtypeStruct((1, HEAD), F32),
            jax.ShapeDtypeStruct((1, C), F32),
        ],
        scratch_shapes=[pltpu.VMEM((PAY2, C), F32)],
        compiler_params=PARAMS,
        name="unpack",
    )(core, mine, other)
    return (
        layer_out,
        grad_points,
        grad_gain.reshape(C),
        grad_feature,
        grad_middle,
        grad_slice,
        grad_temper.reshape(HEAD),
        grad_attend,
        grad_output,
    )


def solution(mesh):
    return jax.shard_map(
        per_device,
        mesh=mesh,
        in_specs=(P("pts", None), P("pts", None), P(), P("pts"), P(), P(), P(), P(), P(), P(), P()),
        out_specs=(P("pts", None), P("pts", None), P(), P(), P(), P(), P(), P(), P()),
        check_vma=False,
    )
```

```python
import math

import jax
import jax.numpy as jnp
from jax import lax
from jax.experimental import pallas as pl
from jax.experimental.pallas import tpu as pltpu
from jax.sharding import PartitionSpec as P

BLOCK = 512
B_DEV = 4
HALF = 2
CAP = 8
C = 256
HEADS = 8
HEAD = 32
SLICES = 64
HS = HEADS * SLICES
ROWS = B_DEV * BLOCK
PAY1 = 640
PAY2 = 800
ORDER = (1, 2, 3)
FT = HALF * BLOCK
BT = ROWS
BF = jnp.bfloat16
F32 = jnp.float32
HIGH = lax.Precision.HIGH
G = C // 2
GS = HS // 2
NN = (((1,), (0,)), ((), ()))
NT = (((1,), (1,)), ((), ()))
TN = (((0,), (0,)), ((), ()))


def dot(a, b, dims=NN):
    return lax.dot_general(a, b, dims, preferred_element_type=F32)


def dot_high(a, b, dims=NN):
    return lax.dot_general(a, b, dims, precision=HIGH, preferred_element_type=F32)


def dot_full(a, b):
    return lax.dot_general(a, b, NN, precision=lax.Precision.HIGHEST, preferred_element_type=F32)


def head_mask(rows):
    row_head = lax.broadcasted_iota(jnp.int32, (rows, C), 0) // SLICES
    lane_head = lax.broadcasted_iota(jnp.int32, (rows, C), 1) // HEAD
    return row_head == lane_head


def fold_heads(full):
    masked = jnp.where(head_mask(HS), full, 0.0)
    return jnp.sum(masked.reshape(HEADS, SLICES, C), axis=0)


def spread_heads(small):
    tiled = jnp.concatenate([small] * HEADS, axis=0)
    return jnp.where(head_mask(HS), tiled, 0.0)


def normalize(points):
    point_f = points.astype(F32)
    center = point_f - jnp.mean(point_f, axis=-1, keepdims=True)
    inv_std = lax.rsqrt(jnp.mean(center * center, axis=-1, keepdims=True) + 1e-05)
    return center * inv_std, inv_std


def slice_softmax(mid_t, bd):
    out = dot(bd, mid_t)
    width = mid_t.shape[1]
    temper = out[HS : HS + 8] + out[HS + 8 : HS + 16] + out[HS + 16 : HS + 24]
    scale = 0.5 + jnp.maximum(temper, 0.0) + jnp.log1p(jnp.exp(-jnp.abs(temper)))
    inv = 1.0 / scale
    powers = out[:HS].reshape(HEADS, SLICES, width) * (inv * math.log2(math.e))[:, None, :]
    top = jnp.max(powers, axis=1, keepdims=True)
    e = jnp.exp2(powers - top)
    prob = e * (1.0 / jnp.sum(e, axis=1, keepdims=True))
    raw_top = top[:, 0] * (scale * math.log(2.0))
    return temper, inv, raw_top, prob


def split_halves(core, full, send, keep):
    half = full.shape[0] // 2

    @pl.when(core == 0)
    def _():
        keep[...] = full[:half].astype(keep.dtype)
        send[...] = full[half:].astype(send.dtype)

    @pl.when(core != 0)
    def _():
        keep[...] = full[half:].astype(keep.dtype)
        send[...] = full[:half].astype(send.dtype)


def join_halves(core, mine, other, full):
    half = full.shape[0] // 2

    @pl.when(core == 0)
    def _():
        full[:half] = mine[...].astype(full.dtype)
        full[half:] = other[...].astype(full.dtype)

    @pl.when(core != 0)
    def _():
        full[:half] = other[...].astype(full.dtype)
        full[half:] = mine[...].astype(full.dtype)


def pick_kernel(rank, counts, table, inner, outer, sel, inner_out, outer_out):
    inner_out[...] = inner[...]
    outer_out[...] = outer[...]

    @pl.when(pl.program_id(0) == 0)
    def _():
        place_blocks(rank, counts, table, sel)


def place_blocks(rank, counts, table, sel):
    here = rank[0]
    found, own = [], []
    for t in range(B_DEV):
        slot = jnp.int32(0)
        hit = jnp.int32(0)
        for s in range(CAP):
            same = table[s] == here * B_DEV + t
            slot = jnp.where(same, s, slot)
            hit = jnp.where(same, 1, hit)
        own.append(slot)
        found.append(hit)
    from_prev = 2 - found[0] - found[1]
    from_next = 2 - found[2] - found[3]
    left = counts[jnp.maximum(here - 1, 0)]
    start = jnp.maximum(left - HALF, 0)
    for t in range(B_DEV):
        sel[0, t] = own[t]
        place = left - from_prev + t - start if t < HALF else t - (B_DEV - from_next)
        sel[1, t] = jnp.clip(place, 0, HALF - 1)
        sel[2, t] = found[t]


def prep_kernel(cot, wout, wf, wm, ws, wt, dmix, wfmt, bd):
    dmix[...] = dot(cot[...], wout[...], NT).astype(BF)
    wfmt[:C] = wf[...].T
    wfmt[C:] = wm[...].T
    spread = spread_matrix()
    slice_rows = dot(ws[...], spread.astype(BF), TN)
    bd[:HS] = spread_heads(slice_rows).astype(BF)
    temper = dot_full(wt[...], spread)
    hi = temper.astype(BF).astype(F32)
    middle = (temper - hi).astype(BF).astype(F32)
    low = temper - hi - middle
    row = lax.broadcasted_iota(jnp.int32, (8, C), 0)
    own_head = row == lax.broadcasted_iota(jnp.int32, (8, C), 1) // HEAD
    parts = [jnp.where(own_head, part, 0.0) for part in (hi, middle, low)]
    bd[HS:] = jnp.concatenate(parts + [jnp.zeros((8, C), F32)], axis=0).astype(BF)


def spread_matrix():
    lane_in = lax.broadcasted_iota(jnp.int32, (HEAD, C), 1) % HEAD
    return (lax.broadcasted_iota(jnp.int32, (HEAD, C), 0) == lane_in).astype(F32)


def prep_back_kernel(bd, wt, attw, bdt, wcol, watt):
    spread = spread_matrix()
    bdt[:C] = bd[...].astype(F32).T.astype(BF)
    row = lax.broadcasted_iota(jnp.int32, (16, HS), 0)
    bdt[C:] = (row == lax.broadcasted_iota(jnp.int32, (16, HS), 1) // SLICES).astype(BF)
    temper = dot_full(wt[...], spread)
    rows = lax.broadcasted_iota(jnp.int32, (C, C), 0)
    cols = lax.broadcasted_iota(jnp.int32, (C, C), 1)
    wcol[...] = jnp.sum(jnp.where(rows == cols, temper, 0.0), axis=1, keepdims=True)
    same_head = rows // HEAD == cols // HEAD
    for i in range(3):
        wide = dot_full(attw[i], spread)
        watt[i] = jnp.where(same_head, jnp.concatenate([wide] * HEADS, axis=0), 0.0)


def first_half(core):
    return 1 - core[0]


def second_half(core):
    return core[0]


def front_first(sel, core, *refs):
    *arrays, pay, acc, den = refs
    front_rows(sel, first_half(core), *arrays, acc, den)
    fold_sums(acc, den, pay)


def front_second(sel, core, *refs):
    ins, pay_first, rest = refs[:9], refs[9], refs[16:]
    *arrays, send, keep, acc, den, pay = rest
    front_rows(sel, second_half(core), *ins, *arrays, acc, den)
    fold_sums(acc, den, pay)
    pay[...] += pay_first[...]
    split_halves(core[0], pay, send, keep)


def front_rows(
    sel, half, own_a, own_b, other_a, other_b, dmix, gain, wf, wmt, bd,
    ptsb, normed_out, feat_out, mid_out, prob_out, aux, acc, den,
):
    for i, (own, other) in enumerate(((own_a, other_a), (own_b, other_b))):
        found = sel[2, HALF * half + i]
        place = slice(i * BLOCK, (i + 1) * BLOCK)

        @pl.when(found == 1)
        def _(own=own, place=place):
            ptsb[place] = own[...]

        @pl.when(found != 1)
        def _(other=other, place=place):
            ptsb[place] = other[...]

    x_hat, _ = normalize(ptsb[...])
    normed = (x_hat * gain[...]).astype(BF)
    normed_out[...] = normed
    feat = dot(normed, wf[...]).astype(BF)
    mid_t = dot(wmt[...], normed, NT).astype(BF)
    feat_out[...] = feat
    mid_out[...] = mid_t
    temper, inv, raw_top, prob = slice_softmax(mid_t, bd[...])
    prob_out[...] = prob.reshape(HS, FT)
    aux[:HEADS] = inv
    aux[HEADS : 2 * HEADS] = inv * jax.nn.sigmoid(temper)
    aux[2 * HEADS :] = raw_top
    weights = prob.reshape(HS, FT).astype(BF)

    grad = dmix[...]
    for i in range(2):
        both = jnp.concatenate([feat[:, i * G : (i + 1) * G], grad[:, i * G : (i + 1) * G]], axis=1)
        acc[i * GS : (i + 1) * GS] = dot(weights[i * GS : (i + 1) * GS], both)
    den[...] = dot(weights, jnp.ones((FT, 128), BF))


def fold_sums(acc, den, pay):
    row_head = lax.broadcasted_iota(jnp.int32, (GS, C), 0) // SLICES
    lane_head = lax.broadcasted_iota(jnp.int32, (GS, C), 1) % G // HEAD
    for i in range(2):
        own_part = jnp.where(row_head == lane_head, acc[i * GS : (i + 1) * GS], 0.0)
        folded = jnp.sum(own_part.reshape(HEADS // 2, SLICES, C), axis=0)
        pay[:, i * G : (i + 1) * G] = folded[:, :G]
        pay[:, C + i * G : C + (i + 1) * G] = folded[:, G:]
    row_head = lax.broadcasted_iota(jnp.int32, (HS, 128), 0) // SLICES
    lane = lax.broadcasted_iota(jnp.int32, (HS, 128), 1)
    placed = jnp.where(row_head == lane, den[...], 0.0)
    pay[:, 2 * C :] = jnp.sum(placed.reshape(HEADS, SLICES, 128), axis=0)


def packed_mask():
    row = lax.broadcasted_iota(jnp.int32, (SLICES, C), 0)
    return lax.broadcasted_iota(jnp.int32, (SLICES, C), 1) // HEAD == row % 8


def attention_step(pay, watt, an, ant, dd, toks):
    numer = pay[:, :C]
    deslice = pay[:, C : 2 * C]
    head_of_lane = lax.broadcasted_iota(jnp.int32, (128, C), 1) // HEAD
    expand = (lax.broadcasted_iota(jnp.int32, (128, C), 0) == head_of_lane).astype(F32)
    inv_den = 1.0 / (dot_high(pay[:, 2 * C :], expand) + 1e-05)
    tokens = numer * inv_den
    mask = head_mask(HS)
    q = dot_high(tokens, watt[0])
    k = dot_high(tokens, watt[1])
    v = dot_high(tokens, watt[2])
    q_bd = spread_heads(q)
    root = 1.0 / math.sqrt(HEAD)
    scores = dot_high(q_bd, k, NT) * root
    top = jnp.max(scores, axis=-1, keepdims=True)
    e = jnp.exp(scores - top)
    att = e / jnp.sum(e, axis=-1, keepdims=True)
    attended = jnp.where(mask, dot_high(att, v), 0.0)
    do_bd = spread_heads(deslice)
    dv = dot_high(att, do_bd, TN)
    d_att = dot_high(do_bd, v, NT)
    ds = att * (d_att - jnp.sum(att * d_att, axis=-1, keepdims=True)) * root
    dq = fold_heads(dot_high(ds, k))
    dk = dot_high(ds, q_bd, TN)
    d_tokens = (
        dot_high(dq, watt[0], NT) + dot_high(dk, watt[1], NT) + dot_high(dv, watt[2], NT)
    )
    d_numer = d_tokens * inv_den
    d_den = -d_numer * tokens
    dd[...] = jnp.sum(spread_heads(d_den), axis=1, keepdims=True)
    d_numer_bd = spread_heads(d_numer)
    for i in range(2):
        rows = slice(i * GS, (i + 1) * GS)
        lanes = slice(i * G, (i + 1) * G)
        both = jnp.concatenate([attended[rows, lanes], d_numer_bd[rows, lanes]], axis=1)
        an[i] = both.astype(BF)
        ant[i] = both.T.astype(BF)
    toks[0] = tokens
    toks[1] = dq
    toks[2] = dk
    toks[3] = dv


def attend_gradients(toks, gatt):
    row_head = lax.broadcasted_iota(jnp.int32, (C, C), 0) // HEAD
    col_head = lax.broadcasted_iota(jnp.int32, (C, C), 1) // HEAD
    same = row_head == col_head
    lane_in = lax.broadcasted_iota(jnp.int32, (C, HEAD), 0) % HEAD
    fold = (lane_in == lax.broadcasted_iota(jnp.int32, (C, HEAD), 1)).astype(F32)
    for i in range(3):
        full = jnp.where(same, dot_high(toks[0], toks[i + 1], TN), 0.0)
        packed = dot_high(full, fold)
        gatt[i] = jnp.sum(packed.reshape(HEADS, HEAD, HEAD), axis=0)


def back_kernel(
    core, mine, other, watt, normed, feat, mid, prob_in, aux, dmix, cot, gain, wfmt, bdt, wcol,
    res, send, keep, toks, an, ant, dd, gfm, gout, gsl, pay, gpay,
):
    join_halves(core[0], mine, other, pay)
    attention_step(pay, watt, an, ant, dd, toks)
    mid_t = mid[...]
    weights = prob_in[...].astype(BF)
    prob = prob_in[...].reshape(HEADS, SLICES, BT)
    inv = aux[:HEADS]
    groups = []
    for i in range(2):
        lanes = slice(i * G, (i + 1) * G)
        groups.append(dot(an[i], jnp.concatenate([dmix[:, lanes], feat[:, lanes]], axis=1), NT))
    dw = jnp.concatenate(groups, axis=0) + dd[...]
    dw = dw.reshape(HEADS, SLICES, BT)
    dl = prob * (dw - jnp.sum(prob * dw, axis=1, keepdims=True))
    d_raw = (dl * inv[:, None, :]).reshape(HS, BT).astype(BF)
    direct = dot(bdt[...], d_raw)
    inner = (mid_t.astype(F32) * direct[:C]).reshape(HEADS, HEAD, BT)
    against_top = jnp.sum(inner, axis=1) - aux[2 * HEADS :] * direct[C : C + HEADS]
    d_temper = -against_top * aux[HEADS : 2 * HEADS]
    low = dot(ant[0], weights[:GS]).astype(BF)
    high = dot(ant[1], weights[GS:]).astype(BF)
    mixed_df = jnp.concatenate([low[:G], high[:G], low[G:], high[G:]], axis=0)
    spread = jnp.broadcast_to(d_temper[:, None, :], (HEADS, HEAD, BT)).reshape(C, BT)
    dm = (direct[:C] + spread * wcol[...]).astype(BF)
    res[: 2 * C] = mixed_df
    res[2 * C :] = dm
    normed_here = normed[...]
    gfm[:C] = dot(mixed_df[C:], normed_here)
    gfm[C:] = dot(dm, normed_here)
    gout[...] = dot(mixed_df[:C], cot[...])
    dt_hi = d_temper.astype(BF)
    dt_lo = (d_temper - dt_hi.astype(F32)).astype(BF)
    gsl[:HS] = dot(d_raw, mid_t, NT)
    gsl[HS:] = dot(jnp.concatenate([dt_hi, dt_lo], axis=0), mid_t, NT)

    grad_fm = gfm[...]
    gpay[: 2 * C] = grad_fm
    gpay[2 * C : 3 * C] = gout[...]
    rows = lax.broadcasted_iota(jnp.int32, (C, C), 0)
    cols = lax.broadcasted_iota(jnp.int32, (C, C), 1)
    over_heads = (rows % HEAD == cols % HEAD).astype(F32)
    packed = jnp.where(packed_mask(), dot_high(fold_heads(gsl[:HS]), over_heads), 0.0)
    gpay[3 * C : 3 * C + 8] = jnp.sum(packed.reshape(8, 8, C), axis=1)
    grad_gain = jnp.sum(grad_fm * wfmt[...].astype(F32), axis=0, keepdims=True) / gain[...]
    both = gsl[HS : HS + 8] + gsl[HS + 8 :]
    row = lax.broadcasted_iota(jnp.int32, (8, C), 0)
    lane_head = lax.broadcasted_iota(jnp.int32, (8, C), 1) // HEAD
    temper_row = jnp.sum(jnp.where(row == lane_head, both, 0.0), axis=0, keepdims=True)
    row = lax.broadcasted_iota(jnp.int32, (PAY2 - 3 * C - 8, C), 0)
    tail = jnp.where(row == 0, grad_gain, jnp.where(row == 1, temper_row, 0.0))
    gpay[3 * C + 8 :] = tail
    split_halves(core[0], gpay, send, keep)


def out_kernel(ptsb, cot, res, gain, wfmt, wout, layer, grad):
    points = ptsb[...]
    x_hat, inv_std = normalize(points)
    mixed_out = dot(res[:C], wout[...], TN)
    layer[...] = (points.astype(F32) + mixed_out).astype(BF)
    d_normed = dot(res[C:], wfmt[...], TN)
    scaled = d_normed * gain[...]
    mean_g = jnp.mean(scaled, axis=-1, keepdims=True)
    mean_gx = jnp.mean(scaled * x_hat, axis=-1, keepdims=True)
    grad[...] = (cot[...].astype(F32) + (scaled - mean_g - x_hat * mean_gx) * inv_std).astype(BF)


def unpack_kernel(core, mine, other, gfeat, gmid, gout, gslice, gtemper, ggain, full):
    join_halves(core[0], mine, other, full)
    gfeat[...] = full[:C].T
    gmid[...] = full[C : 2 * C].T
    gout[...] = full[2 * C : 3 * C]
    lane_in = lax.broadcasted_iota(jnp.int32, (C, HEAD), 0) % HEAD
    fold = (lane_in == lax.broadcasted_iota(jnp.int32, (C, HEAD), 1)).astype(F32)
    rows = jnp.broadcast_to(full[3 * C : 3 * C + 8].reshape(8, 1, C), (8, 8, C))
    spread = jnp.where(packed_mask(), rows.reshape(SLICES, C), 0.0)
    gslice[...] = dot_high(fold, spread, (((0,), (1,)), ((), ())))
    tail = full[3 * C + 8 : 3 * C + 16]
    gtemper[...] = dot_high(tail, fold)[1:2]
    ggain[...] = tail[0:1]


def swap(array, even, odd):
    n = lax.axis_size("pts")
    return lax.ppermute(array, "pts", [(i, i ^ (odd if i % 2 else even)) for i in range(n)])


def quad_sum(x, even, odd, wire):
    w = x.astype(wire)
    got = {k: swap(w, k * even, k * odd).astype(F32) for k in ORDER}
    return (w.astype(F32) + got[1]) + (got[2] + got[3])


def sum_over_chips(send, keep, wire, beside=()):
    x = keep + swap(send, 1, 1).astype(F32)
    done = []
    for i, (even, odd) in enumerate(((2, 8), (8, 32), (32, 2))):
        x = quad_sum(x, even, odd, wire)
        for at, arrays in beside:
            if at == i:
                x, arrays = lax.optimization_barrier((x, arrays))
                done.append(arrays)
    x = x.astype(wire)
    return x, swap(x, 1, 1), done


def neighbour_blocks(inner, outer):
    n = lax.axis_size("pts")
    edges = [(i, i + 1) for i in range(1, n - 1, 2)]
    got_outer = lax.ppermute(outer, "pts", edges + [(j, i) for i, j in edges])
    return swap(inner, 1, 1), got_outer


def whole(shape):
    return pl.BlockSpec(shape, lambda t, *_: (0,) * len(shape))


def rows_spec(width):
    return pl.BlockSpec((BLOCK, width), lambda t, *_: (t, 0))


PARAMS = pltpu.CompilerParams(vmem_limit_bytes=24 * 1024 * 1024)
BACK_PARAMS = pltpu.CompilerParams(vmem_limit_bytes=36 * 1024 * 1024)
SCALARS = pl.BlockSpec(memory_space=pltpu.SMEM)
HBM = pl.BlockSpec(memory_space=pl.ANY)


def per_device(
    loader_points, cotangent, block_counts, dest_table, norm_gain, w_feature, w_middle,
    w_slice, w_temper, attend_weight, w_output,
):
    rank = lax.axis_index("pts").astype(jnp.int32).reshape(1)
    core = lax.rem(rank, 2)
    edge = jax.ShapeDtypeStruct((HALF * BLOCK, C), BF)

    def tail_slot(t, rank, counts):
        return jnp.maximum(counts[rank[0]] - HALF, 0) + t

    def inner_slot(t, rank, counts, table):
        return (jnp.where(rank[0] % 2 == 0, tail_slot(t, rank, counts), t), 0)

    def outer_slot(t, rank, counts, table):
        return (jnp.where(rank[0] % 2 == 0, t, tail_slot(t, rank, counts)), 0)

    sel, inner, outer = pl.pallas_call(
        pick_kernel,
        grid_spec=pltpu.PrefetchScalarGridSpec(
            num_scalar_prefetch=3,
            grid=(HALF,),
            in_specs=[pl.BlockSpec((BLOCK, C), inner_slot), pl.BlockSpec((BLOCK, C), outer_slot)],
            out_specs=[SCALARS] + [rows_spec(C)] * 2,
        ),
        out_shape=[jax.ShapeDtypeStruct((3, B_DEV), jnp.int32), edge, edge],
        name="pick",
    )(rank, block_counts, dest_table, loader_points, loader_points)
    got_inner, got_outer = neighbour_blocks(inner, outer)
    gain = norm_gain.reshape(1, C)
    d_mixed, wfmt, bd = pl.pallas_call(
        prep_kernel,
        grid=(1,),
        in_specs=[whole((ROWS, C))] + [whole((C, C))] * 3 + [whole((HEAD, SLICES)), whole((1, HEAD))],
        out_specs=[whole((ROWS, C)), whole((2 * C, C)), whole((HS + 32, C))],
        out_shape=[
            jax.ShapeDtypeStruct((ROWS, C), BF),
            jax.ShapeDtypeStruct((2 * C, C), BF),
            jax.ShapeDtypeStruct((HS + 32, C), BF),
        ],
        compiler_params=PARAMS,
        cost_estimate=pl.CostEstimate(
            flops=2 * ROWS * C * C, bytes_accessed=4 * 1024 * 1024, transcendentals=0
        ),
        name="prep",
    )(cotangent, w_output, w_feature, w_middle, w_slice, w_temper.reshape(1, HEAD))

    back_weights = pl.pallas_call(
        prep_back_kernel,
        grid=(1,),
        in_specs=[whole((HS, C)), whole((1, HEAD)), whole((3, HEAD, HEAD))],
        out_specs=[whole((C + 16, HS)), whole((C, 1)), whole((3, C, C))],
        out_shape=[
            jax.ShapeDtypeStruct((C + 16, HS), BF),
            jax.ShapeDtypeStruct((C, 1), F32),
            jax.ShapeDtypeStruct((3, C, C), F32),
        ],
        compiler_params=PARAMS,
        cost_estimate=pl.CostEstimate(
            flops=C * C * C, bytes_accessed=2 * 1024 * 1024, transcendentals=0
        ),
        name="prep_back",
    )(bd, w_temper.reshape(1, HEAD), attend_weight)

    wide = jax.ShapeDtypeStruct((ROWS, C), BF)
    half1 = jax.ShapeDtypeStruct((SLICES // 2, PAY1), F32)
    arrays = [wide] * 3 + [
        jax.ShapeDtypeStruct((C, ROWS), BF),
        jax.ShapeDtypeStruct((HS, ROWS), F32),
        jax.ShapeDtypeStruct((3 * HEADS, ROWS), F32),
    ]

    def front_specs(half):
        rows = pl.BlockSpec((FT, C), lambda t, s, c: (half(c), 0))
        cols = lambda n: pl.BlockSpec((n, FT), lambda t, s, c: (0, half(c)))
        block = lambda row, i: pl.BlockSpec(
            (BLOCK, C), lambda t, s, c: (s[row, HALF * half(c) + i], 0)
        )
        ins = [
            block(0, 0),
            block(0, 1),
            block(1, 0),
            block(1, 1),
            rows,
            whole((1, C)),
            whole((C, C)),
            pl.BlockSpec((C, C), lambda t, s, c: (1, 0)),
            whole((HS + 32, C)),
        ]
        return ins, [rows] * 3 + [cols(C), cols(HS), cols(3 * HEADS)]

    sums = [pltpu.VMEM((HS, C), F32), pltpu.VMEM((HS, 128), F32)]
    ins, outs = front_specs(first_half)
    *first, pay = pl.pallas_call(
        front_first,
        grid_spec=pltpu.PrefetchScalarGridSpec(
            num_scalar_prefetch=2,
            grid=(1,),
            in_specs=ins,
            out_specs=outs + [whole((SLICES, PAY1))],
            scratch_shapes=sums,
        ),
        out_shape=arrays + [jax.ShapeDtypeStruct((SLICES, PAY1), F32)],
        compiler_params=PARAMS,
        cost_estimate=pl.CostEstimate(
            flops=2 * ROWS * C * 3 * C, bytes_accessed=6 * 1024 * 1024, transcendentals=0
        ),
        name="front_first",
    )(sel, core, loader_points, loader_points, got_inner, got_inner, d_mixed, gain, w_feature, wfmt, bd)
    pay, (bdt, wcol, watt) = lax.optimization_barrier((pay, back_weights))
    ins, outs = front_specs(second_half)
    *first, send, keep = pl.pallas_call(
        front_second,
        grid_spec=pltpu.PrefetchScalarGridSpec(
            num_scalar_prefetch=2,
            grid=(1,),
            in_specs=ins + [whole((SLICES, PAY1))] + [HBM] * 6,
            out_specs=outs + [whole((SLICES // 2, PAY1))] * 2,
            scratch_shapes=sums + [pltpu.VMEM((SLICES, PAY1), F32)],
        ),
        out_shape=arrays + [half1] * 2,
        input_output_aliases={12 + i: i for i in range(6)},
        compiler_params=PARAMS,
        name="front_second",
    )(
        sel, core, loader_points, loader_points, got_outer, got_outer, d_mixed, gain, w_feature,
        wfmt, bd, pay, *first,
    )
    ptsb, normed, feat, mid, prob, aux = first

    mine, other, _ = sum_over_chips(send, keep, F32)

    back_rows = pl.BlockSpec((BT, C), lambda t: (t, 0))
    back_cols = lambda rows: pl.BlockSpec((rows, BT), lambda t: (0, t))
    res, send, keep, toks = pl.pallas_call(
        back_kernel,
        grid=(ROWS // BT,),
        in_specs=[SCALARS]
        + [whole((SLICES // 2, PAY1))] * 2
        + [whole((3, C, C))]
        + [back_rows] * 2
        + [back_cols(C), back_cols(HS), back_cols(3 * HEADS)]
        + [back_rows] * 2
        + [
            whole((1, C)),
            whole((2 * C, C)),
            whole((C + 16, HS)),
            whole((C, 1)),
        ],
        out_specs=[
            back_cols(3 * C),
            whole((PAY2 // 2, C)),
            whole((PAY2 // 2, C)),
            whole((4, SLICES, C)),
        ],
        out_shape=[
            jax.ShapeDtypeStruct((3 * C, ROWS), BF),
            jax.ShapeDtypeStruct((PAY2 // 2, C), BF),
            jax.ShapeDtypeStruct((PAY2 // 2, C), F32),
            jax.ShapeDtypeStruct((4, SLICES, C), F32),
        ],
        scratch_shapes=[
            pltpu.VMEM((2, GS, C), BF),
            pltpu.VMEM((2, C, GS), BF),
            pltpu.VMEM((HS, 1), F32),
            pltpu.VMEM((2 * C, C), F32),
            pltpu.VMEM((C, C), F32),
            pltpu.VMEM((HS + 16, C), F32),
            pltpu.VMEM((SLICES, PAY1), F32),
            pltpu.VMEM((PAY2, C), F32),
        ],
        compiler_params=BACK_PARAMS,
        name="back",
    )(
        core, mine, other, watt, normed, feat, mid, prob, aux, d_mixed, cotangent, gain, wfmt,
        bdt, wcol,
    )

    out_rows = pl.BlockSpec((FT, C), lambda t: (t, 0))
    layer_out, grad_points = pl.pallas_call(
        out_kernel,
        grid=(ROWS // FT,),
        in_specs=[
            out_rows,
            out_rows,
            pl.BlockSpec((3 * C, FT), lambda t: (0, t)),
            whole((1, C)),
            whole((2 * C, C)),
            whole((C, C)),
        ],
        out_specs=[out_rows] * 2,
        out_shape=[wide] * 2,
        compiler_params=PARAMS,
        cost_estimate=pl.CostEstimate(
            flops=2 * ROWS * C * 3 * C, bytes_accessed=7 * ROWS * C * 2, transcendentals=0
        ),
        name="outputs",
    )(ptsb, cotangent, res, gain, wfmt, w_output)

    grad_attend = pl.pallas_call(
        attend_gradients,
        out_shape=jax.ShapeDtypeStruct((3, HEAD, HEAD), F32),
        compiler_params=PARAMS,
        name="attend_grads",
    )(toks)

    beside = ((0, (layer_out, grad_points)), (1, grad_attend))
    mine, other, done = sum_over_chips(send, keep, BF, beside)
    (layer_out, grad_points), grad_attend = done
    vmem = pl.BlockSpec(memory_space=pltpu.VMEM)
    grad_feature, grad_middle, grad_output, grad_slice, grad_temper, grad_gain = pl.pallas_call(
        unpack_kernel,
        in_specs=[SCALARS, vmem, vmem],
        out_specs=[vmem] * 6,
        out_shape=[
            jax.ShapeDtypeStruct((C, C), F32),
            jax.ShapeDtypeStruct((C, C), F32),
            jax.ShapeDtypeStruct((C, C), F32),
            jax.ShapeDtypeStruct((HEAD, SLICES), F32),
            jax.ShapeDtypeStruct((1, HEAD), F32),
            jax.ShapeDtypeStruct((1, C), F32),
        ],
        scratch_shapes=[pltpu.VMEM((PAY2, C), F32)],
        compiler_params=PARAMS,
        name="unpack",
    )(core, mine, other)
    return (
        layer_out,
        grad_points,
        grad_gain.reshape(C),
        grad_feature,
        grad_middle,
        grad_slice,
        grad_temper.reshape(HEAD),
        grad_attend,
        grad_output,
    )


def solution(mesh):
    return jax.shard_map(
        per_device,
        mesh=mesh,
        in_specs=(P("pts", None), P("pts", None), P(), P("pts"), P(), P(), P(), P(), P(), P(), P()),
        out_specs=(P("pts", None), P("pts", None), P(), P(), P(), P(), P(), P(), P()),
        check_vma=False,
    )
```
